32 devices in a mesh: wide: 8 (over z, y), narrow: 4 (over x, core).
Axes of the slice: x: 2, y: 2, z: 4, core: 2. Of those that a mesh axis runs over, the one named last changes fastest.
Arguments:
- level_rhs: float32 [8, 1024, 512], P('wide', 'narrow'), may hold values from -6 to 6
- galerkin_cols: int32 [3, 8, 16, 5], P(None, 'wide', 'narrow'), may hold values from 0 to 5, as said below
- galerkin_blocks: bfloat16 [3, 8, 16, 5, 64, 64], P(None, 'wide', 'narrow'), as said below
- restrict_cols: int32 [3, 8, 16, 3], P(None, 'wide', 'narrow'), may hold values from 0 to 7, as said below
- restrict_blocks: bfloat16 [3, 8, 16, 3, 64, 64], P(None, 'wide', 'narrow'), as said below
- prolong_cols: int32 [3, 8, 16, 2], P(None, 'wide', 'narrow'), may hold values from 0 to 3, as said below
- prolong_blocks: bfloat16 [3, 8, 16, 2, 64, 64], P(None, 'wide', 'narrow'), as said below
- coarse_inverse: bfloat16 [1024, 1024], P('narrow'), may hold values from -1.5 to 1.5
Outputs:
- correction: float32 [8, 1024, 512], P('wide', 'narrow')
The draws below stay inside these ranges and needn't reach their ends.
Inputs may be any that keep to these rules, and one draw needn't show every extreme that they name: `galerkin_cols`: slot 0 of every block row names the row's own block; values below 4 name blocks of the same piece, 4 the last block of the piece before, 5 the first block of the piece after. At level k the entries of the 2**k subdomains of a group are equal. `galerkin_blocks`: at level k the blocks of the 2**k subdomains of a group are equal. The diagonal entries of every slot-0 block lie between 1 and 4. `restrict_cols`: values below 4 name blocks of the lower joined group, the others block value - 4 of the upper one; slots 0 and 1 of coarse block c name c and 4 + c. At level k the entries of the 2**(k+1) subdomains of a coarse group are equal. `restrict_blocks`: at level k the blocks of the 2**(k+1) subdomains of a coarse group are equal. `prolong_cols`: slot 0 names the fine block's own index. At level k the entries of the 2**k subdomains of a group are equal. `prolong_blocks`: at level k the blocks of the 2**k subdomains of a group are equal.
All inputs are finite; a program needn't handle non-finite values.
Results may differ from the reference program's by a relative error of at most 0.035.
Values may be sent and summed in bfloat16 or wider, within the bound.
No kernel may reach another device: no remote copies, remote signals or barrier semaphores. Data moves between devices by JAX's collectives and lax.ppermute only.
A program may use at most 64 MiB of HBM per device.

```python
import math
import jax
import jax.numpy as jnp
from jax import lax

BS = 64
NB = 4
NNZ = 5
NNZ_R = 3
NNZ_P = 2
NRHS = 512
LEVELS = 3
SUBDOMAINS = 8
GROUP_ROWS = 16
N_NARROW = 4


def spread_levels(key, extra_shift, make_level):
    per_level = []
    for level_idx in range(LEVELS):
        stride = 2 ** (level_idx + extra_shift)
        base_draw = make_level(jax.random.fold_in(key, level_idx), SUBDOMAINS // stride)
        per_level.append(jnp.repeat(base_draw, stride, axis=0))
    return jnp.stack(per_level)


def row_blocks():
    return (jnp.arange(GROUP_ROWS, dtype=jnp.int32) % NB)[None, :, None]


def mixed_normal(sub_key, shape, scale):
    values = jax.random.normal(sub_key, shape, jnp.float32) * scale
    return values


def draw_galerkin_cols(key, part):

    def make_level(sub_key, group_count):
        random_ids = jax.random.randint(sub_key, (group_count, GROUP_ROWS, NNZ), 0, NB + 2, dtype=jnp.int32)
        slot_ids = jnp.arange(NNZ, dtype=jnp.int32)[None, None, :]
        own_block = row_blocks()
        chosen = jnp.where(slot_ids == 0, own_block, random_ids)
        chosen = jnp.where((slot_ids == 1) & (own_block == 0), NB, chosen)
        chosen = jnp.where((slot_ids == 2) & (own_block == NB - 1), NB + 1, chosen)
        return chosen.astype(jnp.int32)
    return spread_levels(key, 0, make_level)


def draw_galerkin_blocks(key, part):

    def make_level(sub_key, group_count):
        coupling = mixed_normal(jax.random.fold_in(sub_key, 1), (group_count, GROUP_ROWS, NNZ, BS, BS), 0.08)
        pivots = jnp.exp(jax.random.uniform(jax.random.fold_in(sub_key, 2), (group_count, GROUP_ROWS, BS), jnp.float32, 0.0, math.log(4.0)))
        on_diag = (jnp.arange(NNZ) == 0)[:, None, None] & jnp.eye(BS, dtype=bool)[None, :, :]
        result = jnp.where(on_diag[None, None], pivots[:, :, None, :, None], coupling)
        return result.astype(jnp.bfloat16)
    return spread_levels(key, 0, make_level)


def draw_restrict_cols(key, part):

    def make_level(sub_key, group_count):
        random_ids = jax.random.randint(sub_key, (group_count, GROUP_ROWS, NNZ_R), 0, 2 * NB, dtype=jnp.int32)
        slot_ids = jnp.arange(NNZ_R, dtype=jnp.int32)[None, None, :]
        own_block = row_blocks()
        chosen = jnp.where(slot_ids == 0, own_block, random_ids)
        chosen = jnp.where(slot_ids == 1, own_block + NB, chosen)
        return chosen.astype(jnp.int32)
    return spread_levels(key, 1, make_level)


def draw_restrict_blocks(key, part):

    def make_level(sub_key, group_count):
        result = mixed_normal(sub_key, (group_count, GROUP_ROWS, NNZ_R, BS, BS), 1.55 / math.sqrt(NNZ_R * BS))
        return result.astype(jnp.bfloat16)
    return spread_levels(key, 1, make_level)


def draw_prolong_cols(key, part):

    def make_level(sub_key, group_count):
        random_ids = jax.random.randint(sub_key, (group_count, GROUP_ROWS, NNZ_P), 0, NB, dtype=jnp.int32)
        slot_ids = jnp.arange(NNZ_P, dtype=jnp.int32)[None, None, :]
        chosen = jnp.where(slot_ids == 0, row_blocks(), random_ids)
        return chosen.astype(jnp.int32)
    return spread_levels(key, 0, make_level)


def draw_prolong_blocks(key, part):

    def make_level(sub_key, group_count):
        result = mixed_normal(sub_key, (group_count, GROUP_ROWS, NNZ_P, BS, BS), 1.5 / math.sqrt(NNZ_P * BS))
        return result.astype(jnp.bfloat16)
    return spread_levels(key, 0, make_level)


def steps_of(rng, shape, shards, low, largest):
    factor_of, own = 1.0, jax.random.fold_in(rng, 6)
    for position, shards_of in shards:
        heights = jnp.exp(jax.random.uniform(jax.random.fold_in(own, position), (shards_of,), jnp.float32, low / len(shards), largest / len(shards)))
        factor_of = factor_of * jnp.repeat(heights, shape[position] // shards_of).reshape([-1 if axis == position else 1 for axis in range(len(shape))])
    return factor_of


def gaussian(key, dims, spread, most, cuts=(), held_as=jnp.bfloat16):
    entries = jax.random.normal(key, dims, jnp.float32) * spread
    if len(cuts) > 0:
        entries = steps_of(key, dims, cuts, -0.22, 0.18) * entries
    return jnp.clip(entries, min=-most, max=most).astype(held_as)


def setup_inputs(seed: int = 0) -> dict:
    seeds = jax.random.split(jax.random.key(seed), 9)
    return {
        "level_rhs": gaussian(seeds[0], (SUBDOMAINS, GROUP_ROWS * BS, NRHS), 1.0, 6.0, ((0, 8), (1, 4)), jnp.float32),
        "galerkin_cols": draw_galerkin_cols(jax.random.fold_in(seeds[8], 71), 0),
        "galerkin_blocks": draw_galerkin_blocks(jax.random.fold_in(seeds[8], 71), 0),
        "restrict_cols": draw_restrict_cols(jax.random.fold_in(seeds[8], 71), 0),
        "restrict_blocks": draw_restrict_blocks(jax.random.fold_in(seeds[8], 71), 0),
        "prolong_cols": draw_prolong_cols(jax.random.fold_in(seeds[8], 71), 0),
        "prolong_blocks": draw_prolong_blocks(jax.random.fold_in(seeds[8], 71), 0),
        "coarse_inverse": gaussian(seeds[7], (GROUP_ROWS * BS, GROUP_ROWS * BS), (GROUP_ROWS * BS // 64) ** -0.5, 1.5, ((0, 4),)),
    }


relax_down = 0.7
relax_up = 0.5


def rim_extend(pieces, with_rims):
    zero_block = jnp.zeros((1, 1) + pieces.shape[2:], pieces.dtype)
    if with_rims:
        before = jnp.concatenate([zero_block, pieces[:-1, -1:]], axis=0)
        after = jnp.concatenate([pieces[1:, :1], zero_block], axis=0)
    else:
        before = jnp.zeros_like(pieces[:, :1])
        after = jnp.zeros_like(pieces[:, :1])
    return jnp.concatenate([pieces, before, after], axis=1)


def pick_piece(source_piece, piece_ids):
    return source_piece[piece_ids]


def take_blocks(source, col_ids):
    return jax.vmap(pick_piece)(source, col_ids)


def block_sum(blocks, picked):
    return jnp.einsum("jbsrc,jbscn->jbrn", blocks.astype(jnp.float32), picked.astype(jnp.float32), precision=lax.Precision.HIGHEST)


def apply_rims(operands):
    col_ids, blocks, rounded = operands
    return block_sum(blocks, take_blocks(rim_extend(rounded, True), col_ids))


def apply_local(operands):
    col_ids, blocks, rounded = operands
    return block_sum(blocks, take_blocks(rim_extend(rounded, False), col_ids))


def transfer(operands):
    col_ids, blocks, source = operands
    return block_sum(blocks, take_blocks(source, col_ids))


def reference(level_rhs, galerkin_cols, galerkin_blocks, restrict_cols, restrict_blocks, prolong_cols, prolong_blocks, coarse_inverse):
    current = level_rhs.reshape(SUBDOMAINS, N_NARROW, NB, BS, NRHS)
    stored = []
    for level_idx in range(LEVELS):
        stride = 2 ** level_idx
        groups = SUBDOMAINS // stride
        col_ids = galerkin_cols[level_idx, ::stride].reshape(groups, N_NARROW, NB, NNZ)
        blocks = galerkin_blocks[level_idx, ::stride].reshape(groups, N_NARROW, NB, NNZ, BS, BS)
        diagonal = jnp.diagonal(blocks[:, :, :, 0], axis1=-2, axis2=-1).astype(jnp.float32)[..., None]
        smoothed = relax_down * current / diagonal
        applied = lax.map(apply_rims, (col_ids, blocks, smoothed.astype(jnp.bfloat16)))
        residual = (current - applied).astype(jnp.bfloat16)
        paired = residual.reshape(groups // 2, 2, N_NARROW, NB, BS, NRHS)
        union = jnp.concatenate([paired[:, 0], paired[:, 1]], axis=2)
        rest_ids = restrict_cols[level_idx, ::2 * stride].reshape(groups // 2, N_NARROW, NB, NNZ_R)
        rest_blocks = restrict_blocks[level_idx, ::2 * stride].reshape(groups // 2, N_NARROW, NB, NNZ_R, BS, BS)
        stored.append((current, smoothed, diagonal, col_ids, blocks))
        current = lax.map(transfer, (rest_ids, rest_blocks, union))
    flat_rhs = current.astype(jnp.bfloat16).reshape(GROUP_ROWS * BS, NRHS)
    solution = jnp.dot(coarse_inverse, flat_rhs, preferred_element_type=jnp.float32).reshape(1, N_NARROW, NB, BS, NRHS)
    for level_idx in reversed(range(LEVELS)):
        stride = 2 ** level_idx
        groups = SUBDOMAINS // stride
        fine_rhs, smoothed, diagonal, col_ids, blocks = stored[level_idx]
        coarse_bf = jnp.repeat(solution.astype(jnp.bfloat16), 2, axis=0)
        pro_ids = prolong_cols[level_idx, ::stride].reshape(groups, N_NARROW, NB, NNZ_P)
        pro_blocks = prolong_blocks[level_idx, ::stride].reshape(groups, N_NARROW, NB, NNZ_P, BS, BS)
        updated = smoothed + lax.map(transfer, (pro_ids, pro_blocks, coarse_bf))
        applied = lax.map(apply_local, (col_ids, blocks, updated.astype(jnp.bfloat16)))
        solution = updated + relax_up * (fine_rhs - applied) / diagonal
    return solution.reshape(SUBDOMAINS, GROUP_ROWS * BS, NRHS)
```

```python
import functools

import jax
import jax.numpy as jnp
from jax import lax
from jax.experimental import pallas as pl
from jax.experimental.pallas import tpu as pltpu
from jax.sharding import PartitionSpec as P

relax_down = 0.7
relax_up = 0.5
f32 = jnp.float32
bf16 = jnp.bfloat16
grant = 12 * 1024 * 1024


def matmul(a, b):
    return jnp.dot(a, b, preferred_element_type=f32)


def array(shape, dtype):
    return jax.ShapeDtypeStruct(shape, dtype)


def whole():
    return pl.BlockSpec(memory_space=pltpu.VMEM)


def level_block(value, level_idx):
    shape = (1,) + value.shape[1:]
    return pl.BlockSpec(shape, lambda i: (level_idx,) + (0,) * (value.ndim - 1))


def scalars():
    return pl.BlockSpec(memory_space=pltpu.SMEM)


def run(body, name, outs, operands, flops=0):
    arrays = [o[0] if isinstance(o, tuple) else o for o in operands]
    specs = [o[1] if isinstance(o, tuple) else whole() for o in operands]
    windows = any(isinstance(o, tuple) and o[1].block_shape is not None for o in operands)
    moved = sum(a.size * a.dtype.itemsize for a in arrays)
    return pl.pallas_call(
        body,
        grid=(1,) if windows else (),
        out_shape=outs,
        in_specs=specs,
        out_specs=[pl.BlockSpec(memory_space=pltpu.VMEM)] * len(outs),
        compiler_params=pltpu.CompilerParams(vmem_limit_bytes=grant),
        cost_estimate=pl.CostEstimate(flops=flops, bytes_accessed=moved, transcendentals=0),
        name=name,
    )(*arrays)


def diagonal_of(block):
    size = block.shape[0]
    rows = lax.broadcasted_iota(jnp.int32, (size, size), 0)
    lanes = lax.broadcasted_iota(jnp.int32, (size, size), 1)
    return jnp.sum(jnp.where(rows == lanes, block, 0.0), axis=1, keepdims=True)


def placed(base, others, ids, target):
    total = base
    for block, ident in zip(others, ids):
        term = block * jnp.where(ident == target, 1.0, 0.0).astype(f32)
        total = term if total is None else total + term
    return total


def parity_of():
    return lax.rem(lax.axis_index("narrow"), 2)


def put_ends(first, last, even_ref, odd_ref):
    even = parity_of() == 0
    even_ref[...] = jnp.where(even, last, first)
    odd_ref[...] = jnp.where(even, first, last)


def assemble_galerkin(level_idx, cols, blocks, local_ref, rim_ref, scale_ref):
    count, slots, size = blocks.shape[2], blocks.shape[3], blocks.shape[4]
    parity = parity_of()
    for b in range(count):
        held = [blocks[0, 0, b, s].astype(f32) for s in range(slots)]
        ids = [cols[level_idx, 0, b, s] for s in range(1, slots)]
        rows = pl.ds(b * size, size)
        scale_ref[rows, :] = 1.0 / diagonal_of(held[0])
        line = [placed(held[0] if c == b else None, held[1:], ids, c) for c in range(count)]
        local_ref[rows, :] = jnp.concatenate(line, axis=1).astype(bf16)
        rims = [
            placed(None, held[1:], ids, count + 1 - parity),
            placed(None, held[1:], ids, count + parity),
        ]
        rim_ref[rows, :] = jnp.concatenate(rims, axis=1).astype(bf16)


def assemble_restrict(level_idx, cols, blocks, out_ref):
    count, slots, size = blocks.shape[2], blocks.shape[3], blocks.shape[4]
    for b in range(count):
        held = [blocks[0, 0, b, s].astype(f32) for s in range(slots)]
        ids = [cols[level_idx, 0, b, s] for s in range(2, slots)]
        fixed = {b: held[0], count + b: held[1]}
        line = [placed(fixed.get(c), held[2:], ids, c) for c in range(2 * count)]
        out_ref[pl.ds(b * size, size), :] = jnp.concatenate(line, axis=1).astype(bf16)


def assemble_prolong(level_idx, cols, blocks, out_ref):
    count, slots, size = blocks.shape[2], blocks.shape[3], blocks.shape[4]
    for b in range(count):
        held = [blocks[0, 0, b, s].astype(f32) for s in range(slots)]
        ids = [cols[level_idx, 0, b, s] for s in range(1, slots)]
        line = [placed(held[0] if c == b else None, held[1:], ids, c) for c in range(count)]
        out_ref[pl.ds(b * size, size), :] = jnp.concatenate(line, axis=1).astype(bf16)


def start_kernel(first_rhs, last_rhs, first_block, last_block, even_ref, odd_ref):
    first = first_rhs[0] * (relax_down / diagonal_of(first_block[0, 0, 0, 0].astype(f32)))
    last = last_rhs[0] * (relax_down / diagonal_of(last_block[0, 0, 0, 0].astype(f32)))
    put_ends(first.astype(bf16), last.astype(bf16), even_ref, odd_ref)


def first_local_kernel(rhs, _, cols, blocks, rcols, rblocks, rest, local, rim, scale, rmat):
    assemble_galerkin(0, cols, blocks, local, rim, scale)
    smoothed = (rhs[0] * (relax_down * scale[...])).astype(bf16)
    rest[...] = rhs[0] - matmul(local[...], smoothed)
    assemble_restrict(0, rcols, rblocks, rmat)


def split_residual_kernel(rest, rim, from_even, from_odd, sent, kept):
    half = sent.shape[1]
    upper = lax.rem(lax.axis_index("wide"), 2)
    for ref, side in ((sent, 1 - upper), (kept, upper)):
        lanes = pl.ds(pl.multiple_of(side * half, half), half)
        rims = jnp.concatenate([from_even[:, lanes], from_odd[:, lanes]], axis=0)
        ref[...] = (rest[:, lanes] - matmul(rim[...], rims)).astype(bf16)


def residual_kernel(rest, rim, from_even, from_odd, out):
    rims = jnp.concatenate([from_even[...], from_odd[...]], axis=0)
    out[...] = (rest[...] - matmul(rim[...], rims)).astype(bf16)


def side_of(rmat, level_idx, own):
    width = rmat.shape[1] // 2
    bit = lax.axis_index("wide") >> level_idx & 1
    side = bit if own else 1 - bit
    return rmat[:, pl.ds(pl.multiple_of(side * width, width), width)]


def own_part_kernel(level_idx, residual, rmat, *refs):
    if len(refs) > 1:
        cols, blocks, rcols, rblocks, part, local, rim, scale, next_rmat = refs
        part[...] = matmul(side_of(rmat, level_idx, True), residual[...])
        assemble_galerkin(level_idx + 1, cols, blocks, local, rim, scale)
        assemble_restrict(level_idx + 1, rcols, rblocks, next_rmat)
    else:
        (part,) = refs
        part[...] = matmul(side_of(rmat, level_idx, True), residual[...])


def join_kernel(level_idx, part, rmat, other, scale, rhs, smoothed, even_ref, odd_ref):
    size = even_ref.shape[0]
    current = part[...] + matmul(side_of(rmat, level_idx, False), other[...])
    rhs[...] = current
    rounded = (current * (relax_down * scale[...])).astype(bf16)
    smoothed[...] = rounded
    put_ends(rounded[:size], rounded[-size:], even_ref, odd_ref)


def last_join_kernel(level_idx, part, rmat, other, rounded):
    current = part[...] + matmul(side_of(rmat, level_idx, False), other[...])
    rounded[...] = current.astype(bf16)


def local_kernel(rhs, local, smoothed, rest):
    rest[...] = rhs[...] - matmul(local[...], smoothed[...])


def inverse_part(inverse, part, offset):
    depth = part.shape[0]
    piece = lax.axis_index("narrow") ^ offset
    return matmul(inverse[:, pl.ds(pl.multiple_of(piece * depth, depth), depth)], part[...])


def coarse_kernel(offsets, with_total, *refs):
    inverse, parts, refs = refs[0], refs[1 : 1 + len(offsets)], refs[1 + len(offsets) :]
    total = refs[0][...] if with_total else None
    for part, offset in zip(parts, offsets):
        term = inverse_part(inverse, part, offset)
        total = term if total is None else total + term
    refs[-1][...] = total


def prolong_kernel(levels, pcols, *refs):
    for level_idx, blocks, out in zip(levels, refs[: len(levels)], refs[len(levels) :]):
        assemble_prolong(level_idx, pcols, blocks, out)


def raise_level(coarse, rhs, scale, local, pmat):
    updated = rhs * (relax_down * scale) + matmul(pmat, coarse)
    applied = matmul(local, updated.astype(bf16))
    return updated + (relax_up * scale) * (rhs - applied)


def up_kernel(offset, depth, inverse, part, total, *refs):
    value = total[...] + inverse_part(inverse, part, offset)
    for step in range(depth):
        rhs, scale, local, pmat = refs[4 * step : 4 * step + 4]
        value = raise_level(value.astype(bf16), rhs[...], scale[...], local[...], pmat[...])
    refs[-1][...] = value.astype(bf16)


def final_own_kernel(coarse, rhs, scale, local, pmat, out):
    half = coarse.shape[1]
    side = lax.rem(lax.axis_index("wide"), 2)
    lanes = pl.ds(pl.multiple_of(side * half, half), half)
    out[...] = raise_level(coarse[...], rhs[0, :, lanes], scale[...], local[...], pmat[...])


def final_kernel(own, coarse, rhs, scale, local, pmat, out):
    half = coarse.shape[1]
    side = lax.rem(lax.axis_index("wide"), 2)
    lanes = pl.ds(pl.multiple_of(side * half, half), half)
    out[0, :, lanes] = own[...]
    lanes = pl.ds(pl.multiple_of((1 - side) * half, half), half)
    out[0, :, lanes] = raise_level(coarse[...], rhs[0, :, lanes], scale[...], local[...], pmat[...])


def exchange(value, axis, bit):
    count = lax.axis_size(axis)
    return lax.ppermute(value, axis, [(i, i ^ bit) for i in range(count)])


def swap_ends(even, odd):
    count = lax.axis_size("narrow")
    pairs = [(i, i ^ 1) for i in range(count) if i ^ 1 < count]
    gaps = [(i, i + 1) for i in range(1, count - 1, 2)]
    gaps = gaps + [(b, a) for a, b in gaps]
    return lax.ppermute(even, "narrow", pairs), lax.ppermute(odd, "narrow", gaps)


def on_device(
    level_rhs,
    galerkin_cols,
    galerkin_blocks,
    restrict_cols,
    restrict_blocks,
    prolong_cols,
    prolong_blocks,
    coarse_inverse,
):
    levels = galerkin_cols.shape[0]
    count = galerkin_cols.shape[2]
    size = galerkin_blocks.shape[-1]
    rows, fields = level_rhs.shape[1:]
    half = fields // 2
    gcols, rcols, pcols = ((c, scalars()) for c in (galerkin_cols, restrict_cols, prolong_cols))
    local_shape = array((rows, rows), bf16)
    rim_shape = array((rows, 2 * size), bf16)
    scale_shape = array((rows, 1), f32)
    rmat_shape = array((rows, 2 * rows), bf16)

    def ends(width):
        return array((size, width), bf16)

    def of_level(value, level_idx):
        return value, level_block(value, level_idx)

    def end_rows(which):
        return level_rhs, pl.BlockSpec((1, size, fields), lambda i: (0, which, 0))

    def end_block(which):
        return galerkin_blocks, pl.BlockSpec((1, 1, 1, 1, size, size), lambda i: (0, 0, which, 0, 0, 0))

    even, odd = run(
        start_kernel, "start", [ends(fields), ends(fields)],
        [end_rows(0), end_rows(count - 1), end_block(0), end_block(count - 1)],
    )
    from_even, from_odd = swap_ends(even, odd)
    rest, local, rim, scale, rmat = run(
        first_local_kernel, "first_local",
        [array((rows, fields), f32), local_shape, rim_shape, scale_shape, rmat_shape],
        [level_rhs, even, gcols, of_level(galerkin_blocks, 0), rcols, of_level(restrict_blocks, 0)],
        flops=2 * rows * rows * fields,
    )
    operators = [(local, scale)]
    sent, kept = run(
        split_residual_kernel, "split_residual", [array((rows, half), bf16)] * 2,
        [rest, rim, from_even, from_odd],
    )
    right_sides = [None]
    for level_idx in range(levels):
        other = exchange(sent, "wide", 1 << level_idx)
        square = 2 * rows * rows * half
        if level_idx + 1 < levels:
            part, local, rim, scale, next_rmat = run(
                functools.partial(own_part_kernel, level_idx), "own_part",
                [array((rows, half), f32), local_shape, rim_shape, scale_shape, rmat_shape],
                [kept, rmat, gcols, of_level(galerkin_blocks, level_idx + 1),
                 rcols, of_level(restrict_blocks, level_idx + 1)],
                flops=square,
            )
            operators.append((local, scale))
            rhs, smoothed, even, odd = run(
                functools.partial(join_kernel, level_idx), "join",
                [array((rows, half), f32), array((rows, half), bf16), ends(half), ends(half)],
                [part, rmat, other, scale],
                flops=square,
            )
            right_sides.append(rhs)
            rmat = next_rmat
            from_even, from_odd = swap_ends(even, odd)
            (rest,) = run(
                local_kernel, "local", [array((rows, half), f32)], [rhs, local, smoothed], flops=square
            )
            (sent,) = run(
                residual_kernel, "residual", [array((rows, half), bf16)], [rest, rim, from_even, from_odd]
            )
            kept = sent
        else:
            (part,) = run(
                functools.partial(own_part_kernel, level_idx), "own_part",
                [array((rows, half), f32)], [kept, rmat], flops=square,
            )
            (mine,) = run(
                functools.partial(last_join_kernel, level_idx), "last_join",
                [array((rows, half), bf16)], [part, rmat, other], flops=square,
            )
    pmats = run(
        functools.partial(prolong_kernel, tuple(range(levels))), "prolong_ops",
        [local_shape] * levels,
        [pcols] + [of_level(prolong_blocks, level_idx) for level_idx in range(levels)],
    )
    pieces = lax.axis_size("narrow")
    parts = {0: mine}
    order = sorted(range(1, pieces), key=lambda o: (bin(o).count("1"), -o))
    for offset in order:
        low = offset & -offset
        parts[offset] = exchange(parts[offset ^ low], "narrow", low)
    total_shape = [array((rows, half), f32)]
    square = 2 * rows * rows * half
    (total,) = run(
        functools.partial(coarse_kernel, (0,), False), "coarse_own", total_shape,
        [coarse_inverse, mine], flops=square,
    )
    middle = tuple(order[:-1])
    if middle:
        (total,) = run(
            functools.partial(coarse_kernel, middle, True), "coarse_middle", total_shape,
            [coarse_inverse] + [parts[o] for o in middle] + [total], flops=square * len(middle),
        )
    operands = []
    for level_idx in reversed(range(1, levels)):
        local, scale = operators[level_idx]
        operands += [right_sides[level_idx], scale, local, pmats[level_idx]]
    (coarse,) = run(
        functools.partial(up_kernel, order[-1], levels - 1), "up", [array((rows, half), bf16)],
        [coarse_inverse, parts[order[-1]], total] + operands, flops=square * (1 + 2 * (levels - 1)),
    )
    other = exchange(coarse, "wide", 1)
    local, scale = operators[0]
    (own,) = run(
        final_own_kernel, "final_own", [array((rows, half), f32)],
        [coarse, level_rhs, scale, local, pmats[0]], flops=2 * square,
    )
    (result,) = run(
        final_kernel, "final", [array((1, rows, fields), f32)],
        [own, other, level_rhs, scale, local, pmats[0]], flops=2 * square,
    )
    return result


def solution(mesh):
    in_specs = (
        P("wide", "narrow", None),
        P(None, "wide", "narrow", None),
        P(None, "wide", "narrow", None, None, None),
        P(None, "wide", "narrow", None),
        P(None, "wide", "narrow", None, None, None),
        P(None, "wide", "narrow", None),
        P(None, "wide", "narrow", None, None, None),
        P("narrow", None),
    )
    out_specs = P("wide", "narrow", None)
    return jax.shard_map(
        on_device, mesh=mesh, in_specs=in_specs, out_specs=out_specs, check_vma=False
    )
```

```python
import functools

import jax
import jax.numpy as jnp
from jax import lax
from jax.experimental import pallas as pl
from jax.experimental.pallas import tpu as pltpu
from jax.sharding import PartitionSpec as P

relax_down = 0.7
relax_up = 0.5
f32 = jnp.float32
bf16 = jnp.bfloat16
grant = 12 * 1024 * 1024


def matmul(a, b):
    return jnp.dot(a, b, preferred_element_type=f32)


def array(shape, dtype):
    return jax.ShapeDtypeStruct(shape, dtype)


def whole():
    return pl.BlockSpec(memory_space=pltpu.VMEM)


def level_block(value, level_idx):
    shape = (1,) + value.shape[1:]
    return pl.BlockSpec(shape, lambda i: (level_idx,) + (0,) * (value.ndim - 1))


def scalars():
    return pl.BlockSpec(memory_space=pltpu.SMEM)


def in_hbm(value):
    return pltpu.with_memory_space_constraint(value, pltpu.HBM), pl.BlockSpec(memory_space=pltpu.HBM)


def run(body, name, outs, operands, flops=0, scratch=()):
    arrays = [o[0] if isinstance(o, tuple) else o for o in operands]
    specs = [o[1] if isinstance(o, tuple) else whole() for o in operands]
    windows = any(isinstance(o, tuple) and o[1].block_shape is not None for o in operands)
    moved = sum(a.size * a.dtype.itemsize for a in arrays)
    return pl.pallas_call(
        body,
        grid=(1,) if windows else (),
        out_shape=outs,
        in_specs=specs,
        out_specs=[pl.BlockSpec(memory_space=pltpu.VMEM)] * len(outs),
        scratch_shapes=list(scratch),
        compiler_params=pltpu.CompilerParams(vmem_limit_bytes=grant),
        cost_estimate=pl.CostEstimate(flops=flops, bytes_accessed=moved, transcendentals=0),
        name=name,
    )(*arrays)


def diagonal_of(block):
    size = block.shape[0]
    rows = lax.broadcasted_iota(jnp.int32, (size, size), 0)
    lanes = lax.broadcasted_iota(jnp.int32, (size, size), 1)
    return jnp.sum(jnp.where(rows == lanes, block, 0.0), axis=1, keepdims=True)


def placed(base, others, ids, target):
    total = base
    for block, ident in zip(others, ids):
        term = block * jnp.where(ident == target, 1.0, 0.0).astype(f32)
        total = term if total is None else total + term
    return total


def parity_of():
    return lax.rem(lax.axis_index("narrow"), 2)


def put_ends(first, last, ends_ref):
    size = first.shape[0]
    even = parity_of() == 0
    ends_ref[:size, :] = jnp.where(even, last, first)
    ends_ref[size:, :] = jnp.where(even, first, last)


def assemble_galerkin(level_idx, cols, blocks, local_ref, rim_ref, scale_ref):
    count, slots, size = blocks.shape[2], blocks.shape[3], blocks.shape[4]
    parity = parity_of()
    for b in range(count):
        held = [blocks[0, 0, b, s].astype(f32) for s in range(slots)]
        ids = [cols[level_idx, 0, b, s] for s in range(1, slots)]
        rows = pl.ds(b * size, size)
        scale_ref[rows, :] = 1.0 / diagonal_of(held[0])
        line = [placed(held[0] if c == b else None, held[1:], ids, c) for c in range(count)]
        local_ref[rows, :] = jnp.concatenate(line, axis=1).astype(bf16)
        rims = [
            placed(None, held[1:], ids, count + 1 - parity),
            placed(None, held[1:], ids, count + parity),
        ]
        rim_ref[rows, :] = jnp.concatenate(rims, axis=1).astype(bf16)


def assemble_restrict(level_idx, cols, blocks, out_ref):
    count, slots, size = blocks.shape[2], blocks.shape[3], blocks.shape[4]
    for b in range(count):
        held = [blocks[0, 0, b, s].astype(f32) for s in range(slots)]
        ids = [cols[level_idx, 0, b, s] for s in range(2, slots)]
        fixed = {b: held[0], count + b: held[1]}
        line = [placed(fixed.get(c), held[2:], ids, c) for c in range(2 * count)]
        out_ref[pl.ds(b * size, size), :] = jnp.concatenate(line, axis=1).astype(bf16)


def assemble_prolong(level_idx, cols, blocks, out_ref):
    count, slots, size = blocks.shape[2], blocks.shape[3], blocks.shape[4]
    for b in range(count):
        held = [blocks[0, 0, b, s].astype(f32) for s in range(slots)]
        ids = [cols[level_idx, 0, b, s] for s in range(1, slots)]
        line = [placed(held[0] if c == b else None, held[1:], ids, c) for c in range(count)]
        out_ref[pl.ds(b * size, size), :] = jnp.concatenate(line, axis=1).astype(bf16)


def start_kernel(rhs, blocks, ends_ref, rows, pivots, sems):
    count, size = blocks.shape[2], blocks.shape[4]
    copies = []
    for slot, which in enumerate((0, count - 1)):
        source = rhs.at[0, pl.ds(which * size, size), :]
        copies.append(pltpu.make_async_copy(source, rows.at[slot], sems.at[slot]))
        source = blocks.at[0, 0, which, 0]
        copies.append(pltpu.make_async_copy(source, pivots.at[slot], sems.at[2 + slot]))
    for copy in copies:
        copy.start()
    for copy in copies:
        copy.wait()
    first, last = (
        (rows[slot] * (relax_down / diagonal_of(pivots[slot].astype(f32)))).astype(bf16)
        for slot in range(2)
    )
    put_ends(first, last, ends_ref)


def first_local_kernel(rhs, _, cols, blocks, rcols, rblocks, rest, local, rim, scale, rmat):
    assemble_galerkin(0, cols, blocks, local, rim, scale)
    smoothed = (rhs[0] * (relax_down * scale[...])).astype(bf16)
    rest[...] = rhs[0] - matmul(local[...], smoothed)
    assemble_restrict(0, rcols, rblocks, rmat)


def bit_of(level_idx):
    return lax.axis_index("wide") >> level_idx & 1


def residual_kernel(level_idx, rest, rim, inner, outer, *refs):
    size = outer.shape[0]
    if len(refs) == 1:
        rims = jnp.concatenate([inner[:size, :], outer[...]], axis=0)
        refs[0][...] = (rest[...] - matmul(rim[...], rims)).astype(bf16)
    else:
        half = refs[0].shape[1]
        bit = bit_of(level_idx)
        for ref, side in zip(refs, (1 - bit, bit)):
            lanes = pl.ds(pl.multiple_of(side * half, half), half)
            rims = jnp.concatenate([inner[:size, lanes], outer[:, lanes]], axis=0)
            ref[...] = (rest[:, lanes] - matmul(rim[...], rims)).astype(bf16)


def side_of(rmat, level_idx, own):
    width = rmat.shape[1] // 2
    bit = bit_of(level_idx)
    side = bit if own else 1 - bit
    return rmat[:, pl.ds(pl.multiple_of(side * width, width), width)]


def own_part_kernel(level_idx, residual, rmat, cols, blocks, rcols, rblocks, *refs):
    part, local, rim, scale, next_rmat = refs
    part[...] = matmul(side_of(rmat, level_idx, True), residual[...])
    assemble_galerkin(level_idx + 1, cols, blocks, local, rim, scale)
    assemble_restrict(level_idx + 1, rcols, rblocks, next_rmat)


def last_part_kernel(level_idx, levels, residual, rmat, pcols, *refs):
    refs[levels][...] = matmul(side_of(rmat, level_idx, True), residual[...])
    for idx, blocks, out in zip(range(levels), refs[:levels], refs[levels + 1 :]):
        assemble_prolong(idx, pcols, blocks, out)


def join_kernel(level_idx, part, rmat, other, scale, rhs, smoothed, ends_ref):
    size = ends_ref.shape[0] // 2
    current = part[...] + matmul(side_of(rmat, level_idx, False), other[...])
    rhs[...] = current
    rounded = (current * (relax_down * scale[...])).astype(bf16)
    smoothed[...] = rounded
    put_ends(rounded[:size], rounded[-size:], ends_ref)


def last_join_kernel(level_idx, part, rmat, other, rounded):
    current = part[...] + matmul(side_of(rmat, level_idx, False), other[...])
    rounded[...] = current.astype(bf16)


def local_kernel(rhs, local, smoothed, rest):
    rest[...] = rhs[...] - matmul(local[...], smoothed[...])


def inverse_part(inverse, part, offset):
    depth = part.shape[0]
    piece = lax.axis_index("narrow") ^ offset
    return matmul(inverse[:, pl.ds(pl.multiple_of(piece * depth, depth), depth)], part[...])


def coarse_kernel(offsets, with_total, *refs):
    inverse, parts, refs = refs[0], refs[1 : 1 + len(offsets)], refs[1 + len(offsets) :]
    total = refs[0][...] if with_total else None
    for part, offset in zip(parts, offsets):
        term = inverse_part(inverse, part, offset)
        total = term if total is None else total + term
    refs[-1][...] = total


def raise_level(coarse, rhs, scale, local, pmat):
    updated = rhs * (relax_down * scale) + matmul(pmat, coarse)
    applied = matmul(local, updated.astype(bf16))
    return updated + (relax_up * scale) * (rhs - applied)


def up_kernel(offset, depth, inverse, part, total, *refs):
    value = total[...] + inverse_part(inverse, part, offset)
    for step in range(depth):
        rhs, scale, local, pmat = refs[4 * step : 4 * step + 4]
        value = raise_level(value.astype(bf16), rhs[...], scale[...], local[...], pmat[...])
    refs[-1][...] = value.astype(bf16)


def lanes_of(place, width):
    start = 0
    for level_idx, flip, step in place:
        start = start + (bit_of(level_idx) ^ flip) * step
    return pl.ds(pl.multiple_of(start, width), width)


def raise_kernel(places, last, *refs):
    count = len(places)
    coarse, outs = refs[:count], refs[-count:]
    rhs, scale, local, pmat = refs[count : count + 4]
    for place, value, out in zip(places, coarse, outs):
        lanes = lanes_of(place, value.shape[1])
        held = rhs[0, :, lanes] if last else rhs[:, lanes]
        raised = raise_level(value[...], held, scale[...], local[...], pmat[...])
        out[...] = raised.astype(out.dtype)


def final_kernel(places, made, *refs):
    count = len(places)
    for place, value in zip(places[:made], refs[:made]):
        out = refs[-1]
        out[0, :, lanes_of(place, value.shape[1])] = value[...]
    rhs, scale, local, pmat, out = refs[count:]
    for place, value in zip(places[made:], refs[made:count]):
        lanes = lanes_of(place, value.shape[1])
        out[0, :, lanes] = raise_level(
            value[...], rhs[0, :, lanes], scale[...], local[...], pmat[...]
        )


def exchange(value, axis, bit):
    count = lax.axis_size(axis)
    return lax.ppermute(value, axis, [(i, i ^ bit) for i in range(count)])


def swap_ends(ends):
    count = lax.axis_size("narrow")
    size = ends.shape[0] // 2
    inner = exchange(ends, "narrow", 1)
    onward = [(i, i + 2) for i in range(0, count - 2, 2)]
    onward = onward + [(i, i - 2) for i in range(3, count, 2)]
    return inner, lax.ppermute(inner[size:], "narrow", onward)


def on_device(
    level_rhs,
    galerkin_cols,
    galerkin_blocks,
    restrict_cols,
    restrict_blocks,
    prolong_cols,
    prolong_blocks,
    coarse_inverse,
):
    levels = galerkin_cols.shape[0]
    count = galerkin_cols.shape[2]
    size = galerkin_blocks.shape[-1]
    rows, fields = level_rhs.shape[1:]
    splits = min(2, levels)
    widths = [fields >> min(level_idx, splits) for level_idx in range(levels + 1)]
    gcols, rcols, pcols = ((c, scalars()) for c in (galerkin_cols, restrict_cols, prolong_cols))
    operator_shapes = [
        array((rows, rows), bf16), array((rows, 2 * size), bf16),
        array((rows, 1), f32), array((rows, 2 * rows), bf16),
    ]

    def ends_shape(width):
        return array((2 * size, width), bf16)

    def of_level(value, level_idx):
        return value, level_block(value, level_idx)

    def flops(width, products=1):
        return 2 * products * rows * rows * width

    (ends,) = run(
        start_kernel, "start", [ends_shape(fields)],
        [in_hbm(level_rhs), in_hbm(galerkin_blocks)],
        scratch=[
            pltpu.VMEM((2, size, fields), f32), pltpu.VMEM((2, size, size), bf16),
            pltpu.SemaphoreType.DMA((4,)),
        ],
    )
    inner, outer = swap_ends(ends)
    rest, local, rim, scale, rmat = run(
        first_local_kernel, "first_local", [array((rows, fields), f32)] + operator_shapes,
        [level_rhs, inner, gcols, of_level(galerkin_blocks, 0), rcols, of_level(restrict_blocks, 0)],
        flops=flops(fields),
    )
    operators = [(scale, local)]
    right_sides = [level_rhs]
    for level_idx in range(levels):
        width = widths[level_idx + 1]
        outs = [array((rows, width), bf16)] * (2 if level_idx < splits else 1)
        outs = run(
            functools.partial(residual_kernel, level_idx), "residual", outs, [rest, rim, inner, outer]
        )
        kept = outs[-1]
        other = exchange(outs[0], "wide", 1 << level_idx)
        if level_idx + 1 < levels:
            part, local, rim, scale, next_rmat = run(
                functools.partial(own_part_kernel, level_idx), "own_part",
                [array((rows, width), f32)] + operator_shapes,
                [kept, rmat, gcols, of_level(galerkin_blocks, level_idx + 1),
                 rcols, of_level(restrict_blocks, level_idx + 1)],
                flops=flops(width),
            )
            operators.append((scale, local))
            rhs, smoothed, ends = run(
                functools.partial(join_kernel, level_idx), "join",
                [array((rows, width), f32), array((rows, width), bf16), ends_shape(width)],
                [part, rmat, other, scale],
                flops=flops(width),
            )
            right_sides.append(rhs)
            rmat = next_rmat
            inner, outer = swap_ends(ends)
            (rest,) = run(
                local_kernel, "local", [array((rows, width), f32)], [rhs, local, smoothed],
                flops=flops(width),
            )
        else:
            part, *pmats = run(
                functools.partial(last_part_kernel, level_idx, levels), "last_part",
                [array((rows, width), f32)] + operator_shapes[:1] * levels,
                [kept, rmat, pcols] + [of_level(prolong_blocks, idx) for idx in range(levels)],
                flops=flops(width),
            )
            (mine,) = run(
                functools.partial(last_join_kernel, level_idx), "last_join",
                [array((rows, width), bf16)], [part, rmat, other], flops=flops(width),
            )
    pieces = lax.axis_size("narrow")
    parts = {0: mine}
    order = sorted(range(1, pieces), key=lambda o: (bin(o).count("1"), -o))
    for offset in order:
        low = offset & -offset
        parts[offset] = exchange(parts[offset ^ low], "narrow", low)
    total_shape = [array((rows, width), f32)]
    (total,) = run(
        functools.partial(coarse_kernel, (0,), False), "coarse_own", total_shape,
        [coarse_inverse, mine], flops=flops(width),
    )
    middle = tuple(order[:-1])
    if middle:
        (total,) = run(
            functools.partial(coarse_kernel, middle, True), "coarse_middle", total_shape,
            [coarse_inverse] + [parts[o] for o in middle] + [total], flops=flops(width, len(middle)),
        )

    def raising(level_idx):
        return [right_sides[level_idx], *operators[level_idx], pmats[level_idx]]

    operands = []
    for level_idx in reversed(range(splits, levels)):
        operands += raising(level_idx)
    (coarse,) = run(
        functools.partial(up_kernel, order[-1], levels - splits), "up", [array((rows, width), bf16)],
        [coarse_inverse, parts[order[-1]], total] + operands,
        flops=flops(width, 1 + 2 * (levels - splits)),
    )
    chunks = [(coarse, ())]
    for level_idx in reversed(range(splits)):
        step = widths[level_idx + 1]
        own = [(value, place + ((level_idx, 0, step),)) for value, place in chunks]
        far = [
            (exchange(value, "wide", 1 << level_idx), place + ((level_idx, 1, step),))
            for value, place in chunks
        ]
        if level_idx > 0:
            raised = []
            for value, place in own + far:
                (result,) = run(
                    functools.partial(raise_kernel, (place,), False), "raise",
                    [array((rows, width), bf16)], [value] + raising(level_idx),
                    flops=flops(width, 2),
                )
                raised.append((result, place))
            chunks = raised
        else:
            places = tuple(place for _, place in own + far)
            early = run(
                functools.partial(raise_kernel, places[: len(own)], True), "raise_own",
                [array((rows, width), f32)] * len(own), [value for value, _ in own] + raising(0),
                flops=flops(width, 2 * len(own)),
            )
            (result,) = run(
                functools.partial(final_kernel, places, len(own)), "final",
                [array((1, rows, fields), f32)],
                list(early) + [value for value, _ in far] + raising(0),
                flops=flops(width, 2 * len(far)),
            )
    return result


def solution(mesh):
    in_specs = (
        P("wide", "narrow", None),
        P(None, "wide", "narrow", None),
        P(None, "wide", "narrow", None, None, None),
        P(None, "wide", "narrow", None),
        P(None, "wide", "narrow", None, None, None),
        P(None, "wide", "narrow", None),
        P(None, "wide", "narrow", None, None, None),
        P("narrow", None),
    )
    out_specs = P("wide", "narrow", None)
    return jax.shard_map(
        on_device, mesh=mesh, in_specs=in_specs, out_specs=out_specs, check_vma=False
    )
```

```python
import functools

import jax
import jax.numpy as jnp
from jax import lax
from jax.experimental import pallas as pl
from jax.experimental.pallas import tpu as pltpu
from jax.sharding import PartitionSpec as P

relax_down = 0.7
relax_up = 0.5
f32 = jnp.float32
bf16 = jnp.bfloat16
grant = 12 * 1024 * 1024


def matmul(a, b):
    return jnp.dot(a, b, preferred_element_type=f32)


def array(shape, dtype):
    return jax.ShapeDtypeStruct(shape, dtype)


def whole():
    return pl.BlockSpec(memory_space=pltpu.VMEM)


def level_block(value, level_idx):
    shape = (1,) + value.shape[1:]
    return pl.BlockSpec(shape, lambda i: (level_idx,) + (0,) * (value.ndim - 1))


def scalars():
    return pl.BlockSpec(memory_space=pltpu.SMEM)


def in_hbm(value):
    return pltpu.with_memory_space_constraint(value, pltpu.HBM), pl.BlockSpec(memory_space=pltpu.HBM)


def run(body, name, outs, operands, flops=0, scratch=(), out_space=pltpu.VMEM, aliases=None):
    arrays = [o[0] if isinstance(o, tuple) else o for o in operands]
    specs = [o[1] if isinstance(o, tuple) else whole() for o in operands]
    windows = any(isinstance(o, tuple) and o[1].block_shape is not None for o in operands)
    moved = sum(a.size * a.dtype.itemsize for a in arrays)
    return pl.pallas_call(
        body,
        grid=(1,) if windows else (),
        out_shape=outs,
        in_specs=specs,
        out_specs=[pl.BlockSpec(memory_space=out_space)] * len(outs),
        input_output_aliases=aliases or {},
        scratch_shapes=list(scratch),
        compiler_params=pltpu.CompilerParams(vmem_limit_bytes=grant),
        cost_estimate=pl.CostEstimate(flops=flops, bytes_accessed=moved, transcendentals=0),
        name=name,
    )(*arrays)


def diagonal_of(block):
    size = block.shape[0]
    rows = lax.broadcasted_iota(jnp.int32, (size, size), 0)
    lanes = lax.broadcasted_iota(jnp.int32, (size, size), 1)
    return jnp.sum(jnp.where(rows == lanes, block, 0.0), axis=1, keepdims=True)


def placed(base, others, ids, target):
    total = base
    for block, ident in zip(others, ids):
        term = block * jnp.where(ident == target, 1.0, 0.0).astype(f32)
        total = term if total is None else total + term
    return total


def parity_of():
    return lax.rem(lax.axis_index("narrow"), 2)


def put_ends(first, last, inner_ref, outer_ref):
    even = parity_of() == 0
    inner_ref[...] = jnp.where(even, last, first)
    outer_ref[...] = jnp.where(even, first, last)


def assemble_galerkin(level_idx, cols, blocks, local_ref, rim_ref, scale_ref):
    count, slots, size = blocks.shape[2], blocks.shape[3], blocks.shape[4]
    parity = parity_of()
    piece = lax.axis_index("narrow")
    last = lax.axis_size("narrow") - 1
    inside = jnp.where((piece == 0) | (piece == last), 0.0, 1.0).astype(f32)
    for b in range(count):
        held = [blocks[0, 0, b, s].astype(f32) for s in range(slots)]
        ids = [cols[level_idx, 0, b, s] for s in range(1, slots)]
        rows = pl.ds(b * size, size)
        scale_ref[rows, :] = 1.0 / diagonal_of(held[0])
        line = [placed(held[0] if c == b else None, held[1:], ids, c) for c in range(count)]
        local_ref[rows, :] = jnp.concatenate(line, axis=1).astype(bf16)
        rims = [
            placed(None, held[1:], ids, count + 1 - parity),
            placed(None, held[1:], ids, count + parity) * inside,
        ]
        rim_ref[rows, :] = jnp.concatenate(rims, axis=1).astype(bf16)


def assemble_restrict(level_idx, cols, blocks, out_ref):
    count, slots, size = blocks.shape[2], blocks.shape[3], blocks.shape[4]
    for b in range(count):
        held = [blocks[0, 0, b, s].astype(f32) for s in range(slots)]
        ids = [cols[level_idx, 0, b, s] for s in range(2, slots)]
        fixed = {b: held[0], count + b: held[1]}
        line = [placed(fixed.get(c), held[2:], ids, c) for c in range(2 * count)]
        out_ref[pl.ds(b * size, size), :] = jnp.concatenate(line, axis=1).astype(bf16)


def assemble_prolong(level_idx, cols, blocks, out_ref):
    count, slots, size = blocks.shape[2], blocks.shape[3], blocks.shape[4]
    for b in range(count):
        held = [blocks[0, 0, b, s].astype(f32) for s in range(slots)]
        ids = [cols[level_idx, 0, b, s] for s in range(1, slots)]
        line = [placed(held[0] if c == b else None, held[1:], ids, c) for c in range(count)]
        out_ref[pl.ds(b * size, size), :] = jnp.concatenate(line, axis=1).astype(bf16)


def start_kernel(rhs, blocks, inner_ref, outer_ref, rows, pivots, sems):
    count, size = blocks.shape[2], blocks.shape[4]
    copies = []
    for slot, which in enumerate((0, count - 1)):
        source = rhs.at[0, pl.ds(which * size, size), :]
        copies.append(pltpu.make_async_copy(source, rows.at[slot], sems.at[slot]))
        source = blocks.at[0, 0, which, 0]
        copies.append(pltpu.make_async_copy(source, pivots.at[slot], sems.at[2 + slot]))
    for copy in copies:
        copy.start()
    for copy in copies:
        copy.wait()
    first, last = (
        (rows[slot] * (relax_down / diagonal_of(pivots[slot].astype(f32)))).astype(bf16)
        for slot in range(2)
    )
    put_ends(first, last, inner_ref, outer_ref)


def first_local_kernel(
    rhs, _, cols, blocks, rcols, rsource, rest, local, rim, scale, rmat, rblocks, sem
):
    copy = pltpu.make_async_copy(rsource.at[pl.ds(0, 1)], rblocks, sem)
    copy.start()
    assemble_galerkin(0, cols, blocks, local, rim, scale)
    smoothed = (rhs[0] * (relax_down * scale[...])).astype(bf16)
    rest[...] = rhs[0] - matmul(local[...], smoothed)
    copy.wait()
    assemble_restrict(0, rcols, rblocks, rmat)


def bit_of(level_idx):
    return lax.axis_index("wide") >> level_idx & 1


def residual_kernel(level_idx, rest, rim, inner, outer, *refs):
    if len(refs) == 1:
        rims = jnp.concatenate([inner[...], outer[...]], axis=0)
        refs[0][...] = (rest[...] - matmul(rim[...], rims)).astype(bf16)
    else:
        half = refs[0].shape[1]
        bit = bit_of(level_idx)
        for ref, side in zip(refs, (1 - bit, bit)):
            lanes = pl.ds(pl.multiple_of(side * half, half), half)
            rims = jnp.concatenate([inner[:, lanes], outer[:, lanes]], axis=0)
            ref[...] = (rest[:, lanes] - matmul(rim[...], rims)).astype(bf16)


def side_of(rmat, level_idx, own):
    width = rmat.shape[1] // 2
    bit = bit_of(level_idx)
    side = bit if own else 1 - bit
    return rmat[:, pl.ds(pl.multiple_of(side * width, width), width)]


def own_part_kernel(level_idx, residual, rmat, cols, blocks, rcols, rblocks, *refs):
    part, local, rim, scale, next_rmat = refs
    part[...] = matmul(side_of(rmat, level_idx, True), residual[...])
    assemble_galerkin(level_idx + 1, cols, blocks, local, rim, scale)
    assemble_restrict(level_idx + 1, rcols, rblocks, next_rmat)


def last_part_kernel(level_idx, levels, residual, rmat, pcols, *refs):
    refs[levels][...] = matmul(side_of(rmat, level_idx, True), residual[...])
    for idx, blocks, out in zip(range(levels), refs[:levels], refs[levels + 1 :]):
        assemble_prolong(idx, pcols, blocks, out)


def join_kernel(level_idx, part, rmat, other, scale, rhs, smoothed, inner_ref, outer_ref):
    size = inner_ref.shape[0]
    current = part[...] + matmul(side_of(rmat, level_idx, False), other[...])
    rhs[...] = current
    rounded = (current * (relax_down * scale[...])).astype(bf16)
    smoothed[...] = rounded
    put_ends(rounded[:size], rounded[-size:], inner_ref, outer_ref)


def last_join_kernel(level_idx, part, rmat, other, rounded):
    current = part[...] + matmul(side_of(rmat, level_idx, False), other[...])
    rounded[...] = current.astype(bf16)


def local_kernel(rhs, local, smoothed, rest):
    rest[...] = rhs[...] - matmul(local[...], smoothed[...])


def inverse_part(inverse, part, offset):
    depth = part.shape[0]
    piece = lax.axis_index("narrow") ^ offset
    return matmul(inverse[:, pl.ds(pl.multiple_of(piece * depth, depth), depth)], part[...])


def coarse_kernel(offsets, with_total, *refs):
    inverse, parts, refs = refs[0], refs[1 : 1 + len(offsets)], refs[1 + len(offsets) :]
    total = refs[0][...] if with_total else None
    for part, offset in zip(parts, offsets):
        term = inverse_part(inverse, part, offset)
        total = term if total is None else total + term
    refs[-1][...] = total


def raise_level(coarse, rhs, scale, local, pmat):
    updated = rhs * (relax_down * scale) + matmul(pmat, coarse)
    applied = matmul(local, updated.astype(bf16))
    return updated + (relax_up * scale) * (rhs - applied)


def up_kernel(offset, depth, inverse, part, total, *refs):
    value = total[...] + inverse_part(inverse, part, offset)
    for step in range(depth):
        rhs, scale, local, pmat = refs[4 * step : 4 * step + 4]
        value = raise_level(value.astype(bf16), rhs[...], scale[...], local[...], pmat[...])
    refs[-1][...] = value.astype(bf16)


def lanes_of(place, width):
    start = 0
    for level_idx, flip, step in place:
        start = start + (bit_of(level_idx) ^ flip) * step
    return pl.ds(pl.multiple_of(start, width), width)


def raise_kernel(place, coarse, rhs, scale, local, pmat, out):
    lanes = lanes_of(place, coarse.shape[1])
    raised = raise_level(coarse[...], rhs[:, lanes], scale[...], local[...], pmat[...])
    out[...] = raised.astype(bf16)


def last_raise_kernel(places, *refs):
    coarse, refs = refs[: len(places)], refs[len(places) :]
    rhs, scale, local, pmat = refs[:4]
    out, sems = refs[-2 - len(places)], refs[-1]
    copies = []
    for slot, (place, value, made) in enumerate(zip(places, coarse, refs[-1 - len(places) : -1])):
        lanes = lanes_of(place, value.shape[1])
        made[...] = raise_level(value[...], rhs[0, :, lanes], scale[...], local[...], pmat[...])
        copy = pltpu.make_async_copy(made, out.at[0, :, lanes], sems.at[slot])
        copy.start()
        copies.append(copy)
    for copy in copies:
        copy.wait()


def exchange(value, axis, bit):
    count = lax.axis_size(axis)
    return lax.ppermute(value, axis, [(i, i ^ bit) for i in range(count)])


def swap_ends(inner, outer):
    count = lax.axis_size("narrow")
    gaps = [(i, (i + 1 if i % 2 else i - 1) % count) for i in range(count)]
    return exchange(inner, "narrow", 1), lax.ppermute(outer, "narrow", gaps)


def on_device(
    level_rhs,
    galerkin_cols,
    galerkin_blocks,
    restrict_cols,
    restrict_blocks,
    prolong_cols,
    prolong_blocks,
    coarse_inverse,
):
    levels = galerkin_cols.shape[0]
    count = galerkin_cols.shape[2]
    size = galerkin_blocks.shape[-1]
    rows, fields = level_rhs.shape[1:]
    splits = min(1, levels)
    widths = [fields >> min(level_idx, splits) for level_idx in range(levels + 1)]
    gcols, rcols, pcols = ((c, scalars()) for c in (galerkin_cols, restrict_cols, prolong_cols))
    operator_shapes = [
        array((rows, rows), bf16), array((rows, 2 * size), bf16),
        array((rows, 1), f32), array((rows, 2 * rows), bf16),
    ]

    def ends_shape(width):
        return array((size, width), bf16)

    def of_level(value, level_idx):
        return value, level_block(value, level_idx)

    def flops(width, products=1):
        return 2 * products * rows * rows * width

    ends = run(
        start_kernel, "start", [ends_shape(fields)] * 2,
        [in_hbm(level_rhs), in_hbm(galerkin_blocks)],
        scratch=[
            pltpu.VMEM((2, size, fields), f32), pltpu.VMEM((2, size, size), bf16),
            pltpu.SemaphoreType.DMA((4,)),
        ],
    )
    inner, outer = swap_ends(*ends)
    rest, local, rim, scale, rmat = run(
        first_local_kernel, "first_local", [array((rows, fields), f32)] + operator_shapes,
        [level_rhs, ends[0], gcols, of_level(galerkin_blocks, 0), rcols, in_hbm(restrict_blocks)],
        flops=flops(fields),
        scratch=[pltpu.VMEM((1,) + restrict_blocks.shape[1:], bf16), pltpu.SemaphoreType.DMA],
    )
    operators = [(scale, local)]
    right_sides = [level_rhs]
    for level_idx in range(levels):
        width = widths[level_idx + 1]
        outs = [array((rows, width), bf16)] * (2 if level_idx < splits else 1)
        outs = run(
            functools.partial(residual_kernel, level_idx), "residual", outs, [rest, rim, inner, outer]
        )
        kept = outs[-1]
        other = exchange(outs[0], "wide", 1 << level_idx)
        if level_idx + 1 < levels:
            part, local, rim, scale, next_rmat = run(
                functools.partial(own_part_kernel, level_idx), "own_part",
                [array((rows, width), f32)] + operator_shapes,
                [kept, rmat, gcols, of_level(galerkin_blocks, level_idx + 1),
                 rcols, of_level(restrict_blocks, level_idx + 1)],
                flops=flops(width),
            )
            operators.append((scale, local))
            rhs, smoothed, *ends = run(
                functools.partial(join_kernel, level_idx), "join",
                [array((rows, width), f32), array((rows, width), bf16)] + [ends_shape(width)] * 2,
                [part, rmat, other, scale],
                flops=flops(width),
            )
            right_sides.append(rhs)
            rmat = next_rmat
            inner, outer = swap_ends(*ends)
            (rest,) = run(
                local_kernel, "local", [array((rows, width), f32)], [rhs, local, smoothed],
                flops=flops(width),
            )
        else:
            part, *pmats = run(
                functools.partial(last_part_kernel, level_idx, levels), "last_part",
                [array((rows, width), f32)] + operator_shapes[:1] * levels,
                [kept, rmat, pcols] + [of_level(prolong_blocks, idx) for idx in range(levels)],
                flops=flops(width),
            )
            (mine,) = run(
                functools.partial(last_join_kernel, level_idx), "last_join",
                [array((rows, width), bf16)], [part, rmat, other], flops=flops(width),
            )
    pieces = lax.axis_size("narrow")
    parts = {0: mine}
    order = sorted(range(1, pieces), key=lambda o: (bin(o).count("1"), -o))
    for offset in order:
        low = offset & -offset
        parts[offset] = exchange(parts[offset ^ low], "narrow", low)
    total_shape = [array((rows, width), f32)]
    (total,) = run(
        functools.partial(coarse_kernel, (0,), False), "coarse_own", total_shape,
        [coarse_inverse, mine], flops=flops(width),
    )
    middle = tuple(order[:-1])
    if middle:
        (total,) = run(
            functools.partial(coarse_kernel, middle, True), "coarse_middle", total_shape,
            [coarse_inverse] + [parts[o] for o in middle] + [total], flops=flops(width, len(middle)),
        )

    def raising(level_idx):
        return [right_sides[level_idx], *operators[level_idx], pmats[level_idx]]

    operands = []
    for level_idx in reversed(range(splits, levels)):
        operands += raising(level_idx)
    (coarse,) = run(
        functools.partial(up_kernel, order[-1], levels - splits), "up", [array((rows, width), bf16)],
        [coarse_inverse, parts[order[-1]], total] + operands,
        flops=flops(width, 1 + 2 * (levels - splits)),
    )
    chunks = [(coarse, ())]
    for level_idx in reversed(range(splits)):
        step = widths[level_idx + 1]
        own = [(value, place + ((level_idx, 0, step),)) for value, place in chunks]
        far = [
            (exchange(value, "wide", 1 << level_idx), place + ((level_idx, 1, step),))
            for value, place in chunks
        ]
        if level_idx > 0:
            raised = []
            for value, place in own + far:
                (result,) = run(
                    functools.partial(raise_kernel, place), "raise",
                    [array((rows, width), bf16)], [value] + raising(level_idx),
                    flops=flops(width, 2),
                )
                raised.append((result, place))
            chunks = raised
        else:
            result = None
            for group in (own, far):
                operands = [value for value, _ in group] + raising(0)
                aliases = {}
                if result is not None:
                    aliases[len(operands)] = 0
                    operands.append(in_hbm(result))
                (result,) = run(
                    functools.partial(last_raise_kernel, tuple(place for _, place in group)),
                    "last_raise", [array((1, rows, fields), f32)], operands,
                    flops=flops(width, 2 * len(group)),
                    scratch=[pltpu.VMEM((rows, width), f32)] * len(group)
                    + [pltpu.SemaphoreType.DMA((len(group),))],
                    out_space=pltpu.HBM, aliases=aliases,
                )
    return result


def solution(mesh):
    in_specs = (
        P("wide", "narrow", None),
        P(None, "wide", "narrow", None),
        P(None, "wide", "narrow", None, None, None),
        P(None, "wide", "narrow", None),
        P(None, "wide", "narrow", None, None, None),
        P(None, "wide", "narrow", None),
        P(None, "wide", "narrow", None, None, None),
        P("narrow", None),
    )
    out_specs = P("wide", "narrow", None)
    return jax.shard_map(
        on_device, mesh=mesh, in_specs=in_specs, out_specs=out_specs, check_vma=False
    )
```

```python
import functools

import jax
import jax.numpy as jnp
from jax import lax
from jax.experimental import pallas as pl
from jax.experimental.pallas import tpu as pltpu
from jax.sharding import PartitionSpec as P

relax_down = 0.7
relax_up = 0.5
f32 = jnp.float32
bf16 = jnp.bfloat16
grant = 12 * 1024 * 1024
chunk_width = 128


def matmul(a, b):
    return jnp.dot(a, b, preferred_element_type=f32)


def array(shape, dtype):
    return jax.ShapeDtypeStruct(shape, dtype)


def whole():
    return pl.BlockSpec(memory_space=pltpu.VMEM)


def level_block(value, level_idx):
    shape = (1,) + value.shape[1:]
    return pl.BlockSpec(shape, lambda i: (level_idx,) + (0,) * (value.ndim - 1))


def scalars():
    return pl.BlockSpec(memory_space=pltpu.SMEM)


def in_hbm(value):
    return pltpu.with_memory_space_constraint(value, pltpu.HBM), pl.BlockSpec(memory_space=pltpu.HBM)


def run(body, name, outs, operands, flops=0, scratch=(), out_space=pltpu.VMEM, aliases=None):
    arrays = [o[0] if isinstance(o, tuple) else o for o in operands]
    specs = [o[1] if isinstance(o, tuple) else whole() for o in operands]
    windows = any(isinstance(o, tuple) and o[1].block_shape is not None for o in operands)
    moved = sum(a.size * a.dtype.itemsize for a in arrays)
    return pl.pallas_call(
        body,
        grid=(1,) if windows else (),
        out_shape=outs,
        in_specs=specs,
        out_specs=[pl.BlockSpec(memory_space=out_space)] * len(outs),
        input_output_aliases=aliases or {},
        scratch_shapes=list(scratch),
        compiler_params=pltpu.CompilerParams(vmem_limit_bytes=grant),
        cost_estimate=pl.CostEstimate(flops=flops, bytes_accessed=moved, transcendentals=0),
        name=name,
    )(*arrays)


def diagonal_of(block):
    size = block.shape[0]
    rows = lax.broadcasted_iota(jnp.int32, (size, size), 0)
    lanes = lax.broadcasted_iota(jnp.int32, (size, size), 1)
    return jnp.sum(jnp.where(rows == lanes, block, 0.0), axis=1, keepdims=True)


def placed(base, others, ids, target):
    total = base
    for block, ident in zip(others, ids):
        term = block * jnp.where(ident == target, 1.0, 0.0).astype(f32)
        total = term if total is None else total + term
    return total


def parity_of():
    return lax.rem(lax.axis_index("narrow"), 2)


def put_ends(first, last, inner_ref, outer_ref):
    even = parity_of() == 0
    inner_ref[...] = jnp.where(even, last, first)
    outer_ref[...] = jnp.where(even, first, last)


def assemble_galerkin(level_idx, cols, blocks, local_ref, rim_ref, scale_ref):
    count, slots, size = blocks.shape[2], blocks.shape[3], blocks.shape[4]
    parity = parity_of()
    piece = lax.axis_index("narrow")
    last = lax.axis_size("narrow") - 1
    inside = jnp.where((piece == 0) | (piece == last), 0.0, 1.0).astype(f32)
    for b in range(count):
        held = [blocks[0, 0, b, s].astype(f32) for s in range(slots)]
        ids = [cols[level_idx, 0, b, s] for s in range(1, slots)]
        rows = pl.ds(b * size, size)
        scale_ref[rows, :] = 1.0 / diagonal_of(held[0])
        line = [placed(held[0] if c == b else None, held[1:], ids, c) for c in range(count)]
        local_ref[rows, :] = jnp.concatenate(line, axis=1).astype(bf16)
        rims = [
            placed(None, held[1:], ids, count + 1 - parity),
            placed(None, held[1:], ids, count + parity) * inside,
        ]
        rim_ref[rows, :] = jnp.concatenate(rims, axis=1).astype(bf16)


def assemble_restrict(level_idx, cols, blocks, out_ref):
    count, slots, size = blocks.shape[2], blocks.shape[3], blocks.shape[4]
    for b in range(count):
        held = [blocks[0, 0, b, s].astype(f32) for s in range(slots)]
        ids = [cols[level_idx, 0, b, s] for s in range(2, slots)]
        fixed = {b: held[0], count + b: held[1]}
        line = [placed(fixed.get(c), held[2:], ids, c) for c in range(2 * count)]
        out_ref[pl.ds(b * size, size), :] = jnp.concatenate(line, axis=1).astype(bf16)


def assemble_prolong(level_idx, cols, blocks, out_ref):
    count, slots, size = blocks.shape[2], blocks.shape[3], blocks.shape[4]
    for b in range(count):
        held = [blocks[0, 0, b, s].astype(f32) for s in range(slots)]
        ids = [cols[level_idx, 0, b, s] for s in range(1, slots)]
        line = [placed(held[0] if c == b else None, held[1:], ids, c) for c in range(count)]
        out_ref[pl.ds(b * size, size), :] = jnp.concatenate(line, axis=1).astype(bf16)


def start_kernel(rhs, blocks, inner_ref, outer_ref, rows, pivots, sems):
    count, size = blocks.shape[2], blocks.shape[4]
    copies = []
    for slot, which in enumerate((0, count - 1)):
        source = rhs.at[0, pl.ds(which * size, size), :]
        copies.append(pltpu.make_async_copy(source, rows.at[slot], sems.at[slot]))
        source = blocks.at[0, 0, which, 0]
        copies.append(pltpu.make_async_copy(source, pivots.at[slot], sems.at[2 + slot]))
    for copy in copies:
        copy.start()
    for copy in copies:
        copy.wait()
    first, last = (
        (rows[slot] * (relax_down / diagonal_of(pivots[slot].astype(f32)))).astype(bf16)
        for slot in range(2)
    )
    put_ends(first, last, inner_ref, outer_ref)


def first_local_kernel(rhs, _, cols, blocks, rest, local, rim, scale):
    assemble_galerkin(0, cols, blocks, local, rim, scale)
    smoothed = (rhs[0] * (relax_down * scale[...])).astype(bf16)
    rest[...] = rhs[0] - matmul(local[...], smoothed)


def bit_of(level_idx):
    return lax.axis_index("wide") >> level_idx & 1


def lanes_of(place, width):
    start = 0
    for level_idx, flip, step in place:
        start = start + (bit_of(level_idx) ^ flip if level_idx >= 0 else flip) * step
    return pl.ds(pl.multiple_of(start, width), width)


def first_residual_kernel(places, rest, rim, inner, outer, *refs):
    for ref, place in zip(refs, places):
        lanes = lanes_of(place, ref.shape[1])
        rims = jnp.concatenate([inner[:, lanes], outer[:, lanes]], axis=0)
        ref[...] = (rest[:, lanes] - matmul(rim[...], rims)).astype(bf16)


def residual_kernel(rhs, local, smoothed, rim, inner, outer, out):
    rims = jnp.concatenate([inner[...], outer[...]], axis=0)
    applied = matmul(local[...], smoothed[...]) + matmul(rim[...], rims)
    out[...] = (rhs[...] - applied).astype(bf16)


def operators_kernel(level_idx, _, rcols, rblocks, cols, blocks, rmat, local, rim, scale):
    assemble_restrict(level_idx, rcols, rblocks, rmat)
    assemble_galerkin(level_idx + 1, cols, blocks, local, rim, scale)


def last_operators_kernel(level_idx, levels, _, rcols, rblocks, pcols, *refs):
    assemble_restrict(level_idx, rcols, rblocks, refs[levels])
    for idx, blocks, out in zip(range(levels), refs[:levels], refs[levels + 1 :]):
        assemble_prolong(idx, pcols, blocks, out)


def restricted(level_idx, rmat, kept, other):
    width = rmat.shape[1] // 2
    own = pl.multiple_of(bit_of(level_idx) * width, width)
    far = pl.multiple_of((1 - bit_of(level_idx)) * width, width)
    total = matmul(rmat[:, pl.ds(own, width)], kept[...])
    return total + matmul(rmat[:, pl.ds(far, width)], other[...])


def join_kernel(level_idx, rmat, kept, other, scale, rhs, smoothed, inner_ref, outer_ref):
    size = inner_ref.shape[0]
    current = restricted(level_idx, rmat, kept, other)
    rhs[...] = current
    rounded = (current * (relax_down * scale[...])).astype(bf16)
    smoothed[...] = rounded
    put_ends(rounded[:size], rounded[-size:], inner_ref, outer_ref)


def last_join_kernel(level_idx, rmat, kept, other, rounded):
    rounded[...] = restricted(level_idx, rmat, kept, other).astype(bf16)


def inverse_part(inverse, part, offset):
    depth = part.shape[0]
    piece = lax.axis_index("narrow") ^ offset
    return matmul(inverse[:, pl.ds(pl.multiple_of(piece * depth, depth), depth)], part[...])


def raise_level(coarse, rhs, scale, local, pmat):
    updated = rhs * (relax_down * scale) + matmul(pmat, coarse)
    applied = matmul(local, updated.astype(bf16))
    return updated + (relax_up * scale) * (rhs - applied)


def up_kernel(offsets, depth, inverse, *refs):
    value = None
    for part, offset in zip(refs, offsets):
        term = inverse_part(inverse, part, offset)
        value = term if value is None else value + term
    refs = refs[len(offsets) :]
    for step in range(depth):
        rhs, scale, local, pmat = refs[4 * step : 4 * step + 4]
        value = raise_level(value.astype(bf16), rhs[...], scale[...], local[...], pmat[...])
    refs[-1][...] = value.astype(bf16)


def last_raise_kernel(places, *refs):
    coarse, refs = refs[: len(places)], refs[len(places) :]
    rhs, scale, local, pmat = refs[:4]
    out, sems = refs[-2 - len(places)], refs[-1]
    copies = []
    for slot, (place, value, made) in enumerate(zip(places, coarse, refs[-1 - len(places) : -1])):
        lanes = lanes_of(place, value.shape[1])
        made[...] = raise_level(value[...], rhs[0, :, lanes], scale[...], local[...], pmat[...])
        copy = pltpu.make_async_copy(made, out.at[0, :, lanes], sems.at[slot])
        copy.start()
        copies.append(copy)
    for copy in copies:
        copy.wait()


def exchange(value, axis, bit):
    count = lax.axis_size(axis)
    return lax.ppermute(value, axis, [(i, i ^ bit) for i in range(count)])


def swap_ends(inner, outer):
    count = lax.axis_size("narrow")
    gaps = [(i, (i + 1 if i % 2 else i - 1) % count) for i in range(count)]
    outer = lax.ppermute(outer, "narrow", gaps)
    return exchange(inner, "narrow", 1), outer


def on_device(
    level_rhs,
    galerkin_cols,
    galerkin_blocks,
    restrict_cols,
    restrict_blocks,
    prolong_cols,
    prolong_blocks,
    coarse_inverse,
):
    levels = galerkin_cols.shape[0]
    count = galerkin_cols.shape[2]
    size = galerkin_blocks.shape[-1]
    rows, fields = level_rhs.shape[1:]
    half = fields // 2
    chunks = range(half // chunk_width)
    width = half // len(chunks)
    gcols, rcols, pcols = ((c, scalars()) for c in (galerkin_cols, restrict_cols, prolong_cols))
    operator_shapes = [
        array((rows, rows), bf16), array((rows, 2 * size), bf16), array((rows, 1), f32)
    ]
    rmat_shape = array((rows, 2 * rows), bf16)
    chunk_shape = array((rows, width), bf16)

    def ends_shape(columns):
        return array((size, columns), bf16)

    def of_level(value, level_idx):
        return value, level_block(value, level_idx)

    def flops(columns, products=1):
        return 2 * products * rows * rows * columns

    def place_of(chunk, flip):
        return (0, flip, half), (-1, chunk, width)

    ends = run(
        start_kernel, "start", [ends_shape(fields)] * 2,
        [in_hbm(level_rhs), in_hbm(galerkin_blocks)],
        scratch=[
            pltpu.VMEM((2, size, fields), f32), pltpu.VMEM((2, size, size), bf16),
            pltpu.SemaphoreType.DMA((4,)),
        ],
    )
    inner, outer = swap_ends(*ends)
    rest, local, rim, scale = run(
        first_local_kernel, "first_local", [array((rows, fields), f32)] + operator_shapes,
        [level_rhs, ends[0], gcols, of_level(galerkin_blocks, 0)], flops=flops(fields),
    )
    operators = [(scale, local)]
    sent, kept = [], []
    for chunk in chunks:
        places = place_of(chunk, 1), place_of(chunk, 0)
        far, near = run(
            functools.partial(first_residual_kernel, places), "first_residual", [chunk_shape] * 2,
            [rest, rim, inner, outer],
        )
        sent.append(far)
        kept.append(near)
    right_sides = [level_rhs]
    for level_idx in range(levels):
        other = [exchange(value, "wide", 1 << level_idx) for value in sent]
        if level_idx + 1 < levels:
            rmat, local, rim, scale = run(
                functools.partial(operators_kernel, level_idx), "operators",
                [rmat_shape] + operator_shapes,
                [kept[0], rcols, of_level(restrict_blocks, level_idx),
                 gcols, of_level(galerkin_blocks, level_idx + 1)],
            )
            operators.append((scale, local))
            sent = []
            sides = []
            for chunk in chunks:
                rhs, smoothed, *ends = run(
                    functools.partial(join_kernel, level_idx), "join",
                    [array((rows, width), f32), chunk_shape] + [ends_shape(width)] * 2,
                    [rmat, kept[chunk], other[chunk], scale], flops=flops(width, 2),
                )
                inner, outer = swap_ends(*ends)
                (value,) = run(
                    residual_kernel, "residual", [chunk_shape],
                    [rhs, local, smoothed, rim, inner, outer], flops=flops(width, 2),
                )
                sides.append(rhs)
                sent.append(value)
            kept = sent
            right_sides.append(sides)
        else:
            rmat, *pmats = run(
                functools.partial(last_operators_kernel, level_idx, levels), "last_operators",
                [rmat_shape] + operator_shapes[:1] * levels,
                [kept[0], rcols, of_level(restrict_blocks, level_idx), pcols]
                + [of_level(prolong_blocks, idx) for idx in range(levels)],
            )
            mine = [
                run(
                    functools.partial(last_join_kernel, level_idx), "last_join", [chunk_shape],
                    [rmat, kept[chunk], other[chunk]], flops=flops(width, 2),
                )[0]
                for chunk in chunks
            ]
    pieces = lax.axis_size("narrow")
    order = sorted(range(1, pieces), key=lambda o: (bin(o).count("1"), -o))
    own, far = [], []
    for chunk in chunks:
        parts = {0: mine[chunk]}
        for offset in order:
            low = offset & -offset
            parts[offset] = exchange(parts[offset ^ low], "narrow", low)
        offsets = tuple(parts)
        operands = [coarse_inverse] + [parts[o] for o in offsets]
        for level_idx in reversed(range(1, levels)):
            operands += [right_sides[level_idx][chunk], *operators[level_idx], pmats[level_idx]]
        (coarse,) = run(
            functools.partial(up_kernel, offsets, levels - 1), "up", [chunk_shape], operands,
            flops=flops(width, len(offsets) + 2 * (levels - 1)),
        )
        own.append((coarse, place_of(chunk, 0)))
        far.append((exchange(coarse, "wide", 1), place_of(chunk, 1)))
    result = None
    for group in [own] + [[value] for value in far]:
        operands = [value for value, _ in group] + [level_rhs, *operators[0], pmats[0]]
        aliases = {}
        if result is not None:
            aliases[len(operands)] = 0
            operands.append(in_hbm(result))
        (result,) = run(
            functools.partial(last_raise_kernel, tuple(place for _, place in group)),
            "last_raise", [array((1, rows, fields), f32)], operands,
            flops=flops(width, 2 * len(group)),
            scratch=[pltpu.VMEM((rows, width), f32)] * len(group)
            + [pltpu.SemaphoreType.DMA((len(group),))],
            out_space=pltpu.HBM, aliases=aliases,
        )
    return result


def solution(mesh):
    in_specs = (
        P("wide", "narrow", None),
        P(None, "wide", "narrow", None),
        P(None, "wide", "narrow", None, None, None),
        P(None, "wide", "narrow", None),
        P(None, "wide", "narrow", None, None, None),
        P(None, "wide", "narrow", None),
        P(None, "wide", "narrow", None, None, None),
        P("narrow", None),
    )
    out_specs = P("wide", "narrow", None)
    return jax.shard_map(
        on_device, mesh=mesh, in_specs=in_specs, out_specs=out_specs, check_vma=False
    )
```

```python
import functools

import jax
import jax.numpy as jnp
from jax import lax
from jax.experimental import pallas as pl
from jax.experimental.pallas import tpu as pltpu
from jax.sharding import PartitionSpec as P

relax_down = 0.7
relax_up = 0.5
f32 = jnp.float32
bf16 = jnp.bfloat16
grant = 12 * 1024 * 1024


def matmul(a, b):
    return jnp.dot(a, b, preferred_element_type=f32)


def array(shape, dtype):
    return jax.ShapeDtypeStruct(shape, dtype)


def whole():
    return pl.BlockSpec(memory_space=pltpu.VMEM)


def level_block(value, level_idx):
    shape = (1,) + value.shape[1:]
    return pl.BlockSpec(shape, lambda i: (level_idx,) + (0,) * (value.ndim - 1))


def scalars():
    return pl.BlockSpec(memory_space=pltpu.SMEM)


def in_hbm(value):
    return pltpu.with_memory_space_constraint(value, pltpu.HBM), pl.BlockSpec(memory_space=pltpu.HBM)


def run(body, name, outs, operands, flops=0, scratch=(), out_space=pltpu.VMEM, aliases=None):
    arrays = [o[0] if isinstance(o, tuple) else o for o in operands]
    specs = [o[1] if isinstance(o, tuple) else whole() for o in operands]
    windows = any(isinstance(o, tuple) and o[1].block_shape is not None for o in operands)
    moved = sum(a.size * a.dtype.itemsize for a in arrays)
    return pl.pallas_call(
        body,
        grid=(1,) if windows else (),
        out_shape=outs,
        in_specs=specs,
        out_specs=[pl.BlockSpec(memory_space=out_space)] * len(outs),
        input_output_aliases=aliases or {},
        scratch_shapes=list(scratch),
        compiler_params=pltpu.CompilerParams(vmem_limit_bytes=grant),
        cost_estimate=pl.CostEstimate(flops=flops, bytes_accessed=moved, transcendentals=0),
        name=name,
    )(*arrays)


def diagonal_of(block):
    size = block.shape[0]
    rows = lax.broadcasted_iota(jnp.int32, (size, size), 0)
    lanes = lax.broadcasted_iota(jnp.int32, (size, size), 1)
    return jnp.sum(jnp.where(rows == lanes, block, 0.0), axis=1, keepdims=True)


def placed(base, others, ids, target):
    total = base
    for block, ident in zip(others, ids):
        term = block * jnp.where(ident == target, 1.0, 0.0).astype(f32)
        total = term if total is None else total + term
    return total


def parity_of():
    return lax.rem(lax.axis_index("narrow"), 2)


def put_ends(first, last, inner_ref, outer_ref):
    even = parity_of() == 0
    inner_ref[...] = jnp.where(even, last, first)
    outer_ref[...] = jnp.where(even, first, last)


def assemble_galerkin(level_idx, cols, blocks, local_ref, rim_ref, scale_ref):
    count, slots, size = blocks.shape[2], blocks.shape[3], blocks.shape[4]
    parity = parity_of()
    piece = lax.axis_index("narrow")
    last = lax.axis_size("narrow") - 1
    inside = jnp.where((piece == 0) | (piece == last), 0.0, 1.0).astype(f32)
    for b in range(count):
        held = [blocks[0, 0, b, s].astype(f32) for s in range(slots)]
        ids = [cols[level_idx, 0, b, s] for s in range(1, slots)]
        rows = pl.ds(b * size, size)
        scale_ref[rows, :] = 1.0 / diagonal_of(held[0])
        line = [placed(held[0] if c == b else None, held[1:], ids, c) for c in range(count)]
        local_ref[rows, :] = jnp.concatenate(line, axis=1).astype(bf16)
        rims = [
            placed(None, held[1:], ids, count + 1 - parity),
            placed(None, held[1:], ids, count + parity) * inside,
        ]
        rim_ref[rows, :] = jnp.concatenate(rims, axis=1).astype(bf16)


def assemble_restrict(level_idx, cols, blocks, out_ref):
    count, slots, size = blocks.shape[2], blocks.shape[3], blocks.shape[4]
    for b in range(count):
        held = [blocks[0, 0, b, s].astype(f32) for s in range(slots)]
        ids = [cols[level_idx, 0, b, s] for s in range(2, slots)]
        fixed = {b: held[0], count + b: held[1]}
        line = [placed(fixed.get(c), held[2:], ids, c) for c in range(2 * count)]
        out_ref[pl.ds(b * size, size), :] = jnp.concatenate(line, axis=1).astype(bf16)


def assemble_prolong(level_idx, cols, blocks, out_ref):
    count, slots, size = blocks.shape[2], blocks.shape[3], blocks.shape[4]
    for b in range(count):
        held = [blocks[0, 0, b, s].astype(f32) for s in range(slots)]
        ids = [cols[level_idx, 0, b, s] for s in range(1, slots)]
        line = [placed(held[0] if c == b else None, held[1:], ids, c) for c in range(count)]
        out_ref[pl.ds(b * size, size), :] = jnp.concatenate(line, axis=1).astype(bf16)


def start_kernel(rhs, blocks, inner_ref, outer_ref, rows, pivots, sems):
    count, size = blocks.shape[2], blocks.shape[4]
    copies = []
    for slot, which in enumerate((0, count - 1)):
        source = rhs.at[0, pl.ds(which * size, size), :]
        copies.append(pltpu.make_async_copy(source, rows.at[slot], sems.at[slot]))
        source = blocks.at[0, 0, which, 0]
        copies.append(pltpu.make_async_copy(source, pivots.at[slot], sems.at[2 + slot]))
    for copy in copies:
        copy.start()
    for copy in copies:
        copy.wait()
    first, last = (
        (rows[slot] * (relax_down / diagonal_of(pivots[slot].astype(f32)))).astype(bf16)
        for slot in range(2)
    )
    put_ends(first, last, inner_ref, outer_ref)


def first_local_kernel(rhs, _, cols, blocks, rest, base, local, rim, scale):
    assemble_galerkin(0, cols, blocks, local, rim, scale)
    smoothed = rhs[0] * (relax_down * scale[...])
    left = rhs[0] - matmul(local[...], smoothed.astype(bf16))
    rest[...] = left
    base[...] = smoothed + (relax_up * scale[...]) * left


def bit_of(level_idx):
    return lax.axis_index("wide") >> level_idx & 1


def lanes_of(place, width):
    start = 0
    for level_idx, flip, step in place:
        start = start + (bit_of(level_idx) ^ flip) * step
    return pl.ds(pl.multiple_of(start, width), width)


def first_residual_kernel(places, rest, rim, outer, inner, *refs):
    for ref, place in zip(refs, places):
        lanes = lanes_of(place, ref.shape[1])
        rims = jnp.concatenate([inner[:, lanes], outer[:, lanes]], axis=0)
        ref[...] = (rest[:, lanes] - matmul(rim[...], rims)).astype(bf16)


def residual_kernel(rhs, smoothed, scale, local, rim, outer, inner, _, out, base):
    rims = jnp.concatenate([inner[...], outer[...]], axis=0)
    left = rhs[...] - matmul(local[...], smoothed[...])
    out[...] = (left - matmul(rim[...], rims)).astype(bf16)
    made = rhs[...] * (relax_down * scale[...]) + (relax_up * scale[...]) * left
    base[...] = made.astype(base.dtype)


def operators_kernel(level_idx, _, rcols, rblocks, cols, blocks, rmat, local, rim, scale):
    assemble_restrict(level_idx, rcols, rblocks, rmat)
    assemble_galerkin(level_idx + 1, cols, blocks, local, rim, scale)


def raising(level_idx, pcols, blocks, local, scale, held):
    assemble_prolong(level_idx, pcols, blocks, held)
    applied = matmul(local[...], held[...])
    return (held[...].astype(f32) - (relax_up * scale[...]) * applied).astype(bf16)


def coarse_operators_kernel(level_idx, first, levels, *refs):
    _, rcols, rblocks, pcols, inverse, one, two, *refs = refs
    places = range(first, levels)
    blocks, refs = refs[: len(places)], refs[len(places) :]
    pairs, refs = refs[: 2 * len(places)], refs[2 * len(places) :]
    rmat, coarse, bases, *up, held = refs
    width = one.shape[1]
    bases[:, :width] = one[...]
    bases[:, width:] = two[...]
    assemble_restrict(level_idx, rcols, rblocks, rmat)
    for idx in places:
        slot = idx - first
        made = raising(idx, pcols, blocks[slot], pairs[2 * slot + 1], pairs[2 * slot], held)
        if idx == levels - 1:
            coarse[...] = matmul(made, inverse[...]).astype(bf16)
        else:
            up[slot][...] = made


def fine_operators_kernel(
    places, _, pcols, blocks_0, blocks_1, scale_0, local_0, scale_1, local_1,
    base, near, far, both, total, held,
):
    lower = raising(0, pcols, blocks_0, local_0, scale_0, held)
    upper = raising(1, pcols, blocks_1, local_1, scale_1, held)
    both[...] = matmul(lower, upper).astype(bf16)
    width = near.shape[1] // 2
    for slot, place in enumerate(places):
        source = near if slot < 2 else far
        lanes = lanes_of(place, width)
        columns = pl.ds(slot % 2 * width, width)
        total[:, lanes] = base[:, lanes] + matmul(lower, source[:, columns])


def restricted(level_idx, rmat, kept, other):
    width = rmat.shape[1] // 2
    own = pl.multiple_of(bit_of(level_idx) * width, width)
    far = pl.multiple_of((1 - bit_of(level_idx)) * width, width)
    total = matmul(rmat[:, pl.ds(own, width)], kept[...])
    return total + matmul(rmat[:, pl.ds(far, width)], other[...])


def join_kernel(level_idx, rmat, kept, other, scale, rhs, smoothed, inner_ref, outer_ref):
    size = inner_ref.shape[0]
    current = restricted(level_idx, rmat, kept, other)
    rhs[...] = current
    rounded = (current * (relax_down * scale[...])).astype(bf16)
    smoothed[...] = rounded
    put_ends(rounded[:size], rounded[-size:], inner_ref, outer_ref)


def last_join_kernel(level_idx, rmat, kept, other, rounded):
    rounded[...] = restricted(level_idx, rmat, kept, other).astype(bf16)


def inverse_part(inverse, part, offset):
    depth = part.shape[0]
    piece = lax.axis_index("narrow") ^ offset
    return matmul(inverse[:, pl.ds(pl.multiple_of(piece * depth, depth), depth)], part[...])


def up_kernel(offsets, inverse, *refs):
    parts, refs = refs[: len(offsets)], refs[len(offsets) :]
    value = refs[0][...]
    for part, offset in zip(parts, offsets):
        value = value + inverse_part(inverse, part, offset)
    for step in range((len(refs) - 2) // 2):
        base, up = refs[1 + 2 * step : 3 + 2 * step]
        value = base[...] + matmul(up[...], value.astype(bf16))
    refs[-1][...] = value.astype(bf16)


def output_kernel(places, *refs):
    coarse, refs = refs[: len(places)], refs[len(places) :]
    total, both = refs[:2]
    out, sems = refs[-2 - len(places)], refs[-1]
    copies = []
    for slot, (place, value, made) in enumerate(zip(places, coarse, refs[-1 - len(places) : -1])):
        lanes = lanes_of(place, value.shape[1])
        made[...] = total[:, lanes] + matmul(both[...], value[...])
        copy = pltpu.make_async_copy(made, out.at[0, :, lanes], sems.at[slot])
        copy.start()
        copies.append(copy)
    for copy in copies:
        copy.wait()


def exchange(value, axis, bit):
    count = lax.axis_size(axis)
    return lax.ppermute(value, axis, [(i, i ^ bit) for i in range(count)])


def swap_ends(inner, outer):
    count = lax.axis_size("narrow")
    gaps = [(i, (i + 1 if i % 2 else i - 1) % count) for i in range(count)]
    outer = lax.ppermute(outer, "narrow", gaps)
    return exchange(inner, "narrow", 1), outer


def on_device(
    level_rhs,
    galerkin_cols,
    galerkin_blocks,
    restrict_cols,
    restrict_blocks,
    prolong_cols,
    prolong_blocks,
    coarse_inverse,
):
    levels = galerkin_cols.shape[0]
    count = galerkin_cols.shape[2]
    size = galerkin_blocks.shape[-1]
    rows, fields = level_rhs.shape[1:]
    half = fields // 2
    width = half // 2
    gcols, rcols, pcols = ((c, scalars()) for c in (galerkin_cols, restrict_cols, prolong_cols))
    square_shape = array((rows, rows), bf16)
    operator_shapes = [square_shape, array((rows, 2 * size), bf16), array((rows, 1), f32)]
    rmat_shape = array((rows, 2 * rows), bf16)
    chunk_shape = array((rows, width), bf16)
    real_shape = array((rows, width), f32)
    held = [pltpu.VMEM((rows, rows), bf16)]

    def ends_shape(columns):
        return array((size, columns), bf16)

    def of_level(value, level_idx):
        return value, level_block(value, level_idx)

    def flops(columns, products=1):
        return 2 * products * rows * rows * columns

    def place_of(far, given):
        return (0, far, half), (1, given, width)

    ends = run(
        start_kernel, "start", [ends_shape(fields)] * 2,
        [in_hbm(level_rhs), in_hbm(galerkin_blocks)],
        scratch=[
            pltpu.VMEM((2, size, fields), f32), pltpu.VMEM((2, size, size), bf16),
            pltpu.SemaphoreType.DMA((4,)),
        ],
    )
    inner, outer = swap_ends(*ends)
    rest, base, local, rim, scale = run(
        first_local_kernel, "first_local", [array((rows, fields), f32)] * 2 + operator_shapes,
        [level_rhs, ends[0], gcols, of_level(galerkin_blocks, 0)], flops=flops(fields),
    )
    operators = [(scale, local)]
    sent, kept = [], []
    for given in (1, 0):
        places = place_of(1, given), place_of(0, given)
        far, near = run(
            functools.partial(first_residual_kernel, places), "first_residual", [chunk_shape] * 2,
            [rest, rim, outer, inner],
        )
        sent.append(far)
        kept.append(near)
    bases = []
    pieces = lax.axis_size("narrow")
    for level_idx in range(levels - 1):
        other = [exchange(value, "wide", 1 << level_idx) for value in sent]
        rmat, local, rim, scale = run(
            functools.partial(operators_kernel, level_idx), "operators",
            [rmat_shape] + operator_shapes,
            [sent[0], rcols, of_level(restrict_blocks, level_idx),
             gcols, of_level(galerkin_blocks, level_idx + 1)],
        )
        operators.append((scale, local))
        joined = []
        for near, far in zip(kept, other):
            rhs, smoothed, *ends = run(
                functools.partial(join_kernel, level_idx), "join",
                [real_shape, chunk_shape] + [ends_shape(width)] * 2,
                [rmat, near, far, scale], flops=flops(width, 2),
            )
            inner, outer = swap_ends(*ends)
            joined.append((rhs, smoothed, scale, local, rim, outer, inner))
        made = []
        for operands in joined:
            value, made_base = run(
                residual_kernel, "residual",
                [chunk_shape, chunk_shape if level_idx == 0 else real_shape],
                [*operands, joined[-1][1]], flops=flops(width, 2),
            )
            made.append(value)
            bases.append(made_base)
        sent, kept = made[:1], made[-1:]
    last = levels - 1
    (other,) = (exchange(value, "wide", 1 << last) for value in sent)
    rmat, coarse_mat, near_bases, *ups = run(
        functools.partial(coarse_operators_kernel, last, 2, levels), "coarse_operators",
        [rmat_shape, array((rows, pieces * rows), bf16), array((rows, half), bf16)]
        + [square_shape] * (levels - 3),
        [kept[0], rcols, of_level(restrict_blocks, last), pcols, coarse_inverse, *bases[:2]]
        + [of_level(prolong_blocks, idx) for idx in range(2, levels)]
        + [value for pair in operators[2:] for value in pair],
        flops=flops(rows, 2 * (levels - 2) + pieces), scratch=held,
    )
    far_bases = exchange(near_bases, "wide", 1)
    (mine,) = run(
        functools.partial(last_join_kernel, last), "last_join", [chunk_shape],
        [rmat, kept[0], other], flops=flops(width, 2),
    )
    order = sorted(range(1, pieces), key=lambda o: (bin(o).count("1"), -o))
    parts = {0: mine}
    for offset in order:
        low = offset & -offset
        parts[offset] = exchange(parts[offset ^ low], "narrow", low)
    places = [place_of(far, given) for far in (0, 1) for given in (1, 0)]
    both, total = run(
        functools.partial(fine_operators_kernel, places), "fine_operators",
        [square_shape, array((rows, fields), f32)],
        [mine, pcols, of_level(prolong_blocks, 0), of_level(prolong_blocks, 1),
         *operators[0], *operators[1], base, near_bases, far_bases],
        flops=flops(rows, 5), scratch=held,
    )
    offsets = tuple(parts)
    operands = [coarse_mat] + [parts[o] for o in offsets] + [bases[-1]]
    for idx in reversed(range(2, last)):
        operands += [bases[idx], ups[idx - 2]]
    (value,) = run(
        functools.partial(up_kernel, offsets), "up", [chunk_shape], operands,
        flops=flops(width, len(offsets) + levels - 3),
    )
    gathered = [(value, place_of(0, 0))]
    for bits in (2, 1, 3):
        gathered.append((exchange(value, "wide", bits), place_of(bits & 1, bits >> 1)))
    result = None
    for group in (gathered[:1], gathered[1:3], gathered[3:]):
        operands = [value for value, _ in group] + [total, both]
        aliases = {}
        if result is not None:
            aliases[len(operands)] = 0
            operands.append(in_hbm(result))
        (result,) = run(
            functools.partial(output_kernel, tuple(place for _, place in group)),
            "output", [array((1, rows, fields), f32)], operands,
            flops=flops(width, len(group)),
            scratch=[pltpu.VMEM((rows, width), f32)] * len(group)
            + [pltpu.SemaphoreType.DMA((len(group),))],
            out_space=pltpu.HBM, aliases=aliases,
        )
    return result


def solution(mesh):
    in_specs = (
        P("wide", "narrow", None),
        P(None, "wide", "narrow", None),
        P(None, "wide", "narrow", None, None, None),
        P(None, "wide", "narrow", None),
        P(None, "wide", "narrow", None, None, None),
        P(None, "wide", "narrow", None),
        P(None, "wide", "narrow", None, None, None),
        P("narrow", None),
    )
    out_specs = P("wide", "narrow", None)
    return jax.shard_map(
        on_device, mesh=mesh, in_specs=in_specs, out_specs=out_specs, check_vma=False
    )
```

```python
import functools

import jax
import jax.numpy as jnp
from jax import lax
from jax.experimental import pallas as pl
from jax.experimental.pallas import tpu as pltpu
from jax.sharding import PartitionSpec as P

relax_down = 0.7
relax_up = 0.5
f32 = jnp.float32
bf16 = jnp.bfloat16
grant = 12 * 1024 * 1024


def matmul(a, b):
    return jnp.dot(a, b, preferred_element_type=f32)


def array(shape, dtype):
    return jax.ShapeDtypeStruct(shape, dtype)


def whole():
    return pl.BlockSpec(memory_space=pltpu.VMEM)


def level_block(value, level_idx):
    shape = (1,) + value.shape[1:]
    return pl.BlockSpec(shape, lambda i: (level_idx,) + (0,) * (value.ndim - 1))


def scalars():
    return pl.BlockSpec(memory_space=pltpu.SMEM)


def in_hbm(value):
    return pltpu.with_memory_space_constraint(value, pltpu.HBM), pl.BlockSpec(memory_space=pltpu.HBM)


def run(body, name, outs, operands, flops=0, scratch=(), out_space=pltpu.VMEM, aliases=None):
    arrays = [o[0] if isinstance(o, tuple) else o for o in operands]
    specs = [o[1] if isinstance(o, tuple) else whole() for o in operands]
    windows = any(isinstance(o, tuple) and o[1].block_shape is not None for o in operands)
    moved = sum(a.size * a.dtype.itemsize for a in arrays)
    return pl.pallas_call(
        body,
        grid=(1,) if windows else (),
        out_shape=outs,
        in_specs=specs,
        out_specs=[pl.BlockSpec(memory_space=out_space)] * len(outs),
        input_output_aliases=aliases or {},
        scratch_shapes=list(scratch),
        compiler_params=pltpu.CompilerParams(vmem_limit_bytes=grant),
        cost_estimate=pl.CostEstimate(flops=flops, bytes_accessed=moved, transcendentals=0),
        name=name,
    )(*arrays)


def diagonal_of(block):
    size = block.shape[0]
    rows = lax.broadcasted_iota(jnp.int32, (size, size), 0)
    lanes = lax.broadcasted_iota(jnp.int32, (size, size), 1)
    return jnp.sum(jnp.where(rows == lanes, block, 0.0), axis=1, keepdims=True)


def placed(base, others, ids, target):
    total = base
    for block, ident in zip(others, ids):
        term = block * jnp.where(ident == target, 1.0, 0.0).astype(f32)
        total = term if total is None else total + term
    return total


def parity_of():
    return lax.rem(lax.axis_index("narrow"), 2)


def put_ends(first, last, inner_ref, outer_ref):
    even = parity_of() == 0
    inner_ref[...] = jnp.where(even, last, first)
    outer_ref[...] = jnp.where(even, first, last)


def assemble_galerkin(level_idx, cols, blocks, local_ref, rim_ref, scale_ref):
    count, slots, size = blocks.shape[2], blocks.shape[3], blocks.shape[4]
    parity = parity_of()
    piece = lax.axis_index("narrow")
    last = lax.axis_size("narrow") - 1
    inside = jnp.where((piece == 0) | (piece == last), 0.0, 1.0).astype(f32)
    for b in range(count):
        held = [blocks[0, 0, b, s].astype(f32) for s in range(slots)]
        ids = [cols[level_idx, 0, b, s] for s in range(1, slots)]
        rows = pl.ds(b * size, size)
        scale_ref[rows, :] = 1.0 / diagonal_of(held[0])
        line = [placed(held[0] if c == b else None, held[1:], ids, c) for c in range(count)]
        local_ref[rows, :] = jnp.concatenate(line, axis=1).astype(bf16)
        rims = [
            placed(None, held[1:], ids, count + 1 - parity),
            placed(None, held[1:], ids, count + parity) * inside,
        ]
        rim_ref[rows, :] = jnp.concatenate(rims, axis=1).astype(bf16)


def assemble_restrict(level_idx, cols, blocks, out_ref):
    count, slots, size = blocks.shape[2], blocks.shape[3], blocks.shape[4]
    for b in range(count):
        held = [blocks[0, 0, b, s].astype(f32) for s in range(slots)]
        ids = [cols[level_idx, 0, b, s] for s in range(2, slots)]
        fixed = {b: held[0], count + b: held[1]}
        line = [placed(fixed.get(c), held[2:], ids, c) for c in range(2 * count)]
        out_ref[pl.ds(b * size, size), :] = jnp.concatenate(line, axis=1).astype(bf16)


def assemble_prolong(level_idx, cols, blocks, out_ref):
    count, slots, size = blocks.shape[2], blocks.shape[3], blocks.shape[4]
    for b in range(count):
        held = [blocks[0, 0, b, s].astype(f32) for s in range(slots)]
        ids = [cols[level_idx, 0, b, s] for s in range(1, slots)]
        line = [placed(held[0] if c == b else None, held[1:], ids, c) for c in range(count)]
        out_ref[pl.ds(b * size, size), :] = jnp.concatenate(line, axis=1).astype(bf16)


def start_kernel(places, rhs, blocks, inner_ref, *refs):
    *outers, rows, outer, pivots, sems = refs
    count, size = blocks.shape[2], blocks.shape[4]
    copies = []
    for slot, which in enumerate((0, count - 1)):
        source = rhs.at[0, pl.ds(which * size, size), :]
        copies.append(pltpu.make_async_copy(source, rows.at[slot], sems.at[slot]))
        source = blocks.at[0, 0, which, 0]
        copies.append(pltpu.make_async_copy(source, pivots.at[slot], sems.at[2 + slot]))
    for copy in copies:
        copy.start()
    for copy in copies:
        copy.wait()
    first, last = (
        (rows[slot] * (relax_down / diagonal_of(pivots[slot].astype(f32)))).astype(bf16)
        for slot in range(2)
    )
    put_ends(first, last, inner_ref, outer)
    for ref, pair in zip(outers, places):
        width = ref.shape[1] // 2
        for slot, place in enumerate(pair):
            ref[:, slot * width : (slot + 1) * width] = outer[:, lanes_of(place, width)]


def first_local_kernel(rhs, _, cols, blocks, rest, base, local, rim, scale):
    assemble_galerkin(0, cols, blocks, local, rim, scale)
    smoothed = rhs[0] * (relax_down * scale[...])
    left = rhs[0] - matmul(local[...], smoothed.astype(bf16))
    rest[...] = left
    base[...] = smoothed + (relax_up * scale[...]) * left


def bit_of(level_idx):
    return lax.axis_index("wide") >> level_idx & 1


def lanes_of(place, width):
    start = 0
    for level_idx, flip, step in place:
        start = start + (bit_of(level_idx) ^ flip) * step
    return pl.ds(pl.multiple_of(start, width), width)


def first_residual_kernel(places, rest, rim, outer, inner, *refs):
    width = refs[0].shape[1]
    for slot, (ref, place) in enumerate(zip(refs, places)):
        lanes = lanes_of(place, width)
        columns = pl.ds(slot * width, width)
        rims = jnp.concatenate([inner[:, lanes], outer[:, columns]], axis=0)
        ref[...] = (rest[:, lanes] - matmul(rim[...], rims)).astype(bf16)


def residual_kernel(rhs, smoothed, scale, local, rim, outer, inner, _, out, base):
    rims = jnp.concatenate([inner[...], outer[...]], axis=0)
    left = rhs[...] - matmul(local[...], smoothed[...])
    out[...] = (left - matmul(rim[...], rims)).astype(bf16)
    made = rhs[...] * (relax_down * scale[...]) + (relax_up * scale[...]) * left
    base[...] = made.astype(base.dtype)


def operators_kernel(level_idx, _, rcols, rblocks, cols, blocks, rmat, local, rim, scale):
    assemble_restrict(level_idx, rcols, rblocks, rmat)
    assemble_galerkin(level_idx + 1, cols, blocks, local, rim, scale)


def raising(level_idx, pcols, blocks, local, scale, held):
    assemble_prolong(level_idx, pcols, blocks, held)
    applied = matmul(local[...], held[...])
    return (held[...].astype(f32) - (relax_up * scale[...]) * applied).astype(bf16)


def coarse_operators_kernel(level_idx, first, levels, *refs):
    _, rcols, rblocks, pcols, inverse, one, two, *refs = refs
    places = range(first, levels)
    blocks, refs = refs[: len(places)], refs[len(places) :]
    pairs, refs = refs[: 2 * len(places)], refs[2 * len(places) :]
    rmat, coarse, bases, *up, held = refs
    width = one.shape[1]
    bases[:, :width] = one[...]
    bases[:, width:] = two[...]
    assemble_restrict(level_idx, rcols, rblocks, rmat)
    for idx in places:
        slot = idx - first
        made = raising(idx, pcols, blocks[slot], pairs[2 * slot + 1], pairs[2 * slot], held)
        if idx == levels - 1:
            coarse[...] = matmul(made, inverse[...]).astype(bf16)
        else:
            up[slot][...] = made


def fine_operators_kernel(
    places, _, pcols, blocks_0, blocks_1, scale_0, local_0, scale_1, local_1,
    base, near, far, both, total, held,
):
    lower = raising(0, pcols, blocks_0, local_0, scale_0, held)
    upper = raising(1, pcols, blocks_1, local_1, scale_1, held)
    both[...] = matmul(lower, upper).astype(bf16)
    width = near.shape[1] // 2
    for slot, place in enumerate(places):
        source = near if slot < 2 else far
        lanes = lanes_of(place, width)
        columns = pl.ds(slot % 2 * width, width)
        total[:, lanes] = base[:, lanes] + matmul(lower, source[:, columns])


def restricted(level_idx, rmat, kept, other):
    width = rmat.shape[1] // 2
    own = pl.multiple_of(bit_of(level_idx) * width, width)
    far = pl.multiple_of((1 - bit_of(level_idx)) * width, width)
    total = matmul(rmat[:, pl.ds(own, width)], kept[...])
    return total + matmul(rmat[:, pl.ds(far, width)], other[...])


def join_kernel(level_idx, rmat, kept, other, scale, rhs, smoothed, inner_ref, outer_ref):
    size = inner_ref.shape[0]
    current = restricted(level_idx, rmat, kept, other)
    rhs[...] = current
    rounded = (current * (relax_down * scale[...])).astype(bf16)
    smoothed[...] = rounded
    put_ends(rounded[:size], rounded[-size:], inner_ref, outer_ref)


def last_join_kernel(level_idx, rmat, kept, other, rounded):
    rounded[...] = restricted(level_idx, rmat, kept, other).astype(bf16)


def inverse_part(inverse, part, offset):
    depth = part.shape[0]
    piece = lax.axis_index("narrow") ^ offset
    return matmul(inverse[:, pl.ds(pl.multiple_of(piece * depth, depth), depth)], part[...])


def up_kernel(offsets, inverse, *refs):
    parts, refs = refs[: len(offsets)], refs[len(offsets) :]
    value = refs[0][...]
    for part, offset in zip(parts, offsets):
        value = value + inverse_part(inverse, part, offset)
    for step in range((len(refs) - 3) // 2):
        base, up = refs[2 + 2 * step : 4 + 2 * step]
        value = base[...] + matmul(up[...], value.astype(bf16))
    refs[-1][...] = value.astype(bf16)


def output_kernel(places, *refs):
    coarse, refs = refs[: len(places)], refs[len(places) :]
    total, both = refs[:2]
    out, sems = refs[-2 - len(places)], refs[-1]
    copies = []
    for slot, (place, value, made) in enumerate(zip(places, coarse, refs[-1 - len(places) : -1])):
        lanes = lanes_of(place, value.shape[1])
        made[...] = total[:, lanes] + matmul(both[...], value[...])
        copy = pltpu.make_async_copy(made, out.at[0, :, lanes], sems.at[slot])
        copy.start()
        copies.append(copy)
    for copy in copies:
        copy.wait()


def exchange(value, axis, bit):
    count = lax.axis_size(axis)
    return lax.ppermute(value, axis, [(i, i ^ bit) for i in range(count)])


def swap_outer(outer):
    count = lax.axis_size("narrow")
    gaps = [(i, (i + 1 if i % 2 else i - 1) % count) for i in range(count)]
    return lax.ppermute(outer, "narrow", gaps)


def on_device(
    level_rhs,
    galerkin_cols,
    galerkin_blocks,
    restrict_cols,
    restrict_blocks,
    prolong_cols,
    prolong_blocks,
    coarse_inverse,
):
    levels = galerkin_cols.shape[0]
    count = galerkin_cols.shape[2]
    size = galerkin_blocks.shape[-1]
    rows, fields = level_rhs.shape[1:]
    half = fields // 2
    width = half // 2
    gcols, rcols, pcols = ((c, scalars()) for c in (galerkin_cols, restrict_cols, prolong_cols))
    square_shape = array((rows, rows), bf16)
    operator_shapes = [square_shape, array((rows, 2 * size), bf16), array((rows, 1), f32)]
    rmat_shape = array((rows, 2 * rows), bf16)
    chunk_shape = array((rows, width), bf16)
    real_shape = array((rows, width), f32)
    held = [pltpu.VMEM((rows, rows), bf16)]

    def ends_shape(columns):
        return array((size, columns), bf16)

    def of_level(value, level_idx):
        return value, level_block(value, level_idx)

    def flops(columns, products=1):
        return 2 * products * rows * rows * columns

    def place_of(far, given):
        return (0, far, half), (1, given, width)

    pairs = [(place_of(1, given), place_of(0, given)) for given in (1, 0)]
    inner, *outers = run(
        functools.partial(start_kernel, pairs), "start",
        [ends_shape(fields)] + [ends_shape(half)] * 2,
        [in_hbm(level_rhs), in_hbm(galerkin_blocks)],
        scratch=[
            pltpu.VMEM((2, size, fields), f32), pltpu.VMEM((size, fields), bf16),
            pltpu.VMEM((2, size, size), bf16), pltpu.SemaphoreType.DMA((4,)),
        ],
    )
    first = outers[0]
    outers = [swap_outer(outer) for outer in outers]
    inner = exchange(inner, "narrow", 1)
    rest, base, local, rim, scale = run(
        first_local_kernel, "first_local", [array((rows, fields), f32)] * 2 + operator_shapes,
        [level_rhs, first, gcols, of_level(galerkin_blocks, 0)], flops=flops(fields),
    )
    operators = [(scale, local)]
    sent, kept = [], []
    for places, outer in zip(pairs, outers):
        far, near = run(
            functools.partial(first_residual_kernel, places), "first_residual", [chunk_shape] * 2,
            [rest, rim, outer, inner],
        )
        sent.append(far)
        kept.append(near)
    bases = []
    anchor = sent[0]
    pieces = lax.axis_size("narrow")
    for level_idx in range(levels - 1):
        other = [exchange(value, "wide", 1 << level_idx) for value in sent]
        rmat, local, rim, scale = run(
            functools.partial(operators_kernel, level_idx), "operators",
            [rmat_shape] + operator_shapes,
            [anchor, rcols, of_level(restrict_blocks, level_idx),
             gcols, of_level(galerkin_blocks, level_idx + 1)],
        )
        operators.append((scale, local))
        joined = []
        for near, far in zip(kept, other):
            rhs, smoothed, *ends = run(
                functools.partial(join_kernel, level_idx), "join",
                [real_shape, chunk_shape] + [ends_shape(width)] * 2,
                [rmat, near, far, scale], flops=flops(width, 2),
            )
            inner, outer = exchange(ends[0], "narrow", 1), swap_outer(ends[1])
            joined.append((rhs, smoothed, scale, local, rim, outer, inner))
        anchor = joined[-1][1]
        made = []
        for operands in joined:
            value, made_base = run(
                residual_kernel, "residual",
                [chunk_shape, chunk_shape if level_idx == 0 else real_shape],
                [*operands, joined[-1][-1]], flops=flops(width, 2),
            )
            made.append(value)
            bases.append(made_base)
        sent, kept = made[:1], made[-1:]
    last = levels - 1
    (other,) = (exchange(value, "wide", 1 << last) for value in sent)
    rmat, coarse_mat, near_bases, *ups = run(
        functools.partial(coarse_operators_kernel, last, 2, levels), "coarse_operators",
        [rmat_shape, array((rows, pieces * rows), bf16), array((rows, half), bf16)]
        + [square_shape] * (levels - 3),
        [kept[0], rcols, of_level(restrict_blocks, last), pcols, coarse_inverse, *bases[:2]]
        + [of_level(prolong_blocks, idx) for idx in range(2, levels)]
        + [value for pair in operators[2:] for value in pair],
        flops=flops(rows, 2 * (levels - 2) + pieces), scratch=held,
    )
    far_bases = exchange(near_bases, "wide", 1)
    (mine,) = run(
        functools.partial(last_join_kernel, last), "last_join", [chunk_shape],
        [rmat, kept[0], other], flops=flops(width, 2),
    )
    order = sorted(range(1, pieces), key=lambda o: (bin(o).count("1"), -o))
    parts = {0: mine}
    for offset in order:
        low = offset & -offset
        parts[offset] = exchange(parts[offset ^ low], "narrow", low)
    places = [place_of(far, given) for far in (0, 1) for given in (1, 0)]
    both, total = run(
        functools.partial(fine_operators_kernel, places), "fine_operators",
        [square_shape, array((rows, fields), f32)],
        [mine, pcols, of_level(prolong_blocks, 0), of_level(prolong_blocks, 1),
         *operators[0], *operators[1], base, near_bases, far_bases],
        flops=flops(rows, 5), scratch=held,
    )
    offsets = tuple(parts)
    operands = [coarse_mat] + [parts[o] for o in offsets] + [bases[-1], both]
    for idx in reversed(range(2, last)):
        operands += [bases[idx], ups[idx - 2]]
    (value,) = run(
        functools.partial(up_kernel, offsets), "up", [chunk_shape], operands,
        flops=flops(width, len(offsets) + levels - 3),
    )
    gathered = [(value, place_of(0, 0))]
    for bits in (3, 1, 2):
        gathered.append((exchange(value, "wide", bits), place_of(bits & 1, bits >> 1)))
    result = None
    for group in (gathered[:1], gathered[1:3], gathered[3:]):
        operands = [value for value, _ in group] + [total, both]
        aliases = {}
        if result is not None:
            aliases[len(operands)] = 0
            operands.append(in_hbm(result))
        (result,) = run(
            functools.partial(output_kernel, tuple(place for _, place in group)),
            "output", [array((1, rows, fields), f32)], operands,
            flops=flops(width, len(group)),
            scratch=[pltpu.VMEM((rows, width), f32)] * len(group)
            + [pltpu.SemaphoreType.DMA((len(group),))],
            out_space=pltpu.HBM, aliases=aliases,
        )
    return result


def solution(mesh):
    in_specs = (
        P("wide", "narrow", None),
        P(None, "wide", "narrow", None),
        P(None, "wide", "narrow", None, None, None),
        P(None, "wide", "narrow", None),
        P(None, "wide", "narrow", None, None, None),
        P(None, "wide", "narrow", None),
        P(None, "wide", "narrow", None, None, None),
        P("narrow", None),
    )
    out_specs = P("wide", "narrow", None)
    return jax.shard_map(
        on_device, mesh=mesh, in_specs=in_specs, out_specs=out_specs, check_vma=False
    )
```

```python
import functools

import jax
import jax.numpy as jnp
from jax import lax
from jax.experimental import pallas as pl
from jax.experimental.pallas import tpu as pltpu
from jax.sharding import PartitionSpec as P

relax_down = 0.7
relax_up = 0.5
f32 = jnp.float32
bf16 = jnp.bfloat16
grant = 12 * 1024 * 1024
late_cost = 4 * 10**9


def matmul(a, b):
    return jnp.dot(a, b, preferred_element_type=f32)


def array(shape, dtype):
    return jax.ShapeDtypeStruct(shape, dtype)


def whole():
    return pl.BlockSpec(memory_space=pltpu.VMEM)


def level_block(value, level_idx):
    shape = (1,) + value.shape[1:]
    return pl.BlockSpec(shape, lambda i: (level_idx,) + (0,) * (value.ndim - 1))


def scalars():
    return pl.BlockSpec(memory_space=pltpu.SMEM)


def in_hbm(value):
    return pltpu.with_memory_space_constraint(value, pltpu.HBM), pl.BlockSpec(memory_space=pltpu.HBM)


def in_vmem(value):
    return pltpu.with_memory_space_constraint(value, pltpu.VMEM)


def run(body, name, outs, operands, flops=0, scratch=(), out_space=pltpu.VMEM, aliases=None):
    arrays = [o[0] if isinstance(o, tuple) else in_vmem(o) for o in operands]
    specs = [o[1] if isinstance(o, tuple) else whole() for o in operands]
    windows = any(isinstance(o, tuple) and o[1].block_shape is not None for o in operands)
    moved = sum(a.size * a.dtype.itemsize for a in arrays)
    return pl.pallas_call(
        body,
        grid=(1,) if windows else (),
        out_shape=[out_space(o.shape, o.dtype) for o in outs],
        in_specs=specs,
        out_specs=[pl.BlockSpec(memory_space=out_space)] * len(outs),
        input_output_aliases=aliases or {},
        scratch_shapes=list(scratch),
        compiler_params=pltpu.CompilerParams(vmem_limit_bytes=grant),
        cost_estimate=pl.CostEstimate(flops=flops, bytes_accessed=moved, transcendentals=0),
        name=name,
    )(*arrays)


def diagonal_of(block):
    size = block.shape[0]
    rows = lax.broadcasted_iota(jnp.int32, (size, size), 0)
    lanes = lax.broadcasted_iota(jnp.int32, (size, size), 1)
    return jnp.sum(jnp.where(rows == lanes, block, 0.0), axis=1, keepdims=True)


def placed(base, others, ids, target):
    total = base
    for block, ident in zip(others, ids):
        term = block * jnp.where(ident == target, 1.0, 0.0).astype(f32)
        total = term if total is None else total + term
    return total


def parity_of():
    return lax.rem(lax.axis_index("narrow"), 2)


def put_ends(first, last, inner_ref, outer_ref):
    even = parity_of() == 0
    inner_ref[...] = jnp.where(even, last, first)
    outer_ref[...] = jnp.where(even, first, last)


def assemble_galerkin(level_idx, cols, blocks, local_ref, rim_ref, scale_ref):
    count, slots, size = blocks.shape[2], blocks.shape[3], blocks.shape[4]
    parity = parity_of()
    piece = lax.axis_index("narrow")
    last = lax.axis_size("narrow") - 1
    inside = jnp.where((piece == 0) | (piece == last), 0.0, 1.0).astype(f32)
    for b in range(count):
        held = [blocks[0, 0, b, s].astype(f32) for s in range(slots)]
        ids = [cols[level_idx, 0, b, s] for s in range(1, slots)]
        rows = pl.ds(b * size, size)
        scale_ref[rows, :] = 1.0 / diagonal_of(held[0])
        line = [placed(held[0] if c == b else None, held[1:], ids, c) for c in range(count)]
        local_ref[rows, :] = jnp.concatenate(line, axis=1).astype(bf16)
        rims = [
            placed(None, held[1:], ids, count + 1 - parity),
            placed(None, held[1:], ids, count + parity) * inside,
        ]
        rim_ref[rows, :] = jnp.concatenate(rims, axis=1).astype(bf16)


def assemble_restrict(level_idx, cols, blocks, out_ref):
    count, slots, size = blocks.shape[2], blocks.shape[3], blocks.shape[4]
    for b in range(count):
        held = [blocks[0, 0, b, s].astype(f32) for s in range(slots)]
        ids = [cols[level_idx, 0, b, s] for s in range(2, slots)]
        fixed = {b: held[0], count + b: held[1]}
        line = [placed(fixed.get(c), held[2:], ids, c) for c in range(2 * count)]
        out_ref[pl.ds(b * size, size), :] = jnp.concatenate(line, axis=1).astype(bf16)


def assemble_prolong(level_idx, cols, blocks, out_ref):
    count, slots, size = blocks.shape[2], blocks.shape[3], blocks.shape[4]
    for b in range(count):
        held = [blocks[0, 0, b, s].astype(f32) for s in range(slots)]
        ids = [cols[level_idx, 0, b, s] for s in range(1, slots)]
        line = [placed(held[0] if c == b else None, held[1:], ids, c) for c in range(count)]
        out_ref[pl.ds(b * size, size), :] = jnp.concatenate(line, axis=1).astype(bf16)


def start_kernel(places, rhs, blocks, *refs):
    table, held, inner_ref, *outers, rows, outer, pivots, sems = refs
    count, size = blocks.shape[2], blocks.shape[4]
    copies = []
    for slot, which in enumerate((0, count - 1)):
        source = rhs.at[0, pl.ds(which * size, size), :]
        copies.append(pltpu.make_async_copy(source, rows.at[slot], sems.at[slot]))
        source = blocks.at[0, 0, which, 0]
        copies.append(pltpu.make_async_copy(source, pivots.at[slot], sems.at[2 + slot]))
    copies.append(pltpu.make_async_copy(table, held, sems.at[4]))
    for copy in copies:
        copy.start()
    for copy in copies:
        copy.wait()
    first, last = (
        (rows[slot] * (relax_down / diagonal_of(pivots[slot].astype(f32)))).astype(bf16)
        for slot in range(2)
    )
    put_ends(first, last, inner_ref, outer)
    for ref, pair in zip(outers, places):
        width = ref.shape[1] // 2
        for slot, place in enumerate(pair):
            ref[:, slot * width : (slot + 1) * width] = outer[:, lanes_of(place, width)]


def first_local_kernel(rhs, _, cols, blocks, rest, base, local, rim, scale):
    assemble_galerkin(0, cols, blocks, local, rim, scale)
    smoothed = rhs[0] * (relax_down * scale[...])
    left = rhs[0] - matmul(local[...], smoothed.astype(bf16))
    rest[...] = left
    base[...] = smoothed + (relax_up * scale[...]) * left


def bit_of(level_idx):
    return lax.axis_index("wide") >> level_idx & 1


def lanes_of(place, width):
    start = 0
    for level_idx, flip, step in place:
        start = start + (bit_of(level_idx) ^ flip) * step
    return pl.ds(pl.multiple_of(start, width), width)


def first_residual_kernel(places, rest, rim, outer, inner, *refs):
    width = refs[0].shape[1]
    for slot, (ref, place) in enumerate(zip(refs, places)):
        lanes = lanes_of(place, width)
        columns = pl.ds(slot * width, width)
        rims = jnp.concatenate([inner[:, lanes], outer[:, columns]], axis=0)
        ref[...] = (rest[:, lanes] - matmul(rim[...], rims)).astype(bf16)


def residual_kernel(rhs, smoothed, scale, local, rim, outer, inner, _, out, base):
    rims = jnp.concatenate([inner[...], outer[...]], axis=0)
    left = rhs[...] - matmul(local[...], smoothed[...])
    out[...] = (left - matmul(rim[...], rims)).astype(bf16)
    made = rhs[...] * (relax_down * scale[...]) + (relax_up * scale[...]) * left
    base[...] = made.astype(base.dtype)


def operators_kernel(level_idx, _, rcols, rblocks, cols, blocks, rmat, local, rim, scale):
    assemble_restrict(level_idx, rcols, rblocks, rmat)
    assemble_galerkin(level_idx + 1, cols, blocks, local, rim, scale)


def raising(level_idx, pcols, blocks, local, scale, held):
    assemble_prolong(level_idx, pcols, blocks, held)
    applied = matmul(local[...], held[...])
    return (held[...].astype(f32) - (relax_up * scale[...]) * applied).astype(bf16)


def coarse_operators_kernel(level_idx, first, levels, *refs):
    _, rcols, rblocks, pcols, inverse, one, two, *refs = refs
    places = range(first, levels)
    blocks, refs = refs[: len(places)], refs[len(places) :]
    pairs, refs = refs[: 2 * len(places)], refs[2 * len(places) :]
    rmat, coarse, bases, *up, held = refs
    width = one.shape[1]
    bases[:, :width] = one[...]
    bases[:, width:] = two[...]
    assemble_restrict(level_idx, rcols, rblocks, rmat)
    for idx in places:
        slot = idx - first
        made = raising(idx, pcols, blocks[slot], pairs[2 * slot + 1], pairs[2 * slot], held)
        if idx == levels - 1:
            coarse[...] = matmul(made, inverse[...]).astype(bf16)
        else:
            up[slot][...] = made


def fine_operators_kernel(
    places, _, pcols, blocks_0, blocks_1, scale_0, local_0, scale_1, local_1,
    base, near, far, both, total, held,
):
    lower = raising(0, pcols, blocks_0, local_0, scale_0, held)
    upper = raising(1, pcols, blocks_1, local_1, scale_1, held)
    both[...] = matmul(lower, upper).astype(bf16)
    width = near.shape[1] // 2
    for slot, place in enumerate(places):
        source = near if slot < 2 else far
        lanes = lanes_of(place, width)
        columns = pl.ds(slot % 2 * width, width)
        total[:, lanes] = base[:, lanes] + matmul(lower, source[:, columns])


def restricted(level_idx, rmat, kept, other):
    width = rmat.shape[1] // 2
    own = pl.multiple_of(bit_of(level_idx) * width, width)
    far = pl.multiple_of((1 - bit_of(level_idx)) * width, width)
    total = matmul(rmat[:, pl.ds(own, width)], kept[...])
    return total + matmul(rmat[:, pl.ds(far, width)], other[...])


def join_kernel(level_idx, rmat, kept, other, scale, rhs, smoothed, inner_ref, outer_ref):
    size = inner_ref.shape[0]
    current = restricted(level_idx, rmat, kept, other)
    rhs[...] = current
    rounded = (current * (relax_down * scale[...])).astype(bf16)
    smoothed[...] = rounded
    put_ends(rounded[:size], rounded[-size:], inner_ref, outer_ref)


def last_join_kernel(level_idx, rmat, kept, other, rounded):
    rounded[...] = restricted(level_idx, rmat, kept, other).astype(bf16)


def inverse_part(inverse, part, offset):
    depth = part.shape[0]
    piece = lax.axis_index("narrow") ^ offset
    return matmul(inverse[:, pl.ds(pl.multiple_of(piece * depth, depth), depth)], part[...])


def up_kernel(offsets, inverse, *refs):
    parts, refs = refs[: len(offsets)], refs[len(offsets) :]
    value = refs[0][...]
    for part, offset in zip(parts, offsets):
        value = value + inverse_part(inverse, part, offset)
    for step in range((len(refs) - 3) // 2):
        base, up = refs[2 + 2 * step : 4 + 2 * step]
        value = base[...] + matmul(up[...], value.astype(bf16))
    for peer in range(refs[-1].shape[0]):
        refs[-1][peer] = value.astype(bf16)


def output_kernel(gathered, total, both, out, made, sems):
    peers, _, width = gathered.shape
    half = peers * width // 2
    copies = []
    for peer in range(peers):
        lanes = pl.ds(peer % 2 * half + peer // 2 * width, width)
        made[peer] = total[:, lanes] + matmul(both[...], gathered[peer])
        copy = pltpu.make_async_copy(made.at[peer], out.at[0, :, lanes], sems.at[peer])
        copy.start()
        copies.append(copy)
    for copy in copies:
        copy.wait()


def exchange(value, axis, bit):
    count = lax.axis_size(axis)
    return lax.ppermute(value, axis, [(i, i ^ bit) for i in range(count)])


def swap_outer(outer):
    count = lax.axis_size("narrow")
    gaps = [(i, (i + 1 if i % 2 else i - 1) % count) for i in range(count)]
    return lax.ppermute(outer, "narrow", gaps)


def on_device(
    level_rhs,
    galerkin_cols,
    galerkin_blocks,
    restrict_cols,
    restrict_blocks,
    prolong_cols,
    prolong_blocks,
    coarse_inverse,
):
    levels = galerkin_cols.shape[0]
    count = galerkin_cols.shape[2]
    size = galerkin_blocks.shape[-1]
    rows, fields = level_rhs.shape[1:]
    half = fields // 2
    width = half // 2
    rcols, pcols = ((c, scalars()) for c in (restrict_cols, prolong_cols))
    square_shape = array((rows, rows), bf16)
    operator_shapes = [square_shape, array((rows, 2 * size), bf16), array((rows, 1), f32)]
    rmat_shape = array((rows, 2 * rows), bf16)
    chunk_shape = array((rows, width), bf16)
    real_shape = array((rows, width), f32)
    held = [pltpu.VMEM((rows, rows), bf16)]

    def ends_shape(columns):
        return array((size, columns), bf16)

    def of_level(value, level_idx):
        return value, level_block(value, level_idx)

    def flops(columns, products=1):
        return 2 * products * rows * rows * columns

    def place_of(far, given):
        return (0, far, half), (1, given, width)

    pairs = [(place_of(1, given), place_of(0, given)) for given in (1, 0)]
    gcols, inner, *outers = run(
        functools.partial(start_kernel, pairs), "start",
        [array(galerkin_cols.shape, jnp.int32), ends_shape(fields)] + [ends_shape(half)] * 2,
        [in_hbm(level_rhs), in_hbm(galerkin_blocks), in_hbm(galerkin_cols)],
        scratch=[
            pltpu.VMEM((2, size, fields), f32), pltpu.VMEM((size, fields), bf16),
            pltpu.VMEM((2, size, size), bf16), pltpu.SemaphoreType.DMA((5,)),
        ],
    )
    gcols = in_vmem(gcols), scalars()
    first = outers[0]
    outers = [swap_outer(outer) for outer in outers]
    inner = exchange(inner, "narrow", 1)
    rest, base, local, rim, scale = run(
        first_local_kernel, "first_local", [array((rows, fields), f32)] * 2 + operator_shapes,
        [level_rhs, first, gcols, of_level(galerkin_blocks, 0)], flops=flops(fields),
    )
    operators = [(scale, local)]
    sent, kept = [], []
    for places, outer in zip(pairs, outers):
        far, near = run(
            functools.partial(first_residual_kernel, places), "first_residual", [chunk_shape] * 2,
            [rest, rim, outer, inner],
        )
        sent.append(far)
        kept.append(near)
    bases = []
    anchor = sent[0]
    pieces = lax.axis_size("narrow")
    for level_idx in range(levels - 1):
        other = [exchange(value, "wide", 1 << level_idx) for value in sent]
        rmat, local, rim, scale = run(
            functools.partial(operators_kernel, level_idx), "operators",
            [rmat_shape] + operator_shapes,
            [anchor, rcols, of_level(restrict_blocks, level_idx),
             gcols, of_level(galerkin_blocks, level_idx + 1)],
        )
        operators.append((scale, local))
        joined = []
        for near, far in zip(kept, other):
            rhs, smoothed, *ends = run(
                functools.partial(join_kernel, level_idx), "join",
                [real_shape, chunk_shape] + [ends_shape(width)] * 2,
                [rmat, near, far, scale], flops=flops(width, 2),
            )
            inner, outer = exchange(ends[0], "narrow", 1), swap_outer(ends[1])
            joined.append((rhs, smoothed, scale, local, rim, outer, inner))
        made = []
        for operands in joined:
            value, made_base = run(
                residual_kernel, "residual",
                [chunk_shape, chunk_shape if level_idx == 0 else real_shape],
                [*operands, joined[-1][1]], flops=flops(width, 2) if not made else late_cost,
            )
            made.append(value)
            bases.append(made_base)
        sent, kept = made[:1], made[-1:]
        anchor = made[0]
    last = levels - 1
    (other,) = (exchange(value, "wide", 1 << last) for value in sent)
    rmat, coarse_mat, near_bases, *ups = run(
        functools.partial(coarse_operators_kernel, last, 2, levels), "coarse_operators",
        [rmat_shape, array((rows, pieces * rows), bf16), array((rows, half), bf16)]
        + [square_shape] * (levels - 3),
        [kept[0], rcols, of_level(restrict_blocks, last), pcols, coarse_inverse, *bases[:2]]
        + [of_level(prolong_blocks, idx) for idx in range(2, levels)]
        + [value for pair in operators[2:] for value in pair],
        flops=flops(rows, 2 * (levels - 2) + pieces), scratch=held,
    )
    far_bases = exchange(near_bases, "wide", 1)
    (mine,) = run(
        functools.partial(last_join_kernel, last), "last_join", [chunk_shape],
        [rmat, kept[0], other], flops=flops(width, 2),
    )
    order = sorted(range(1, pieces), key=lambda o: (bin(o).count("1"), -o))
    parts = {0: mine}
    for offset in order:
        low = offset & -offset
        parts[offset] = exchange(parts[offset ^ low], "narrow", low)
    places = [place_of(far, given) for far in (0, 1) for given in (1, 0)]
    both, total = run(
        functools.partial(fine_operators_kernel, places), "fine_operators",
        [square_shape, array((rows, fields), f32)],
        [mine, pcols, of_level(prolong_blocks, 0), of_level(prolong_blocks, 1),
         *operators[0], *operators[1], base, near_bases, far_bases],
        flops=flops(rows, 5), scratch=held,
    )
    offsets = tuple(parts)
    operands = [coarse_mat] + [parts[o] for o in offsets] + [bases[-1], both]
    for idx in reversed(range(2, last)):
        operands += [bases[idx], ups[idx - 2]]
    (value,) = run(
        functools.partial(up_kernel, offsets), "up", [array((4, rows, width), bf16)], operands,
        flops=flops(width, len(offsets) + levels - 3),
    )
    peers = 4
    groups = [list(range(i, i + peers)) for i in range(0, lax.axis_size("wide"), peers)]
    gathered = lax.all_to_all(value, "wide", 0, 0, axis_index_groups=groups)
    (result,) = run(
        output_kernel, "output", [array((1, rows, fields), f32)], [gathered, total, both],
        flops=flops(fields), out_space=pltpu.HBM,
        scratch=[pltpu.VMEM((peers, rows, width), f32), pltpu.SemaphoreType.DMA((peers,))],
    )
    return result


def solution(mesh):
    in_specs = (
        P("wide", "narrow", None),
        P(None, "wide", "narrow", None),
        P(None, "wide", "narrow", None, None, None),
        P(None, "wide", "narrow", None),
        P(None, "wide", "narrow", None, None, None),
        P(None, "wide", "narrow", None),
        P(None, "wide", "narrow", None, None, None),
        P("narrow", None),
    )
    out_specs = P("wide", "narrow", None)
    return jax.shard_map(
        on_device, mesh=mesh, in_specs=in_specs, out_specs=out_specs, check_vma=False
    )
```

```python
import functools

import jax
import jax.numpy as jnp
from jax import lax
from jax.experimental import pallas as pl
from jax.experimental.pallas import tpu as pltpu
from jax.sharding import PartitionSpec as P

relax_down = 0.7
relax_up = 0.5
f32 = jnp.float32
bf16 = jnp.bfloat16
grant = 12 * 1024 * 1024
late_cost = 4 * 10**9


def matmul(a, b):
    return jnp.dot(a, b, preferred_element_type=f32)


def array(shape, dtype):
    return jax.ShapeDtypeStruct(shape, dtype)


def whole():
    return pl.BlockSpec(memory_space=pltpu.VMEM)


def level_block(value, level_idx):
    shape = (1,) + value.shape[1:]
    return pl.BlockSpec(shape, lambda i: (level_idx,) + (0,) * (value.ndim - 1))


def scalars():
    return pl.BlockSpec(memory_space=pltpu.SMEM)


def in_hbm(value):
    return pltpu.with_memory_space_constraint(value, pltpu.HBM), pl.BlockSpec(memory_space=pltpu.HBM)


def in_vmem(value):
    return pltpu.with_memory_space_constraint(value, pltpu.VMEM)


def run(body, name, outs, operands, flops=0, scratch=(), out_space=pltpu.VMEM, aliases=None):
    arrays = [o[0] if isinstance(o, tuple) else in_vmem(o) for o in operands]
    specs = [o[1] if isinstance(o, tuple) else whole() for o in operands]
    windows = any(isinstance(o, tuple) and o[1].block_shape is not None for o in operands)
    moved = sum(a.size * a.dtype.itemsize for a in arrays)
    return pl.pallas_call(
        body,
        grid=(1,) if windows else (),
        out_shape=[out_space(o.shape, o.dtype) for o in outs],
        in_specs=specs,
        out_specs=[pl.BlockSpec(memory_space=out_space)] * len(outs),
        input_output_aliases=aliases or {},
        scratch_shapes=list(scratch),
        compiler_params=pltpu.CompilerParams(vmem_limit_bytes=grant),
        cost_estimate=pl.CostEstimate(flops=flops, bytes_accessed=moved, transcendentals=0),
        name=name,
    )(*arrays)


def diagonal_of(block):
    size = block.shape[0]
    rows = lax.broadcasted_iota(jnp.int32, (size, size), 0)
    lanes = lax.broadcasted_iota(jnp.int32, (size, size), 1)
    return jnp.sum(jnp.where(rows == lanes, block, 0.0), axis=1, keepdims=True)


def placed(base, others, ids, target):
    total = base
    for block, ident in zip(others, ids):
        term = block * jnp.where(ident == target, 1.0, 0.0).astype(f32)
        total = term if total is None else total + term
    return total


def parity_of():
    return lax.rem(lax.axis_index("narrow"), 2)


def put_ends(first, last, inner_ref, outer_ref):
    even = parity_of() == 0
    inner_ref[...] = jnp.where(even, last, first)
    outer_ref[...] = jnp.where(even, first, last)


def assemble_galerkin(level_idx, cols, blocks, local_ref, rim_ref, scale_ref):
    count, slots, size = blocks.shape[2], blocks.shape[3], blocks.shape[4]
    parity = parity_of()
    piece = lax.axis_index("narrow")
    last = lax.axis_size("narrow") - 1
    inside = jnp.where((piece == 0) | (piece == last), 0.0, 1.0).astype(f32)
    for b in range(count):
        held = [blocks[0, 0, b, s].astype(f32) for s in range(slots)]
        ids = [cols[level_idx, 0, b, s] for s in range(1, slots)]
        rows = pl.ds(b * size, size)
        scale_ref[rows, :] = 1.0 / diagonal_of(held[0])
        line = [placed(held[0] if c == b else None, held[1:], ids, c) for c in range(count)]
        local_ref[rows, :] = jnp.concatenate(line, axis=1).astype(bf16)
        rims = [
            placed(None, held[1:], ids, count + 1 - parity),
            placed(None, held[1:], ids, count + parity) * inside,
        ]
        rim_ref[rows, :] = jnp.concatenate(rims, axis=1).astype(bf16)


def assemble_restrict(level_idx, cols, blocks, out_ref):
    count, slots, size = blocks.shape[2], blocks.shape[3], blocks.shape[4]
    for b in range(count):
        held = [blocks[0, 0, b, s].astype(f32) for s in range(slots)]
        ids = [cols[level_idx, s, 0, b] for s in range(2, slots)]
        fixed = {b: held[0], count + b: held[1]}
        line = [placed(fixed.get(c), held[2:], ids, c) for c in range(2 * count)]
        out_ref[pl.ds(b * size, size), :] = jnp.concatenate(line, axis=1).astype(bf16)


def assemble_prolong(level_idx, cols, blocks, out_ref):
    count, slots, size = blocks.shape[2], blocks.shape[3], blocks.shape[4]
    for b in range(count):
        held = [blocks[0, 0, b, s].astype(f32) for s in range(slots)]
        ids = [cols[level_idx, 0, s, b] for s in range(1, slots)]
        line = [placed(held[0] if c == b else None, held[1:], ids, c) for c in range(count)]
        out_ref[pl.ds(b * size, size), :] = jnp.concatenate(line, axis=1).astype(bf16)


def start_kernel(places, rhs, blocks, *refs):
    table, held, inner_ref, *outers, rows, outer, pivots, sems = refs
    count, size = blocks.shape[2], blocks.shape[4]
    copies = []
    for slot, which in enumerate((0, count - 1)):
        source = rhs.at[0, pl.ds(which * size, size), :]
        copies.append(pltpu.make_async_copy(source, rows.at[slot], sems.at[slot]))
        source = blocks.at[0, 0, which, 0]
        copies.append(pltpu.make_async_copy(source, pivots.at[slot], sems.at[2 + slot]))
    copies.append(pltpu.make_async_copy(table, held, sems.at[4]))
    for copy in copies:
        copy.start()
    for copy in copies:
        copy.wait()
    first, last = (
        (rows[slot] * (relax_down / diagonal_of(pivots[slot].astype(f32)))).astype(bf16)
        for slot in range(2)
    )
    put_ends(first, last, inner_ref, outer)
    for ref, pair in zip(outers, places):
        width = ref.shape[1] // 2
        for slot, place in enumerate(pair):
            ref[:, slot * width : (slot + 1) * width] = outer[:, lanes_of(place, width)]


def first_local_kernel(rhs, _, cols, blocks, rest, base, local, rim, scale):
    assemble_galerkin(0, cols, blocks, local, rim, scale)
    smoothed = rhs[0] * (relax_down * scale[...])
    left = rhs[0] - matmul(local[...], smoothed.astype(bf16))
    rest[...] = left
    base[...] = smoothed + (relax_up * scale[...]) * left


def bit_of(level_idx):
    return lax.axis_index("wide") >> level_idx & 1


def lanes_of(place, width):
    start = 0
    for level_idx, flip, step in place:
        start = start + (bit_of(level_idx) ^ flip) * step
    return pl.ds(pl.multiple_of(start, width), width)


def first_residual_kernel(places, rest, rim, outer, inner, *refs):
    width = refs[0].shape[1]
    for slot, (ref, place) in enumerate(zip(refs, places)):
        lanes = lanes_of(place, width)
        columns = pl.ds(slot * width, width)
        rims = jnp.concatenate([inner[:, lanes], outer[:, columns]], axis=0)
        ref[...] = (rest[:, lanes] - matmul(rim[...], rims)).astype(bf16)


def residual_kernel(rhs, smoothed, scale, local, rim, outer, inner, _, out, base):
    rims = jnp.concatenate([inner[...], outer[...]], axis=0)
    left = rhs[...] - matmul(local[...], smoothed[...])
    out[...] = (left - matmul(rim[...], rims)).astype(bf16)
    base[...] = rhs[...] * (relax_down * scale[...]) + (relax_up * scale[...]) * left


def operators_kernel(level_idx, _, rcols, rblocks, cols, blocks, rmat, local, rim, scale):
    assemble_restrict(level_idx, rcols, rblocks, rmat)
    assemble_galerkin(level_idx + 1, cols, blocks, local, rim, scale)


def raising(level_idx, pcols, blocks, local, scale, held):
    assemble_prolong(level_idx, pcols, blocks, held)
    applied = matmul(local[...], held[...])
    return (held[...].astype(f32) - (relax_up * scale[...]) * applied).astype(bf16)


def coarse_operators_kernel(level_idx, first, levels, *refs):
    _, rcols, rblocks, pcols, inverse, *refs = refs
    places = range(first, levels)
    blocks, refs = refs[: len(places)], refs[len(places) :]
    pairs, refs = refs[: 2 * len(places)], refs[2 * len(places) :]
    rmat, coarse, *up, held = refs
    assemble_restrict(level_idx, rcols, rblocks, rmat)
    for idx in places:
        slot = idx - first
        made = raising(idx, pcols, blocks[slot], pairs[2 * slot + 1], pairs[2 * slot], held)
        if idx == levels - 1:
            coarse[...] = matmul(made, inverse[...]).astype(bf16)
        else:
            up[slot][...] = made


def fine_operators_kernel(
    _, pcols, blocks_0, blocks_1, scale_0, local_0, scale_1, local_1, lower, upper, held
):
    upper[...] = raising(1, pcols, blocks_1, local_1, scale_1, held)
    lower[...] = raising(0, pcols, blocks_0, local_0, scale_0, held)


def restricted(level_idx, rmat, kept, other):
    width = rmat.shape[1] // 2
    own = pl.multiple_of(bit_of(level_idx) * width, width)
    far = pl.multiple_of((1 - bit_of(level_idx)) * width, width)
    total = matmul(rmat[:, pl.ds(own, width)], kept[...])
    return total + matmul(rmat[:, pl.ds(far, width)], other[...])


def join_kernel(level_idx, rmat, kept, other, scale, rhs, smoothed, inner_ref, outer_ref):
    size = inner_ref.shape[0]
    current = restricted(level_idx, rmat, kept, other)
    rhs[...] = current
    rounded = (current * (relax_down * scale[...])).astype(bf16)
    smoothed[...] = rounded
    put_ends(rounded[:size], rounded[-size:], inner_ref, outer_ref)


def last_join_kernel(level_idx, rmat, kept, other, rounded):
    rounded[...] = restricted(level_idx, rmat, kept, other).astype(bf16)


def inverse_part(inverse, part, offset):
    depth = part.shape[0]
    piece = lax.axis_index("narrow") ^ offset
    return matmul(inverse[:, pl.ds(pl.multiple_of(piece * depth, depth), depth)], part[...])


def up_kernel(offsets, inverse, *refs):
    parts, refs = refs[: len(offsets)], refs[len(offsets) :]
    value = refs[0][...]
    for part, offset in zip(parts, offsets):
        value = value + inverse_part(inverse, part, offset)
    refs, (base, up, coarse, raised) = refs[1:-4], refs[-4:]
    for step in range(len(refs) // 2):
        value = refs[2 * step][...] + matmul(refs[2 * step + 1][...], value.astype(bf16))
    value = value.astype(bf16)
    coarse[...] = value
    raised[...] = (base[...] + matmul(up[...], value)).astype(bf16)


def raise_kernel(coarse, base, up, out):
    out[...] = (base[...] + matmul(up[...], coarse[...])).astype(bf16)


def output_kernel(places, *refs):
    coarse, (base, lower), refs = refs[: len(places)], refs[len(places) :][:2], refs[len(places) + 2 :]
    out, made, sems = refs[-3:]
    copies = []
    for slot, (place, value) in enumerate(zip(places, coarse)):
        lanes = lanes_of(place, value.shape[1])
        made[slot] = base[:, lanes] + matmul(lower[...], value[...])
        copy = pltpu.make_async_copy(made.at[slot], out.at[0, :, lanes], sems.at[slot])
        copy.start()
        copies.append(copy)
    for copy in copies:
        copy.wait()


def exchange(value, axis, bit):
    count = lax.axis_size(axis)
    return lax.ppermute(value, axis, [(i, i ^ bit) for i in range(count)])


def swap_outer(outer):
    count = lax.axis_size("narrow")
    gaps = [(i, (i + 1 if i % 2 else i - 1) % count) for i in range(count)]
    return lax.ppermute(outer, "narrow", gaps)


def on_device(
    level_rhs,
    galerkin_cols,
    galerkin_blocks,
    restrict_cols,
    restrict_blocks,
    prolong_cols,
    prolong_blocks,
    coarse_inverse,
):
    levels = galerkin_cols.shape[0]
    count = galerkin_cols.shape[2]
    size = galerkin_blocks.shape[-1]
    rows, fields = level_rhs.shape[1:]
    half = fields // 2
    width = half // 2
    rcols = restrict_cols.transpose(0, 3, 1, 2), scalars()
    pcols = prolong_cols.transpose(0, 1, 3, 2), scalars()
    square_shape = array((rows, rows), bf16)
    operator_shapes = [square_shape, array((rows, 2 * size), bf16), array((rows, 1), f32)]
    rmat_shape = array((rows, 2 * rows), bf16)
    chunk_shape = array((rows, width), bf16)
    real_shape = array((rows, width), f32)
    held = [pltpu.VMEM((rows, rows), bf16)]

    def ends_shape(columns):
        return array((size, columns), bf16)

    def of_level(value, level_idx):
        return value, level_block(value, level_idx)

    def flops(columns, products=1):
        return 2 * products * rows * rows * columns

    def place_of(far, given):
        return (0, far, half), (1, given, width)

    pairs = [(place_of(1, given), place_of(0, given)) for given in (1, 0)]
    gcols, inner, *outers = run(
        functools.partial(start_kernel, pairs), "start",
        [array(galerkin_cols.shape, jnp.int32), ends_shape(fields)] + [ends_shape(half)] * 2,
        [in_hbm(level_rhs), in_hbm(galerkin_blocks), in_hbm(galerkin_cols)],
        scratch=[
            pltpu.VMEM((2, size, fields), f32), pltpu.VMEM((size, fields), bf16),
            pltpu.VMEM((2, size, size), bf16), pltpu.SemaphoreType.DMA((5,)),
        ],
    )
    gcols = in_vmem(gcols), scalars()
    first = outers[0]
    outers = [swap_outer(outer) for outer in outers]
    inner = exchange(inner, "narrow", 1)
    rest, base, local, rim, scale = run(
        first_local_kernel, "first_local", [array((rows, fields), f32)] * 2 + operator_shapes,
        [level_rhs, first, gcols, of_level(galerkin_blocks, 0)], flops=flops(fields),
    )
    operators = [(scale, local)]
    sent, kept = [], []
    for places, outer in zip(pairs, outers):
        far, near = run(
            functools.partial(first_residual_kernel, places), "first_residual", [chunk_shape] * 2,
            [rest, rim, outer, inner],
        )
        sent.append(far)
        kept.append(near)
    bases = []
    anchor = sent[0]
    pieces = lax.axis_size("narrow")
    for level_idx in range(levels - 1):
        other = [exchange(value, "wide", 1 << level_idx) for value in sent]
        rmat, local, rim, scale = run(
            functools.partial(operators_kernel, level_idx), "operators",
            [rmat_shape] + operator_shapes,
            [anchor, rcols, of_level(restrict_blocks, level_idx),
             gcols, of_level(galerkin_blocks, level_idx + 1)],
        )
        operators.append((scale, local))
        joined = []
        for near, far in zip(kept, other):
            rhs, smoothed, *ends = run(
                functools.partial(join_kernel, level_idx), "join",
                [real_shape, chunk_shape] + [ends_shape(width)] * 2,
                [rmat, near, far, scale], flops=flops(width, 2),
            )
            inner, outer = exchange(ends[0], "narrow", 1), swap_outer(ends[1])
            joined.append((rhs, smoothed, scale, local, rim, outer, inner))
        made = []
        for operands in joined:
            value, made_base = run(
                residual_kernel, "residual",
                [chunk_shape, real_shape],
                [*operands, joined[-1][1]], flops=flops(width, 2) if not made else late_cost,
            )
            made.append(value)
            bases.append(made_base)
        sent, kept = made[:1], made[-1:]
        anchor = made[0]
    last = levels - 1
    (other,) = (exchange(value, "wide", 1 << last) for value in sent)
    rmat, coarse_mat, *ups = run(
        functools.partial(coarse_operators_kernel, last, 2, levels), "coarse_operators",
        [rmat_shape, array((rows, pieces * rows), bf16)]
        + [square_shape] * (levels - 3),
        [kept[0], rcols, of_level(restrict_blocks, last), pcols, coarse_inverse]
        + [of_level(prolong_blocks, idx) for idx in range(2, levels)]
        + [value for pair in operators[2:] for value in pair],
        flops=flops(rows, 2 * (levels - 2) + pieces), scratch=held,
    )
    (mine,) = run(
        functools.partial(last_join_kernel, last), "last_join", [chunk_shape],
        [rmat, kept[0], other], flops=flops(width, 2),
    )
    order = sorted(range(1, pieces), key=lambda o: (bin(o).count("1"), -o))
    parts = {0: mine}
    for offset in order:
        low = offset & -offset
        parts[offset] = exchange(parts[offset ^ low], "narrow", low)
    lower, upper = run(
        fine_operators_kernel, "fine_operators", [square_shape] * 2,
        [mine, pcols, of_level(prolong_blocks, 0), of_level(prolong_blocks, 1),
         *operators[0], *operators[1]],
        flops=flops(rows, 2), scratch=held,
    )
    offsets = tuple(parts)
    operands = [coarse_mat] + [parts[o] for o in offsets] + [bases[-1]]
    for idx in reversed(range(2, last)):
        operands += [bases[idx], ups[idx - 2]]
    coarse, near = run(
        functools.partial(up_kernel, offsets), "up", [chunk_shape] * 2,
        operands + [bases[1], upper], flops=flops(width, len(offsets) + levels - 2),
    )
    other = exchange(coarse, "wide", 2)
    far = exchange(near, "wide", 1)
    (near_other,) = run(
        raise_kernel, "raise", [chunk_shape], [other, bases[0], upper], flops=flops(width)
    )
    far_other = exchange(near_other, "wide", 1)
    result = None
    for group in (
        [(near, place_of(0, 0))],
        [(near_other, place_of(0, 1)), (far, place_of(1, 0))],
        [(far_other, place_of(1, 1))],
    ):
        operands = [value for value, _ in group] + [base, lower]
        aliases = {}
        if result is not None:
            aliases[len(operands)] = 0
            operands.append(in_hbm(result))
        (result,) = run(
            functools.partial(output_kernel, tuple(place for _, place in group)),
            "output", [array((1, rows, fields), f32)], operands,
            flops=flops(width, len(group)), out_space=pltpu.HBM, aliases=aliases,
            scratch=[
                pltpu.VMEM((len(group), rows, width), f32), pltpu.SemaphoreType.DMA((len(group),))
            ],
        )
    return result


def solution(mesh):
    in_specs = (
        P("wide", "narrow", None),
        P(None, "wide", "narrow", None),
        P(None, "wide", "narrow", None, None, None),
        P(None, "wide", "narrow", None),
        P(None, "wide", "narrow", None, None, None),
        P(None, "wide", "narrow", None),
        P(None, "wide", "narrow", None, None, None),
        P("narrow", None),
    )
    out_specs = P("wide", "narrow", None)
    return jax.shard_map(
        on_device, mesh=mesh, in_specs=in_specs, out_specs=out_specs, check_vma=False
    )
```

```python
import functools

import jax
import jax.numpy as jnp
from jax import lax
from jax.experimental import pallas as pl
from jax.experimental.pallas import tpu as pltpu
from jax.sharding import PartitionSpec as P

relax_down = 0.7
relax_up = 0.5
f32 = jnp.float32
bf16 = jnp.bfloat16
grant = 12 * 1024 * 1024
late_cost = 4 * 10**9


def matmul(a, b):
    return jnp.dot(a, b, preferred_element_type=f32)


def array(shape, dtype):
    return jax.ShapeDtypeStruct(shape, dtype)


def whole():
    return pl.BlockSpec(memory_space=pltpu.VMEM)


def level_block(value, level_idx):
    shape = (1,) + value.shape[1:]
    return pl.BlockSpec(shape, lambda i: (level_idx,) + (0,) * (value.ndim - 1))


def scalars():
    return pl.BlockSpec(memory_space=pltpu.SMEM)


def in_hbm(value):
    return pltpu.with_memory_space_constraint(value, pltpu.HBM), pl.BlockSpec(memory_space=pltpu.HBM)


def in_vmem(value):
    return pltpu.with_memory_space_constraint(value, pltpu.VMEM)


def run(body, name, outs, operands, flops=0, scratch=(), out_space=pltpu.VMEM, aliases=None):
    arrays = [o[0] if isinstance(o, tuple) else in_vmem(o) for o in operands]
    specs = [o[1] if isinstance(o, tuple) else whole() for o in operands]
    windows = any(isinstance(o, tuple) and o[1].block_shape is not None for o in operands)
    moved = sum(a.size * a.dtype.itemsize for a in arrays)
    return pl.pallas_call(
        body,
        grid=(1,) if windows else (),
        out_shape=[out_space(o.shape, o.dtype) for o in outs],
        in_specs=specs,
        out_specs=[pl.BlockSpec(memory_space=out_space)] * len(outs),
        input_output_aliases=aliases or {},
        scratch_shapes=list(scratch),
        compiler_params=pltpu.CompilerParams(vmem_limit_bytes=grant),
        cost_estimate=pl.CostEstimate(flops=flops, bytes_accessed=moved, transcendentals=0),
        name=name,
    )(*arrays)


def diagonal_of(block):
    size = block.shape[0]
    rows = lax.broadcasted_iota(jnp.int32, (size, size), 0)
    lanes = lax.broadcasted_iota(jnp.int32, (size, size), 1)
    return jnp.sum(jnp.where(rows == lanes, block, 0.0), axis=1, keepdims=True)


def placed(base, others, ids, target):
    total = base
    for block, ident in zip(others, ids):
        term = block * jnp.where(ident == target, 1.0, 0.0).astype(f32)
        total = term if total is None else total + term
    return total


def parity_of():
    return lax.rem(lax.axis_index("narrow"), 2)


def put_ends(first, last, inner_ref, outer_ref):
    even = parity_of() == 0
    inner_ref[...] = jnp.where(even, last, first)
    outer_ref[...] = jnp.where(even, first, last)


def assemble_galerkin(level_idx, cols, blocks, local_ref, rim_ref, scale_ref):
    count, slots, size = blocks.shape[2], blocks.shape[3], blocks.shape[4]
    parity = parity_of()
    piece = lax.axis_index("narrow")
    last = lax.axis_size("narrow") - 1
    inside = jnp.where((piece == 0) | (piece == last), 0.0, 1.0).astype(f32)
    for b in range(count):
        held = [blocks[0, 0, b, s].astype(f32) for s in range(slots)]
        ids = [cols[level_idx, 0, b, s] for s in range(1, slots)]
        rows = pl.ds(b * size, size)
        scale_ref[rows, :] = 1.0 / diagonal_of(held[0])
        line = [placed(held[0] if c == b else None, held[1:], ids, c) for c in range(count)]
        local_ref[rows, :] = jnp.concatenate(line, axis=1).astype(bf16)
        rims = [
            placed(None, held[1:], ids, count + 1 - parity),
            placed(None, held[1:], ids, count + parity) * inside,
        ]
        rim_ref[rows, :] = jnp.concatenate(rims, axis=1).astype(bf16)


def assemble_restrict(level_idx, cols, blocks, out_ref):
    count, slots, size = blocks.shape[2], blocks.shape[3], blocks.shape[4]
    for b in range(count):
        held = [blocks[0, 0, b, s].astype(f32) for s in range(slots)]
        ids = [cols[level_idx, s, 0, b] for s in range(2, slots)]
        fixed = {b: held[0], count + b: held[1]}
        line = [placed(fixed.get(c), held[2:], ids, c) for c in range(2 * count)]
        out_ref[pl.ds(b * size, size), :] = jnp.concatenate(line, axis=1).astype(bf16)


def assemble_prolong(level_idx, cols, blocks, out_ref):
    count, slots, size = blocks.shape[2], blocks.shape[3], blocks.shape[4]
    for b in range(count):
        held = [blocks[0, 0, b, s].astype(f32) for s in range(slots)]
        ids = [cols[level_idx, 0, s, b] for s in range(1, slots)]
        line = [placed(held[0] if c == b else None, held[1:], ids, c) for c in range(count)]
        out_ref[pl.ds(b * size, size), :] = jnp.concatenate(line, axis=1).astype(bf16)


def start_kernel(places, rhs, blocks, *refs):
    table, held, inner_ref, *outers, rows, outer, pivots, sems = refs
    count, size = blocks.shape[2], blocks.shape[4]
    copies = []
    for slot, which in enumerate((0, count - 1)):
        source = rhs.at[0, pl.ds(which * size, size), :]
        copies.append(pltpu.make_async_copy(source, rows.at[slot], sems.at[slot]))
        source = blocks.at[0, 0, which, 0]
        copies.append(pltpu.make_async_copy(source, pivots.at[slot], sems.at[2 + slot]))
    copies.append(pltpu.make_async_copy(table, held, sems.at[4]))
    for copy in copies:
        copy.start()
    for copy in copies:
        copy.wait()
    first, last = (
        (rows[slot] * (relax_down / diagonal_of(pivots[slot].astype(f32)))).astype(bf16)
        for slot in range(2)
    )
    put_ends(first, last, inner_ref, outer)
    for ref, pair in zip(outers, places):
        width = ref.shape[1] // 2
        for slot, place in enumerate(pair):
            ref[:, slot * width : (slot + 1) * width] = outer[:, lanes_of(place, width)]


def first_local_kernel(rhs, _, cols, blocks, rest, base, local, rim, scale):
    assemble_galerkin(0, cols, blocks, local, rim, scale)
    smoothed = rhs[0] * (relax_down * scale[...])
    left = rhs[0] - matmul(local[...], smoothed.astype(bf16))
    rest[...] = left
    base[...] = smoothed + (relax_up * scale[...]) * left


def bit_of(level_idx):
    return lax.axis_index("wide") >> level_idx & 1


def lanes_of(place, width):
    start = 0
    for level_idx, flip, step in place:
        start = start + (bit_of(level_idx) ^ flip) * step
    return pl.ds(pl.multiple_of(start, width), width)


def first_residual_kernel(places, rest, rim, outer, inner, *refs):
    width = refs[0].shape[1]
    for slot, (ref, place) in enumerate(zip(refs, places)):
        lanes = lanes_of(place, width)
        columns = pl.ds(slot * width, width)
        rims = jnp.concatenate([inner[:, lanes], outer[:, columns]], axis=0)
        ref[...] = (rest[:, lanes] - matmul(rim[...], rims)).astype(bf16)


def residual_kernel(rhs, smoothed, scale, local, rim, outer, inner, _, out, base):
    rims = jnp.concatenate([inner[...], outer[...]], axis=0)
    left = rhs[...] - matmul(local[...], smoothed[...])
    out[...] = (left - matmul(rim[...], rims)).astype(bf16)
    made = rhs[...] * (relax_down * scale[...]) + (relax_up * scale[...]) * left
    base[...] = made.astype(base.dtype)


def operators_kernel(level_idx, _, rcols, rblocks, cols, blocks, rmat, local, rim, scale):
    assemble_restrict(level_idx, rcols, rblocks, rmat)
    assemble_galerkin(level_idx + 1, cols, blocks, local, rim, scale)


def raising(level_idx, pcols, blocks, local, scale, held):
    assemble_prolong(level_idx, pcols, blocks, held)
    applied = matmul(local[...], held[...])
    return (held[...].astype(f32) - (relax_up * scale[...]) * applied).astype(bf16)


def coarse_operators_kernel(level_idx, first, levels, *refs):
    _, _, rcols, rblocks, pcols, inverse, *refs = refs
    places = range(first, levels)
    blocks, refs = refs[: len(places)], refs[len(places) :]
    pairs, refs = refs[: 2 * len(places)], refs[2 * len(places) :]
    rmat, coarse, *up, held = refs
    assemble_restrict(level_idx, rcols, rblocks, rmat)
    for idx in places:
        slot = idx - first
        made = raising(idx, pcols, blocks[slot], pairs[2 * slot + 1], pairs[2 * slot], held)
        if idx == levels - 1:
            coarse[...] = matmul(made, inverse[...]).astype(bf16)
        else:
            up[slot][...] = made


def fine_operators_kernel(
    _, pcols, blocks_0, blocks_1, scale_0, local_0, scale_1, local_1, lower, upper, held
):
    upper[...] = raising(1, pcols, blocks_1, local_1, scale_1, held)
    lower[...] = raising(0, pcols, blocks_0, local_0, scale_0, held)


def restricted(level_idx, rmat, kept, other):
    width = rmat.shape[1] // 2
    own = pl.multiple_of(bit_of(level_idx) * width, width)
    far = pl.multiple_of((1 - bit_of(level_idx)) * width, width)
    total = matmul(rmat[:, pl.ds(own, width)], kept[...])
    return total + matmul(rmat[:, pl.ds(far, width)], other[...])


def join_kernel(level_idx, rmat, kept, other, scale, rhs, smoothed, inner_ref, outer_ref):
    size = inner_ref.shape[0]
    current = restricted(level_idx, rmat, kept, other)
    rhs[...] = current
    rounded = (current * (relax_down * scale[...])).astype(bf16)
    smoothed[...] = rounded
    put_ends(rounded[:size], rounded[-size:], inner_ref, outer_ref)


def last_join_kernel(level_idx, rmat, kept, other, rounded):
    rounded[...] = restricted(level_idx, rmat, kept, other).astype(bf16)


def inverse_part(inverse, part, offset):
    depth = part.shape[0]
    piece = lax.axis_index("narrow") ^ offset
    return matmul(inverse[:, pl.ds(pl.multiple_of(piece * depth, depth), depth)], part[...])


def up_kernel(offsets, inverse, *refs):
    parts, refs = refs[: len(offsets)], refs[len(offsets) :]
    value = refs[0][...]
    for part, offset in zip(parts, offsets):
        value = value + inverse_part(inverse, part, offset)
    refs, (base, up, coarse, raised) = refs[1:-4], refs[-4:]
    for step in range(len(refs) // 2):
        value = refs[2 * step][...] + matmul(refs[2 * step + 1][...], value.astype(bf16))
    value = value.astype(bf16)
    coarse[...] = value
    raised[...] = (base[...] + matmul(up[...], value)).astype(bf16)


def output_kernel(places, raised, *refs):
    count = len(places)
    coarse, refs = refs[:count], refs[count:]
    bases, refs = refs[: sum(raised)], refs[sum(raised) :]
    base, lower, upper = refs[:3]
    out, made, sems = refs[-3:]
    copies = []
    for slot, (place, value) in enumerate(zip(places, coarse)):
        value = value[...]
        if raised[slot]:
            value = (bases[sum(raised[:slot])][...] + matmul(upper[...], value)).astype(bf16)
        lanes = lanes_of(place, value.shape[1])
        made[slot] = base[:, lanes] + matmul(lower[...], value)
        copy = pltpu.make_async_copy(made.at[slot], out.at[0, :, lanes], sems.at[slot])
        copy.start()
        copies.append(copy)
    for copy in copies:
        copy.wait()


def exchange(value, axis, bit):
    count = lax.axis_size(axis)
    return lax.ppermute(value, axis, [(i, i ^ bit) for i in range(count)])


def swap_outer(outer):
    count = lax.axis_size("narrow")
    gaps = [(i, (i + 1 if i % 2 else i - 1) % count) for i in range(count)]
    return lax.ppermute(outer, "narrow", gaps)


def on_device(
    level_rhs,
    galerkin_cols,
    galerkin_blocks,
    restrict_cols,
    restrict_blocks,
    prolong_cols,
    prolong_blocks,
    coarse_inverse,
):
    levels = galerkin_cols.shape[0]
    count = galerkin_cols.shape[2]
    size = galerkin_blocks.shape[-1]
    rows, fields = level_rhs.shape[1:]
    half = fields // 2
    width = half // 2
    rcols = restrict_cols.transpose(0, 3, 1, 2), scalars()
    pcols = prolong_cols.transpose(0, 1, 3, 2), scalars()
    square_shape = array((rows, rows), bf16)
    operator_shapes = [square_shape, array((rows, 2 * size), bf16), array((rows, 1), f32)]
    rmat_shape = array((rows, 2 * rows), bf16)
    chunk_shape = array((rows, width), bf16)
    real_shape = array((rows, width), f32)
    held = [pltpu.VMEM((rows, rows), bf16)]

    def ends_shape(columns):
        return array((size, columns), bf16)

    def of_level(value, level_idx):
        return value, level_block(value, level_idx)

    def flops(columns, products=1):
        return 2 * products * rows * rows * columns

    def place_of(far, given):
        return (0, far, half), (1, given, width)

    pairs = [(place_of(1, given), place_of(0, given)) for given in (1, 0)]
    gcols, inner, *outers = run(
        functools.partial(start_kernel, pairs), "start",
        [array(galerkin_cols.shape, jnp.int32), ends_shape(fields)] + [ends_shape(half)] * 2,
        [in_hbm(level_rhs), in_hbm(galerkin_blocks), in_hbm(galerkin_cols)],
        scratch=[
            pltpu.VMEM((2, size, fields), f32), pltpu.VMEM((size, fields), bf16),
            pltpu.VMEM((2, size, size), bf16), pltpu.SemaphoreType.DMA((5,)),
        ],
    )
    gcols = in_vmem(gcols), scalars()
    first = outers[0]
    outers = [swap_outer(outer) for outer in outers]
    inner = exchange(inner, "narrow", 1)
    rest, base, local, rim, scale = run(
        first_local_kernel, "first_local", [array((rows, fields), f32)] * 2 + operator_shapes,
        [level_rhs, first, gcols, of_level(galerkin_blocks, 0)], flops=flops(fields),
    )
    operators = [(scale, local)]
    sent, kept = [], []
    for places, outer in zip(pairs, outers):
        far, near = run(
            functools.partial(first_residual_kernel, places), "first_residual", [chunk_shape] * 2,
            [rest, rim, outer, inner],
        )
        sent.append(far)
        kept.append(near)
    bases = []
    anchor = sent[0]
    pieces = lax.axis_size("narrow")
    for level_idx in range(levels - 1):
        other = [exchange(value, "wide", 1 << level_idx) for value in sent]
        rmat, local, rim, scale = run(
            functools.partial(operators_kernel, level_idx), "operators",
            [rmat_shape] + operator_shapes,
            [anchor, rcols, of_level(restrict_blocks, level_idx),
             gcols, of_level(galerkin_blocks, level_idx + 1)],
        )
        operators.append((scale, local))
        joined = []
        for near, far in zip(kept, other):
            rhs, smoothed, *ends = run(
                functools.partial(join_kernel, level_idx), "join",
                [real_shape, chunk_shape] + [ends_shape(width)] * 2,
                [rmat, near, far, scale], flops=flops(width, 2),
            )
            inner, outer = exchange(ends[0], "narrow", 1), swap_outer(ends[1])
            joined.append((rhs, smoothed, scale, local, rim, outer, inner))
        made = []
        for operands in joined:
            value, made_base = run(
                residual_kernel, "residual",
                [chunk_shape, real_shape if made or level_idx else chunk_shape],
                [*operands, joined[-1][1]], flops=flops(width, 2) if not made else late_cost,
            )
            made.append(value)
            bases.append(made_base)
        sent, kept = made[:1], made[-1:]
        anchor = made[0]
    last = levels - 1
    (other,) = (exchange(value, "wide", 1 << last) for value in sent)
    far_base = exchange(bases[0], "wide", 1)
    rmat, coarse_mat, *ups = run(
        functools.partial(coarse_operators_kernel, last, 2, levels), "coarse_operators",
        [rmat_shape, array((rows, pieces * rows), bf16)]
        + [square_shape] * (levels - 3),
        [kept[0], far_base, rcols, of_level(restrict_blocks, last), pcols, coarse_inverse]
        + [of_level(prolong_blocks, idx) for idx in range(2, levels)]
        + [value for pair in operators[2:] for value in pair],
        flops=flops(rows, 2 * (levels - 2) + pieces), scratch=held,
    )
    (mine,) = run(
        functools.partial(last_join_kernel, last), "last_join", [chunk_shape],
        [rmat, kept[0], other], flops=flops(width, 2),
    )
    order = sorted(range(1, pieces), key=lambda o: (bin(o).count("1"), -o))
    parts = {0: mine}
    for offset in order:
        low = offset & -offset
        parts[offset] = exchange(parts[offset ^ low], "narrow", low)
    lower, upper = run(
        fine_operators_kernel, "fine_operators", [square_shape] * 2,
        [mine, pcols, of_level(prolong_blocks, 0), of_level(prolong_blocks, 1),
         *operators[0], *operators[1]],
        flops=flops(rows, 2), scratch=held,
    )
    offsets = tuple(parts)
    operands = [coarse_mat] + [parts[o] for o in offsets] + [bases[-1]]
    for idx in reversed(range(2, last)):
        operands += [bases[idx], ups[idx - 2]]
    coarse, near = run(
        functools.partial(up_kernel, offsets), "up", [chunk_shape] * 2,
        operands + [bases[1], upper], flops=flops(width, len(offsets) + levels - 2),
    )
    diagonal = exchange(coarse, "wide", 3)
    far = exchange(near, "wide", 1)
    other = exchange(coarse, "wide", 2)
    result = None
    for group in (
        [(near, place_of(0, 0), None)],
        [(diagonal, place_of(1, 1), far_base),
         (far, place_of(1, 0), None),
         (other, place_of(0, 1), bases[0])],
    ):
        values, places, raising_bases = zip(*group)
        raised = tuple(value is not None for value in raising_bases)
        operands = list(values) + [value for value in raising_bases if value is not None]
        operands += [base, lower, upper]
        aliases = {}
        if result is not None:
            aliases[len(operands)] = 0
            operands.append(in_hbm(result))
        (result,) = run(
            functools.partial(output_kernel, places, raised),
            "output", [array((1, rows, fields), f32)], operands,
            flops=flops(width, len(group)), out_space=pltpu.HBM, aliases=aliases,
            scratch=[
                pltpu.VMEM((len(group), rows, width), f32), pltpu.SemaphoreType.DMA((len(group),))
            ],
        )
    return result


def solution(mesh):
    in_specs = (
        P("wide", "narrow", None),
        P(None, "wide", "narrow", None),
        P(None, "wide", "narrow", None, None, None),
        P(None, "wide", "narrow", None),
        P(None, "wide", "narrow", None, None, None),
        P(None, "wide", "narrow", None),
        P(None, "wide", "narrow", None, None, None),
        P("narrow", None),
    )
    out_specs = P("wide", "narrow", None)
    return jax.shard_map(
        on_device, mesh=mesh, in_specs=in_specs, out_specs=out_specs, check_vma=False
    )
```

```python
import functools

import jax
import jax.numpy as jnp
from jax import lax
from jax.experimental import pallas as pl
from jax.experimental.pallas import tpu as pltpu
from jax.sharding import PartitionSpec as P

relax_down = 0.7
relax_up = 0.5
f32 = jnp.float32
bf16 = jnp.bfloat16
grant = 12 * 1024 * 1024
late_cost = 4 * 10**9


def matmul(a, b):
    return jnp.dot(a, b, preferred_element_type=f32)


def array(shape, dtype):
    return jax.ShapeDtypeStruct(shape, dtype)


def whole():
    return pl.BlockSpec(memory_space=pltpu.VMEM)


def level_block(value, level_idx):
    shape = (1,) + value.shape[1:]
    return pl.BlockSpec(shape, lambda i: (level_idx,) + (0,) * (value.ndim - 1))


def scalars():
    return pl.BlockSpec(memory_space=pltpu.SMEM)


def in_hbm(value):
    return pltpu.with_memory_space_constraint(value, pltpu.HBM), pl.BlockSpec(memory_space=pltpu.HBM)


def in_vmem(value):
    return pltpu.with_memory_space_constraint(value, pltpu.VMEM)


def run(body, name, outs, operands, flops=0, scratch=(), out_space=pltpu.VMEM, aliases=None):
    arrays = [o[0] if isinstance(o, tuple) else in_vmem(o) for o in operands]
    specs = [o[1] if isinstance(o, tuple) else whole() for o in operands]
    windows = any(isinstance(o, tuple) and o[1].block_shape is not None for o in operands)
    moved = sum(a.size * a.dtype.itemsize for a in arrays)
    return pl.pallas_call(
        body,
        grid=(1,) if windows else (),
        out_shape=[out_space(o.shape, o.dtype) for o in outs],
        in_specs=specs,
        out_specs=[pl.BlockSpec(memory_space=out_space)] * len(outs),
        input_output_aliases=aliases or {},
        scratch_shapes=list(scratch),
        compiler_params=pltpu.CompilerParams(vmem_limit_bytes=grant),
        cost_estimate=pl.CostEstimate(flops=flops, bytes_accessed=moved, transcendentals=0),
        name=name,
    )(*arrays)


def diagonal_of(block):
    size = block.shape[0]
    rows = lax.broadcasted_iota(jnp.int32, (size, size), 0)
    lanes = lax.broadcasted_iota(jnp.int32, (size, size), 1)
    return jnp.sum(jnp.where(rows == lanes, block, 0.0), axis=1, keepdims=True)


def placed(base, others, ids, target):
    total = base
    for block, ident in zip(others, ids):
        term = block * jnp.where(ident == target, 1.0, 0.0).astype(f32)
        total = term if total is None else total + term
    return total


def parity_of():
    return lax.rem(lax.axis_index("narrow"), 2)


def put_ends(first, last, inner_ref, outer_ref):
    even = parity_of() == 0
    inner_ref[...] = jnp.where(even, last, first)
    outer_ref[...] = jnp.where(even, first, last)


def assemble_galerkin(level_idx, cols, blocks, local_ref, rim_ref, scale_ref):
    count, slots, size = blocks.shape[2], blocks.shape[3], blocks.shape[4]
    parity = parity_of()
    piece = lax.axis_index("narrow")
    last = lax.axis_size("narrow") - 1
    inside = jnp.where((piece == 0) | (piece == last), 0.0, 1.0).astype(f32)
    for b in range(count):
        held = [blocks[0, 0, b, s].astype(f32) for s in range(slots)]
        ids = [cols[level_idx, 0, b, s] for s in range(1, slots)]
        rows = pl.ds(b * size, size)
        scale_ref[rows, :] = 1.0 / diagonal_of(held[0])
        line = [placed(held[0] if c == b else None, held[1:], ids, c) for c in range(count)]
        local_ref[rows, :] = jnp.concatenate(line, axis=1).astype(bf16)
        rims = [
            placed(None, held[1:], ids, count + 1 - parity),
            placed(None, held[1:], ids, count + parity) * inside,
        ]
        rim_ref[rows, :] = jnp.concatenate(rims, axis=1).astype(bf16)


def assemble_restrict(level_idx, cols, blocks, out_ref):
    count, slots, size = blocks.shape[2], blocks.shape[3], blocks.shape[4]
    for b in range(count):
        held = [blocks[0, 0, b, s].astype(f32) for s in range(slots)]
        ids = [cols[level_idx, s, 0, b] for s in range(2, slots)]
        fixed = {b: held[0], count + b: held[1]}
        line = [placed(fixed.get(c), held[2:], ids, c) for c in range(2 * count)]
        out_ref[pl.ds(b * size, size), :] = jnp.concatenate(line, axis=1).astype(bf16)


def assemble_share(level_idx, cols, blocks, out_ref):
    count, slots, size = blocks.shape[2], blocks.shape[3], blocks.shape[4]
    bit = bit_of(level_idx)
    for b in range(count):
        held = [blocks[0, 0, b, s].astype(f32) for s in range(slots)]
        ids = [cols[level_idx, s, 0, b] for s in range(2, slots)]
        own = jnp.where(bit == 0, held[0], held[1])
        first = bit * count
        line = [placed(own if c == b else None, held[2:], ids, first + c) for c in range(count)]
        out_ref[pl.ds(b * size, size), :] = jnp.concatenate(line, axis=1).astype(bf16)


def assemble_prolong(level_idx, cols, blocks, out_ref):
    count, slots, size = blocks.shape[2], blocks.shape[3], blocks.shape[4]
    for b in range(count):
        held = [blocks[0, 0, b, s].astype(f32) for s in range(slots)]
        ids = [cols[level_idx, 0, s, b] for s in range(1, slots)]
        line = [placed(held[0] if c == b else None, held[1:], ids, c) for c in range(count)]
        out_ref[pl.ds(b * size, size), :] = jnp.concatenate(line, axis=1).astype(bf16)


def start_kernel(places, rhs, blocks, *refs):
    table, held, inner_ref, *outers, rows, outer, pivots, sems = refs
    count, size = blocks.shape[2], blocks.shape[4]
    copies = []
    for slot, which in enumerate((0, count - 1)):
        source = rhs.at[0, pl.ds(which * size, size), :]
        copies.append(pltpu.make_async_copy(source, rows.at[slot], sems.at[slot]))
        source = blocks.at[0, 0, which, 0]
        copies.append(pltpu.make_async_copy(source, pivots.at[slot], sems.at[2 + slot]))
    copies.append(pltpu.make_async_copy(table, held, sems.at[4]))
    for copy in copies:
        copy.start()
    for copy in copies:
        copy.wait()
    first, last = (
        (rows[slot] * (relax_down / diagonal_of(pivots[slot].astype(f32)))).astype(bf16)
        for slot in range(2)
    )
    put_ends(first, last, inner_ref, outer)
    for ref, pair in zip(outers, places):
        width = ref.shape[1] // 2
        for slot, place in enumerate(pair):
            ref[:, slot * width : (slot + 1) * width] = outer[:, lanes_of(place, width)]


def first_local_kernel(rhs, _, cols, blocks, rest, base, local, rim, scale):
    assemble_galerkin(0, cols, blocks, local, rim, scale)
    smoothed = rhs[0] * (relax_down * scale[...])
    left = rhs[0] - matmul(local[...], smoothed.astype(bf16))
    rest[...] = left
    base[...] = smoothed + (relax_up * scale[...]) * left


def bit_of(level_idx):
    return lax.axis_index("wide") >> level_idx & 1


def lanes_of(place, width):
    start = 0
    for level_idx, flip, step in place:
        start = start + (bit_of(level_idx) ^ flip) * step
    return pl.ds(pl.multiple_of(start, width), width)


def first_residual_kernel(places, rest, rim, outer, inner, *refs):
    width = refs[0].shape[1]
    for slot, (ref, place) in enumerate(zip(refs, places)):
        lanes = lanes_of(place, width)
        columns = pl.ds(slot * width, width)
        rims = jnp.concatenate([inner[:, lanes], outer[:, columns]], axis=0)
        ref[...] = (rest[:, lanes] - matmul(rim[...], rims)).astype(bf16)


def residual_kernel(rhs, smoothed, scale, local, rim, outer, inner, _, out, base):
    rims = jnp.concatenate([inner[...], outer[...]], axis=0)
    left = rhs[...] - matmul(local[...], smoothed[...])
    out[...] = (left - matmul(rim[...], rims)).astype(bf16)
    made = rhs[...] * (relax_down * scale[...]) + (relax_up * scale[...]) * left
    base[...] = made.astype(base.dtype)


def last_residual_kernel(rhs, smoothed, scale, local, rim, outer, inner, share, out, base):
    rims = jnp.concatenate([inner[...], outer[...]], axis=0)
    left = rhs[...] - matmul(local[...], smoothed[...])
    residual = (left - matmul(rim[...], rims)).astype(bf16)
    out[...] = matmul(share[...], residual).astype(bf16)
    base[...] = rhs[...] * (relax_down * scale[...]) + (relax_up * scale[...]) * left


def operators_kernel(level_idx, _, rcols, rblocks, cols, blocks, *refs):
    if len(refs) > 4:
        last_blocks, *refs = refs
        assemble_share(level_idx + 1, rcols, last_blocks, refs.pop())
    rmat, local, rim, scale = refs
    assemble_restrict(level_idx, rcols, rblocks, rmat)
    assemble_galerkin(level_idx + 1, cols, blocks, local, rim, scale)


def raising(level_idx, pcols, blocks, local, scale, held):
    assemble_prolong(level_idx, pcols, blocks, held)
    applied = matmul(local[...], held[...])
    return (held[...].astype(f32) - (relax_up * scale[...]) * applied).astype(bf16)


def coarse_operators_kernel(first, levels, *refs):
    _, _, pcols, inverse, *refs = refs
    places = range(first, levels)
    blocks, refs = refs[: len(places)], refs[len(places) :]
    pairs, refs = refs[: 2 * len(places)], refs[2 * len(places) :]
    coarse, *up, held = refs
    for idx in places:
        slot = idx - first
        made = raising(idx, pcols, blocks[slot], pairs[2 * slot + 1], pairs[2 * slot], held)
        if idx == levels - 1:
            coarse[...] = matmul(made, inverse[...]).astype(bf16)
        else:
            up[slot][...] = made


def fine_operators_kernel(
    _, pcols, blocks_0, blocks_1, scale_0, local_0, scale_1, local_1, lower, upper, held
):
    upper[...] = raising(1, pcols, blocks_1, local_1, scale_1, held)
    lower[...] = raising(0, pcols, blocks_0, local_0, scale_0, held)


def restricted(level_idx, rmat, kept, other):
    width = rmat.shape[1] // 2
    own = pl.multiple_of(bit_of(level_idx) * width, width)
    far = pl.multiple_of((1 - bit_of(level_idx)) * width, width)
    total = matmul(rmat[:, pl.ds(own, width)], kept[...])
    return total + matmul(rmat[:, pl.ds(far, width)], other[...])


def join_kernel(level_idx, rmat, kept, other, scale, rhs, smoothed, inner_ref, outer_ref):
    size = inner_ref.shape[0]
    current = restricted(level_idx, rmat, kept, other)
    rhs[...] = current
    rounded = (current * (relax_down * scale[...])).astype(bf16)
    smoothed[...] = rounded
    put_ends(rounded[:size], rounded[-size:], inner_ref, outer_ref)


def inverse_part(inverse, part, offset):
    depth = part.shape[0]
    piece = lax.axis_index("narrow") ^ offset
    return matmul(inverse[:, pl.ds(pl.multiple_of(piece * depth, depth), depth)], part[...])


def share_sum_kernel(far, own, *refs):
    refs[-1][...] = (far[...].astype(f32) + own[...].astype(f32)).astype(bf16)


def up_kernel(offsets, inverse, *refs):
    value = refs[len(offsets)][...]
    for part, offset in zip(refs, offsets):
        value = value + inverse_part(inverse, part, offset)
    refs = refs[len(offsets) + 1 :]
    refs, (base, up, coarse, raised) = refs[:-4], refs[-4:]
    for step in range(len(refs) // 2):
        value = refs[2 * step][...] + matmul(refs[2 * step + 1][...], value.astype(bf16))
    value = value.astype(bf16)
    coarse[...] = value
    raised[...] = (base[...] + matmul(up[...], value)).astype(bf16)


def output_kernel(places, raised, *refs):
    count = len(places)
    coarse, refs = refs[:count], refs[count:]
    bases, refs = refs[: sum(raised)], refs[sum(raised) :]
    base, lower, upper = refs[:3]
    out, made, sems = refs[-3:]
    copies = []
    for slot, (place, value) in enumerate(zip(places, coarse)):
        value = value[...]
        if raised[slot]:
            value = (bases[sum(raised[:slot])][...] + matmul(upper[...], value)).astype(bf16)
        lanes = lanes_of(place, value.shape[1])
        made[slot] = base[:, lanes] + matmul(lower[...], value)
        copy = pltpu.make_async_copy(made.at[slot], out.at[0, :, lanes], sems.at[slot])
        copy.start()
        copies.append(copy)
    for copy in copies:
        copy.wait()


def exchange(value, axis, bit):
    count = lax.axis_size(axis)
    return lax.ppermute(value, axis, [(i, i ^ bit) for i in range(count)])


def exchange_both(value, bit, offset):
    wide, narrow = lax.axis_size("wide"), lax.axis_size("narrow")
    pairs = [
        (w * narrow + j, (w ^ bit) * narrow + (j ^ offset))
        for w in range(wide) for j in range(narrow)
    ]
    return lax.ppermute(value, ("wide", "narrow"), pairs)


def swap_outer(outer):
    count = lax.axis_size("narrow")
    gaps = [(i, (i + 1 if i % 2 else i - 1) % count) for i in range(count)]
    return lax.ppermute(outer, "narrow", gaps)


def on_device(
    level_rhs,
    galerkin_cols,
    galerkin_blocks,
    restrict_cols,
    restrict_blocks,
    prolong_cols,
    prolong_blocks,
    coarse_inverse,
):
    levels = galerkin_cols.shape[0]
    count = galerkin_cols.shape[2]
    size = galerkin_blocks.shape[-1]
    rows, fields = level_rhs.shape[1:]
    half = fields // 2
    width = half // 2
    rcols = restrict_cols.transpose(0, 3, 1, 2), scalars()
    pcols = prolong_cols.transpose(0, 1, 3, 2), scalars()
    square_shape = array((rows, rows), bf16)
    operator_shapes = [square_shape, array((rows, 2 * size), bf16), array((rows, 1), f32)]
    rmat_shape = array((rows, 2 * rows), bf16)
    chunk_shape = array((rows, width), bf16)
    real_shape = array((rows, width), f32)
    held = [pltpu.VMEM((rows, rows), bf16)]

    def ends_shape(columns):
        return array((size, columns), bf16)

    def of_level(value, level_idx):
        return value, level_block(value, level_idx)

    def flops(columns, products=1):
        return 2 * products * rows * rows * columns

    def place_of(far, given):
        return (0, far, half), (1, given, width)

    pairs = [(place_of(1, given), place_of(0, given)) for given in (1, 0)]
    gcols, inner, *outers = run(
        functools.partial(start_kernel, pairs), "start",
        [array(galerkin_cols.shape, jnp.int32), ends_shape(fields)] + [ends_shape(half)] * 2,
        [in_hbm(level_rhs), in_hbm(galerkin_blocks), in_hbm(galerkin_cols)],
        scratch=[
            pltpu.VMEM((2, size, fields), f32), pltpu.VMEM((size, fields), bf16),
            pltpu.VMEM((2, size, size), bf16), pltpu.SemaphoreType.DMA((5,)),
        ],
    )
    gcols = in_vmem(gcols), scalars()
    first = outers[0]
    outers = [swap_outer(outer) for outer in outers]
    inner = exchange(inner, "narrow", 1)
    rest, base, local, rim, scale = run(
        first_local_kernel, "first_local", [array((rows, fields), f32)] * 2 + operator_shapes,
        [level_rhs, first, gcols, of_level(galerkin_blocks, 0)], flops=flops(fields),
    )
    operators = [(scale, local)]
    sent, kept = [], []
    for places, outer in zip(pairs, outers):
        far, near = run(
            functools.partial(first_residual_kernel, places), "first_residual", [chunk_shape] * 2,
            [rest, rim, outer, inner],
        )
        sent.append(far)
        kept.append(near)
    last = levels - 1
    bases = []
    anchor = sent[0]
    pieces = lax.axis_size("narrow")
    for level_idx in range(levels - 1):
        other = [exchange(value, "wide", 1 << level_idx) for value in sent]
        shapes = [rmat_shape] + operator_shapes
        operands = [anchor, rcols, of_level(restrict_blocks, level_idx),
                    gcols, of_level(galerkin_blocks, level_idx + 1)]
        if level_idx + 1 == last:
            shapes.append(square_shape)
            operands.append(of_level(restrict_blocks, last))
        rmat, local, rim, scale, *share = run(
            functools.partial(operators_kernel, level_idx), "operators", shapes, operands
        )
        operators.append((scale, local))
        joined = []
        for near, far in zip(kept, other):
            rhs, smoothed, *ends = run(
                functools.partial(join_kernel, level_idx), "join",
                [real_shape, chunk_shape] + [ends_shape(width)] * 2,
                [rmat, near, far, scale], flops=flops(width, 2),
            )
            inner, outer = exchange(ends[0], "narrow", 1), swap_outer(ends[1])
            joined.append((rhs, smoothed, scale, local, rim, outer, inner))
        made = []
        for operands in joined:
            value, made_base = run(
                last_residual_kernel if share else residual_kernel, "residual",
                [chunk_shape, real_shape if made or level_idx else chunk_shape],
                [*operands, *(share or [joined[-1][1]])],
                flops=flops(width, 2) if not made else late_cost,
            )
            made.append(value)
            bases.append(made_base)
        sent, kept = made[:1], made[-1:]
        anchor = made[0]
    (mine,) = kept
    far_parts = {o: exchange_both(mine, 1 << last, o) for o in range(0, pieces, 2)}
    far_base = exchange(bases[0], "wide", 1)
    own_parts = {o: exchange(mine, "narrow", o) if o else mine for o in range(0, pieces, 2)}
    coarse_mat, *ups = run(
        functools.partial(coarse_operators_kernel, 2, levels), "coarse_operators",
        [array((rows, pieces * rows), bf16)] + [square_shape] * (levels - 3),
        [mine, far_base, pcols, coarse_inverse]
        + [of_level(prolong_blocks, idx) for idx in range(2, levels)]
        + [value for pair in operators[2:] for value in pair],
        flops=flops(rows, 2 * (levels - 2) + pieces), scratch=held,
    )
    lower, upper = run(
        fine_operators_kernel, "fine_operators", [square_shape] * 2,
        [mine, pcols, of_level(prolong_blocks, 0), of_level(prolong_blocks, 1),
         *operators[0], *operators[1]],
        flops=flops(rows, 2), scratch=held,
    )
    parts = {}
    for offset in range(0, pieces, 2):
        (parts[offset],) = run(
            share_sum_kernel, "share_sum", [chunk_shape],
            [far_parts[offset], own_parts[offset], coarse_mat, upper],
        )
        parts[offset + 1] = exchange(parts[offset], "narrow", 1)
    offsets = tuple(parts)
    operands = [coarse_mat] + [parts[o] for o in offsets] + [bases[-1]]
    for idx in reversed(range(2, last)):
        operands += [bases[idx], ups[idx - 2]]
    coarse, near = run(
        functools.partial(up_kernel, offsets), "up", [chunk_shape] * 2,
        operands + [bases[1], upper], flops=flops(width, len(offsets) + levels - 2),
    )
    diagonal = exchange(coarse, "wide", 3)
    far = exchange(near, "wide", 1)
    other = exchange(coarse, "wide", 2)
    result = None
    for group in (
        [(near, place_of(0, 0), None)],
        [(diagonal, place_of(1, 1), far_base),
         (far, place_of(1, 0), None),
         (other, place_of(0, 1), bases[0])],
    ):
        values, places, raising_bases = zip(*group)
        raised = tuple(value is not None for value in raising_bases)
        operands = list(values) + [value for value in raising_bases if value is not None]
        operands += [base, lower, upper]
        aliases = {}
        if result is not None:
            aliases[len(operands)] = 0
            operands.append(in_hbm(result))
        (result,) = run(
            functools.partial(output_kernel, places, raised),
            "output", [array((1, rows, fields), f32)], operands,
            flops=flops(width, len(group)), out_space=pltpu.HBM, aliases=aliases,
            scratch=[
                pltpu.VMEM((len(group), rows, width), f32), pltpu.SemaphoreType.DMA((len(group),))
            ],
        )
    return result


def solution(mesh):
    in_specs = (
        P("wide", "narrow", None),
        P(None, "wide", "narrow", None),
        P(None, "wide", "narrow", None, None, None),
        P(None, "wide", "narrow", None),
        P(None, "wide", "narrow", None, None, None),
        P(None, "wide", "narrow", None),
        P(None, "wide", "narrow", None, None, None),
        P("narrow", None),
    )
    out_specs = P("wide", "narrow", None)
    return jax.shard_map(
        on_device, mesh=mesh, in_specs=in_specs, out_specs=out_specs, check_vma=False
    )
```

```python
import functools

import jax
import jax.numpy as jnp
from jax import lax
from jax.experimental import pallas as pl
from jax.experimental.pallas import tpu as pltpu
from jax.sharding import PartitionSpec as P

relax_down = 0.7
relax_up = 0.5
f32 = jnp.float32
bf16 = jnp.bfloat16
grant = 12 * 1024 * 1024


def matmul(a, b):
    return jnp.dot(a, b, preferred_element_type=f32)


def array(shape, dtype):
    return jax.ShapeDtypeStruct(shape, dtype)


def whole():
    return pl.BlockSpec(memory_space=pltpu.VMEM)


def level_block(value, level_idx):
    shape = (1,) + value.shape[1:]
    return pl.BlockSpec(shape, lambda i: (level_idx,) + (0,) * (value.ndim - 1))


def scalars():
    return pl.BlockSpec(memory_space=pltpu.SMEM)


def in_hbm(value):
    return pltpu.with_memory_space_constraint(value, pltpu.HBM), pl.BlockSpec(memory_space=pltpu.HBM)


def in_vmem(value):
    return pltpu.with_memory_space_constraint(value, pltpu.VMEM)


def run(body, name, outs, operands, flops=0, scratch=(), out_space=pltpu.VMEM, aliases=None):
    arrays = [o[0] if isinstance(o, tuple) else in_vmem(o) for o in operands]
    specs = [o[1] if isinstance(o, tuple) else whole() for o in operands]
    windows = any(isinstance(o, tuple) and o[1].block_shape is not None for o in operands)
    moved = sum(a.size * a.dtype.itemsize for a in arrays)
    return pl.pallas_call(
        body,
        grid=(1,) if windows else (),
        out_shape=[out_space(o.shape, o.dtype) for o in outs],
        in_specs=specs,
        out_specs=[pl.BlockSpec(memory_space=out_space)] * len(outs),
        input_output_aliases=aliases or {},
        scratch_shapes=list(scratch),
        compiler_params=pltpu.CompilerParams(vmem_limit_bytes=grant),
        cost_estimate=pl.CostEstimate(flops=flops, bytes_accessed=moved, transcendentals=0),
        name=name,
    )(*arrays)


def diagonal_of(block):
    size = block.shape[0]
    rows = lax.broadcasted_iota(jnp.int32, (size, size), 0)
    lanes = lax.broadcasted_iota(jnp.int32, (size, size), 1)
    return jnp.sum(jnp.where(rows == lanes, block, 0.0), axis=1, keepdims=True)


def placed(base, others, ids, target):
    total = base
    for block, ident in zip(others, ids):
        term = block * jnp.where(ident == target, 1.0, 0.0).astype(f32)
        total = term if total is None else total + term
    return total


def parity_of():
    return lax.rem(lax.axis_index("narrow"), 2)


def put_ends(first, last, inner_ref, outer_ref):
    even = parity_of() == 0
    inner_ref[...] = jnp.where(even, last, first)
    outer_ref[...] = jnp.where(even, first, last)


def assemble_galerkin(level_idx, cols, blocks, local_ref, rim_ref, scale_ref):
    count, slots, size = blocks.shape[2], blocks.shape[3], blocks.shape[4]
    parity = parity_of()
    piece = lax.axis_index("narrow")
    last = lax.axis_size("narrow") - 1
    inside = jnp.where((piece == 0) | (piece == last), 0.0, 1.0).astype(f32)
    for b in range(count):
        held = [blocks[0, 0, b, s].astype(f32) for s in range(slots)]
        ids = [cols[level_idx, 0, b, s] for s in range(1, slots)]
        rows = pl.ds(b * size, size)
        scale_ref[rows, :] = 1.0 / diagonal_of(held[0])
        line = [placed(held[0] if c == b else None, held[1:], ids, c) for c in range(count)]
        local_ref[rows, :] = jnp.concatenate(line, axis=1).astype(bf16)
        rims = [
            placed(None, held[1:], ids, count + 1 - parity),
            placed(None, held[1:], ids, count + parity) * inside,
        ]
        rim_ref[rows, :] = jnp.concatenate(rims, axis=1).astype(bf16)


def assemble_share(level_idx, cols, blocks, out_ref):
    count, slots, size = blocks.shape[2], blocks.shape[3], blocks.shape[4]
    bit = bit_of(level_idx)
    for b in range(count):
        held = [blocks[0, 0, b, s].astype(f32) for s in range(slots)]
        ids = [cols[level_idx, s, 0, b] for s in range(2, slots)]
        own = jnp.where(bit == 0, held[0], held[1])
        first = bit * count
        line = [placed(own if c == b else None, held[2:], ids, first + c) for c in range(count)]
        out_ref[pl.ds(b * size, size), :] = jnp.concatenate(line, axis=1).astype(bf16)


def assemble_prolong(level_idx, cols, blocks, out_ref):
    count, slots, size = blocks.shape[2], blocks.shape[3], blocks.shape[4]
    for b in range(count):
        held = [blocks[0, 0, b, s].astype(f32) for s in range(slots)]
        ids = [cols[level_idx, 0, s, b] for s in range(1, slots)]
        line = [placed(held[0] if c == b else None, held[1:], ids, c) for c in range(count)]
        out_ref[pl.ds(b * size, size), :] = jnp.concatenate(line, axis=1).astype(bf16)


def start_kernel(places, rhs, blocks, gtable, rtable, rblocks, *refs):
    gheld, rheld, rheld_blocks, held, inner_ref, *outers, rows, outer, pivots, sems = refs
    count, size = blocks.shape[2], blocks.shape[4]
    copies = []
    for slot, which in enumerate((0, count - 1)):
        source = rhs.at[0, pl.ds(which * size, size), :]
        copies.append(pltpu.make_async_copy(source, rows.at[slot], sems.at[slot]))
        source = blocks.at[0, 0, which, 0]
        copies.append(pltpu.make_async_copy(source, pivots.at[slot], sems.at[2 + slot]))
    copies.append(pltpu.make_async_copy(gtable, gheld, sems.at[4]))
    copies.append(pltpu.make_async_copy(rtable, rheld, sems.at[5]))
    copies.append(pltpu.make_async_copy(rblocks.at[pl.ds(0, 1)], rheld_blocks, sems.at[6]))
    for which in range(count):
        source = blocks.at[1, 0, which, 0]
        copies.append(pltpu.make_async_copy(source, held.at[which], sems.at[7 + which]))
    for copy in copies:
        copy.start()
    for copy in copies:
        copy.wait()
    first, last = (
        (rows[slot] * (relax_down / diagonal_of(pivots[slot].astype(f32)))).astype(bf16)
        for slot in range(2)
    )
    put_ends(first, last, inner_ref, outer)
    for ref, pair in zip(outers, places):
        width = ref.shape[1] // 2
        for slot, place in enumerate(pair):
            ref[:, slot * width : (slot + 1) * width] = outer[:, lanes_of(place, width)]


def first_local_kernel(
    rhs, _, cols, blocks, rcols, rblocks, pivots, rest, base, local, rim, scale, share, next_scale
):
    assemble_galerkin(0, cols, blocks, local, rim, scale)
    smoothed = rhs[0] * (relax_down * scale[...])
    left = rhs[0] - matmul(local[...], smoothed.astype(bf16))
    rest[...] = left
    base[...] = smoothed + (relax_up * scale[...]) * left
    assemble_share(0, rcols, rblocks, share)
    size = pivots.shape[1]
    for b in range(pivots.shape[0]):
        next_scale[pl.ds(b * size, size), :] = relax_down / diagonal_of(pivots[b].astype(f32))


def bit_of(level_idx):
    return lax.axis_index("wide") >> level_idx & 1


def lanes_of(place, width):
    start = 0
    for level_idx, flip, step in place:
        start = start + (bit_of(level_idx) ^ flip) * step
    return pl.ds(pl.multiple_of(start, width), width)


def ends_of(part, next_scale):
    size = part.shape[0] // 4
    first = (part[:size] * next_scale[:size, :]).astype(bf16)
    last = (part[-size:] * next_scale[-size:, :]).astype(bf16)
    even = parity_of() == 0
    return jnp.where(even, last, first), jnp.where(even, first, last)


def first_residual_kernel(places, rest, rim, outer, inner, share, next_scale, *refs):
    held, refs = refs[:-6], refs[-6:]
    kept, joined = refs[0], refs[1:]
    ends = joined[1:]
    width = kept.shape[1]
    for slot, place in enumerate(places):
        lanes = lanes_of(place, width)
        columns = pl.ds(slot * width, width)
        rims = jnp.concatenate([inner[:, lanes], outer[:, columns]], axis=0)
        residual = (rest[:, lanes] - matmul(rim[...], rims)).astype(bf16)
        part = matmul(share[...], residual)
        if slot:
            kept[...] = part
        else:
            joined[0][:, joined[0].shape[1] - width :] = part.astype(bf16)
        for ref, made in zip(ends[2 * slot : 2 * slot + 2], ends_of(part, next_scale)):
            ref[:, ref.shape[1] - width :] = made
    for ref, value in zip(joined, held):
        ref[:, :width] = value[...]


def level_kernel(slot, kinds, rhs_own, rhs_far, scale, local, rim, *refs):
    far_inner, far_outer, near_inner, near_outer, share, *refs = refs
    width = rhs_own.shape[1]
    columns = pl.ds(slot * width, width)
    halo = [
        (far[:, columns].astype(f32) + near[:, columns].astype(f32)).astype(bf16)
        for far, near in ((far_inner, near_inner), (far_outer, near_outer))
    ]
    rhs = rhs_own[...] + rhs_far[:, columns].astype(f32)
    smoothed = rhs * (relax_down * scale[...])
    left = rhs - matmul(local[...], smoothed.astype(bf16))
    rims = jnp.concatenate(halo, axis=0)
    residual = (left - matmul(rim[...], rims)).astype(bf16)
    part = matmul(share[...], residual)
    if "ends" in kinds:
        next_scale, *refs = refs
    base, *refs = refs
    made = smoothed + (relax_up * scale[...]) * left
    base[...] = made.astype(base.dtype)
    if "sent" in kinds:
        refs[0][...] = part.astype(bf16)
        refs = refs[1:]
    if "kept" in kinds:
        refs[0][...] = part
        refs = refs[1:]
    if "ends" in kinds:
        refs[0][...], refs[1][...] = ends_of(part, next_scale)


def operators_kernel(level_idx, _, cols, blocks, rcols, rblocks, *refs):
    if len(refs) > 4:
        pivots, *refs, next_scale = refs
        size = pivots.shape[-1]
        for b in range(pivots.shape[2]):
            made = relax_down / diagonal_of(pivots[0, 0, b, 0].astype(f32))
            next_scale[pl.ds(b * size, size), :] = made
    local, rim, scale, share = refs
    assemble_galerkin(level_idx, cols, blocks, local, rim, scale)
    assemble_share(level_idx, rcols, rblocks, share)


def raising(level_idx, pcols, blocks, local, scale, held):
    assemble_prolong(level_idx, pcols, blocks, held)
    applied = matmul(local[...], held[...])
    return (held[...].astype(f32) - (relax_up * scale[...]) * applied).astype(bf16)


def coarse_operators_kernel(first, levels, *refs):
    _, one, two, pcols, inverse, *refs = refs
    places = range(first, levels)
    blocks, refs = refs[: len(places)], refs[len(places) :]
    pairs, refs = refs[: 2 * len(places)], refs[2 * len(places) :]
    pair, coarse, *up, held = refs
    width = one.shape[1]
    pair[:, :width] = one[...]
    pair[:, width:] = two[...]
    for idx in places:
        slot = idx - first
        made = raising(idx, pcols, blocks[slot], pairs[2 * slot + 1], pairs[2 * slot], held)
        if idx == levels - 1:
            coarse[...] = matmul(made, inverse[...]).astype(bf16)
        else:
            up[slot][...] = made


def fine_operators_kernel(
    places, _, pcols, blocks_0, blocks_1, scale_0, local_0, scale_1, local_1,
    base, bases, lower, both, total, held,
):
    lower[...] = raising(0, pcols, blocks_0, local_0, scale_0, held)
    upper = raising(1, pcols, blocks_1, local_1, scale_1, held)
    both[...] = matmul(lower[...], upper).astype(bf16)
    total_kernel(places, base, bases, lower, total)


def total_kernel(places, base, bases, lower, total):
    width = bases.shape[1] // len(places)
    for slot, place in enumerate(places):
        columns = pl.ds(slot * width, width)
        lanes = lanes_of(place, width)
        total[:, columns] = base[:, lanes] + matmul(lower[...], bases[:, columns])


def inverse_part(inverse, part, offset):
    depth = part.shape[0]
    piece = lax.axis_index("narrow") ^ offset
    return matmul(inverse[:, pl.ds(pl.multiple_of(piece * depth, depth), depth)], part[...])


def share_sum_kernel(far, own, *refs):
    refs[-1][...] = (far[...].astype(f32) + own[...].astype(f32)).astype(bf16)


def up_kernel(offsets, inverse, *refs):
    value = refs[len(offsets)][...]
    for part, offset in zip(refs, offsets):
        value = value + inverse_part(inverse, part, offset)
    refs, out = refs[len(offsets) + 1 : -1], refs[-1]
    for step in range(len(refs) // 2):
        value = refs[2 * step][...] + matmul(refs[2 * step + 1][...], value.astype(bf16))
    out[...] = value.astype(bf16)


def output_kernel(places, slots, *refs):
    coarse, totals = refs[: len(places)], refs[len(places) : 2 * len(places)]
    both, refs = refs[2 * len(places)], refs[2 * len(places) :]
    out, made, sems = refs[-3:]
    copies = []
    for item, (place, value) in enumerate(zip(places, coarse)):
        width = value.shape[1]
        held = totals[item][:, slots[item] * width : (slots[item] + 1) * width]
        made[item] = held + matmul(both[...], value[...])
        target = out.at[0, :, lanes_of(place, width)]
        copy = pltpu.make_async_copy(made.at[item], target, sems.at[item])
        copy.start()
        copies.append(copy)
    for copy in copies:
        copy.wait()


def exchange(value, axis, bit):
    count = lax.axis_size(axis)
    return lax.ppermute(value, axis, [(i, i ^ bit) for i in range(count)])


def exchange_both(value, bit, beside):
    wide, narrow = lax.axis_size("wide"), lax.axis_size("narrow")
    pairs = [
        (w * narrow + j, (w ^ bit) * narrow + beside(j)) for w in range(wide) for j in range(narrow)
    ]
    return lax.ppermute(value, ("wide", "narrow"), pairs)


def swap_ends(inner, outer, bit):
    count = lax.axis_size("narrow")
    outer = exchange_both(outer, bit, lambda j: (j + 1 if j % 2 else j - 1) % count)
    return exchange_both(inner, bit, lambda j: j ^ 1), outer


def swap_outer(outer):
    count = lax.axis_size("narrow")
    gaps = [(i, (i + 1 if i % 2 else i - 1) % count) for i in range(count)]
    return lax.ppermute(outer, "narrow", gaps)


def on_device(
    level_rhs,
    galerkin_cols,
    galerkin_blocks,
    restrict_cols,
    restrict_blocks,
    prolong_cols,
    prolong_blocks,
    coarse_inverse,
):
    levels = galerkin_cols.shape[0]
    count = galerkin_cols.shape[2]
    size = galerkin_blocks.shape[-1]
    rows, fields = level_rhs.shape[1:]
    half = fields // 2
    width = half // 2
    last = levels - 1
    pieces = lax.axis_size("narrow")
    pcols = prolong_cols.transpose(0, 1, 3, 2), scalars()
    rtable = restrict_cols.transpose(0, 3, 1, 2)
    square_shape = array((rows, rows), bf16)
    scale_shape = array((rows, 1), f32)
    operator_shapes = [square_shape, array((rows, 2 * size), bf16), scale_shape]
    chunk_shape = array((rows, width), bf16)
    real_shape = array((rows, width), f32)
    held = [pltpu.VMEM((rows, rows), bf16)]

    def ends_shape(columns):
        return array((size, columns), bf16)

    def of_level(value, level_idx):
        return value, level_block(value, level_idx)

    def pivots_of(level_idx):
        shape = (1, 1, count, 1, size, size)
        return galerkin_blocks, pl.BlockSpec(shape, lambda i: (level_idx, 0, 0, 0, 0, 0))

    def flops(columns, products=1):
        return 2 * products * rows * rows * columns

    def place_of(far, given):
        return (0, far, half), (1, given, width)

    pairs = [(place_of(1, given), place_of(0, given)) for given in (1, 0)]
    first_restrict = (1,) + restrict_blocks.shape[1:]
    gcols, rcols, rfirst, pivots, inner, *outers = run(
        functools.partial(start_kernel, pairs), "start",
        [array(galerkin_cols.shape, jnp.int32), array(rtable.shape, jnp.int32),
         array(first_restrict, bf16), array((count, size, size), bf16), ends_shape(fields)]
        + [ends_shape(half)] * 2,
        [in_hbm(value) for value in
         (level_rhs, galerkin_blocks, galerkin_cols, rtable, restrict_blocks)],
        scratch=[
            pltpu.VMEM((2, size, fields), f32), pltpu.VMEM((size, fields), bf16),
            pltpu.VMEM((2, size, size), bf16), pltpu.SemaphoreType.DMA((7 + count,)),
        ],
    )
    gcols, rcols = ((in_vmem(value), scalars()) for value in (gcols, rcols))
    first = outers[0]
    outers = [swap_outer(outer) for outer in outers]
    inner = exchange(inner, "narrow", 1)
    rest, base, local, rim, scale, share, next_scale = run(
        first_local_kernel, "first_local",
        [array((rows, fields), f32)] * 2 + operator_shapes + [square_shape, scale_shape],
        [level_rhs, first, gcols, of_level(galerkin_blocks, 0), rcols, rfirst, pivots],
        flops=flops(fields),
    )
    operators = [(scale, local)]
    kept, joined = [], []
    for places, outer in zip(pairs, outers):
        columns = half if kept else width
        near, *joined = run(
            functools.partial(first_residual_kernel, places), "first_residual",
            [real_shape, array((rows, columns), bf16)] + [ends_shape(columns)] * 4,
            [rest, rim, outer, inner, share, next_scale, *joined],
            flops=flops(width, 3),
        )
        kept.append(near)
    sent, far_ends, near_ends = joined[0], joined[1:3], joined[3:]
    bases = []
    for level_idx in range(1, levels):
        bit = 1 << level_idx - 1
        far_ends = swap_ends(*far_ends, bit)
        other = exchange(sent, "wide", bit)
        near_ends = swap_ends(*near_ends, 0)
        shapes = operator_shapes + [square_shape]
        operands = [sent, gcols, of_level(galerkin_blocks, level_idx),
                    rcols, of_level(restrict_blocks, level_idx)]
        if level_idx < last:
            shapes = shapes + [scale_shape]
            operands.append(pivots_of(level_idx + 1))
        local, rim, scale, share, *next_scale = run(
            functools.partial(operators_kernel, level_idx), "operators", shapes, operands
        )
        operators.append((scale, local))
        for slot, mine in enumerate(kept):
            kinds = ["base", "sent", "kept", "ends"]
            if level_idx == 1:
                kinds = ["base", "kept", "ends"] if slot else ["base", "sent", "ends"]
            elif level_idx == last:
                kinds = ["base", "sent"]
            shapes = [real_shape]
            operands = [mine, other, scale, local, rim, *far_ends, *near_ends, share, *next_scale]
            if level_idx == 1:
                shapes = [chunk_shape]
            if "sent" in kinds:
                shapes.append(chunk_shape)
            if "kept" in kinds:
                shapes.append(real_shape)
            if "ends" in kinds:
                shapes += [ends_shape(width)] * 2
            made_base, *made = run(
                functools.partial(level_kernel, slot, kinds), "level", shapes, operands,
                flops=flops(width, 3),
            )
            bases.append(made_base)
            if "sent" in kinds:
                next_sent = made.pop(0)
            if "kept" in kinds:
                own = [made.pop(0)]
            if "ends" in kinds:
                if "sent" in kinds:
                    sent_ends = made
                kept_ends = made
        sent = next_sent
        if level_idx < last:
            kept, far_ends, near_ends = own, sent_ends, kept_ends
    mine = sent
    far_parts = {
        o: exchange_both(mine, 1 << last, functools.partial(lambda o, j: j ^ o, o))
        for o in range(0, pieces, 2)
    }
    own_parts = {o: exchange(mine, "narrow", o) if o else mine for o in range(0, pieces, 2)}
    near_bases, coarse_mat, *ups = run(
        functools.partial(coarse_operators_kernel, 2, levels), "coarse_operators",
        [array((rows, half), bf16), array((rows, pieces * rows), bf16)]
        + [square_shape] * (levels - 3),
        [mine, *bases[:2], pcols, coarse_inverse]
        + [of_level(prolong_blocks, idx) for idx in range(2, levels)]
        + [value for pair in operators[2:] for value in pair],
        flops=flops(rows, 2 * (levels - 2) + pieces), scratch=held,
    )
    near_places, far_places = ([place_of(far, given) for given in (1, 0)] for far in (0, 1))
    total_shape = array((rows, half), f32)
    lower, both, near_total = run(
        functools.partial(fine_operators_kernel, near_places), "fine_operators",
        [square_shape] * 2 + [total_shape],
        [mine, pcols, of_level(prolong_blocks, 0), of_level(prolong_blocks, 1),
         *operators[0], *operators[1], base, near_bases],
        flops=flops(rows, 4), scratch=held,
    )
    far_bases = exchange(near_bases, "wide", 1)
    (far_total,) = run(
        functools.partial(total_kernel, far_places), "far_total", [total_shape],
        [base, far_bases, lower], flops=flops(half),
    )
    parts = {}
    for offset in range(0, pieces, 2):
        (parts[offset],) = run(
            share_sum_kernel, "share_sum", [chunk_shape],
            [far_parts[offset], own_parts[offset], coarse_mat, both],
        )
        parts[offset + 1] = exchange(parts[offset], "narrow", 1)
    offsets = tuple(parts)
    operands = [coarse_mat] + [parts[o] for o in offsets] + [bases[-1]]
    for idx in reversed(range(2, last)):
        operands += [bases[idx], ups[idx - 2]]
    (coarse,) = run(
        functools.partial(up_kernel, offsets), "up", [chunk_shape], operands,
        flops=flops(width, len(offsets) + levels - 3),
    )
    diagonal, far, other = (exchange(coarse, "wide", bits) for bits in (3, 1, 2))
    result = None
    for group in (
        [(coarse, near_total, place_of(0, 0), 1)],
        [(diagonal, far_total, place_of(1, 1), 0)],
        [(far, far_total, place_of(1, 0), 1), (other, near_total, place_of(0, 1), 0)],
    ):
        values, totals, places, slots = zip(*group)
        operands = [*values, *totals, both]
        aliases = {}
        if result is not None:
            aliases[len(operands)] = 0
            operands.append(in_hbm(result))
        (result,) = run(
            functools.partial(output_kernel, places, slots), "output",
            [array((1, rows, fields), f32)], operands,
            flops=flops(width, len(group)), out_space=pltpu.HBM, aliases=aliases,
            scratch=[
                pltpu.VMEM((len(group), rows, width), f32), pltpu.SemaphoreType.DMA((len(group),))
            ],
        )
    return result


def solution(mesh):
    in_specs = (
        P("wide", "narrow", None),
        P(None, "wide", "narrow", None),
        P(None, "wide", "narrow", None, None, None),
        P(None, "wide", "narrow", None),
        P(None, "wide", "narrow", None, None, None),
        P(None, "wide", "narrow", None),
        P(None, "wide", "narrow", None, None, None),
        P("narrow", None),
    )
    out_specs = P("wide", "narrow", None)
    return jax.shard_map(
        on_device, mesh=mesh, in_specs=in_specs, out_specs=out_specs, check_vma=False
    )
```

```python
import functools

import jax
import jax.numpy as jnp
from jax import lax
from jax.experimental import pallas as pl
from jax.experimental.pallas import tpu as pltpu
from jax.sharding import PartitionSpec as P

relax_down = 0.7
relax_up = 0.5
f32 = jnp.float32
bf16 = jnp.bfloat16
grant = 12 * 1024 * 1024
late_cost = 4 * 10**9


def matmul(a, b):
    return jnp.dot(a, b, preferred_element_type=f32)


def array(shape, dtype):
    return jax.ShapeDtypeStruct(shape, dtype)


def whole():
    return pl.BlockSpec(memory_space=pltpu.VMEM)


def level_block(value, level_idx):
    shape = (1,) + value.shape[1:]
    return pl.BlockSpec(shape, lambda i: (level_idx,) + (0,) * (value.ndim - 1))


def scalars():
    return pl.BlockSpec(memory_space=pltpu.SMEM)


def in_hbm(value):
    return pltpu.with_memory_space_constraint(value, pltpu.HBM), pl.BlockSpec(memory_space=pltpu.HBM)


def in_vmem(value):
    return pltpu.with_memory_space_constraint(value, pltpu.VMEM)


def run(body, name, outs, operands, flops=0, scratch=(), out_space=pltpu.VMEM, aliases=None):
    arrays = [o[0] if isinstance(o, tuple) else in_vmem(o) for o in operands]
    specs = [o[1] if isinstance(o, tuple) else whole() for o in operands]
    windows = any(isinstance(o, tuple) and o[1].block_shape is not None for o in operands)
    moved = sum(a.size * a.dtype.itemsize for a in arrays)
    return pl.pallas_call(
        body,
        grid=(1,) if windows else (),
        out_shape=[out_space(o.shape, o.dtype) for o in outs],
        in_specs=specs,
        out_specs=[pl.BlockSpec(memory_space=out_space)] * len(outs),
        input_output_aliases=aliases or {},
        scratch_shapes=list(scratch),
        compiler_params=pltpu.CompilerParams(vmem_limit_bytes=grant),
        cost_estimate=pl.CostEstimate(flops=flops, bytes_accessed=moved, transcendentals=0),
        name=name,
    )(*arrays)


def diagonal_of(block):
    size = block.shape[0]
    rows = lax.broadcasted_iota(jnp.int32, (size, size), 0)
    lanes = lax.broadcasted_iota(jnp.int32, (size, size), 1)
    return jnp.sum(jnp.where(rows == lanes, block, 0.0), axis=1, keepdims=True)


def placed(base, others, ids, target):
    total = base
    for block, ident in zip(others, ids):
        term = block * jnp.where(ident == target, 1.0, 0.0).astype(f32)
        total = term if total is None else total + term
    return total


def parity_of():
    return lax.rem(lax.axis_index("narrow"), 2)


def put_ends(first, last, inner_ref, outer_ref):
    even = parity_of() == 0
    inner_ref[...] = jnp.where(even, last, first)
    outer_ref[...] = jnp.where(even, first, last)


def assemble_galerkin(level_idx, cols, blocks, local_ref, rim_ref, scale_ref):
    count, slots, size = blocks.shape[2], blocks.shape[3], blocks.shape[4]
    parity = parity_of()
    piece = lax.axis_index("narrow")
    last = lax.axis_size("narrow") - 1
    inside = jnp.where((piece == 0) | (piece == last), 0.0, 1.0).astype(f32)
    for b in range(count):
        held = [blocks[0, 0, b, s].astype(f32) for s in range(slots)]
        ids = [cols[level_idx, 0, b, s] for s in range(1, slots)]
        rows = pl.ds(b * size, size)
        scale_ref[rows, :] = 1.0 / diagonal_of(held[0])
        line = [placed(held[0] if c == b else None, held[1:], ids, c) for c in range(count)]
        local_ref[rows, :] = jnp.concatenate(line, axis=1).astype(bf16)
        rims = [
            placed(None, held[1:], ids, count + 1 - parity),
            placed(None, held[1:], ids, count + parity) * inside,
        ]
        rim_ref[rows, :] = jnp.concatenate(rims, axis=1).astype(bf16)


def assemble_restrict(level_idx, cols, blocks, out_ref):
    count, slots, size = blocks.shape[2], blocks.shape[3], blocks.shape[4]
    for b in range(count):
        held = [blocks[0, 0, b, s].astype(f32) for s in range(slots)]
        ids = [cols[level_idx, s, 0, b] for s in range(2, slots)]
        fixed = {b: held[0], count + b: held[1]}
        line = [placed(fixed.get(c), held[2:], ids, c) for c in range(2 * count)]
        out_ref[pl.ds(b * size, size), :] = jnp.concatenate(line, axis=1).astype(bf16)


def assemble_share(level_idx, cols, blocks, out_ref):
    count, slots, size = blocks.shape[2], blocks.shape[3], blocks.shape[4]
    bit = bit_of(level_idx)
    for b in range(count):
        held = [blocks[0, 0, b, s].astype(f32) for s in range(slots)]
        ids = [cols[level_idx, s, 0, b] for s in range(2, slots)]
        own = jnp.where(bit == 0, held[0], held[1])
        first = bit * count
        line = [placed(own if c == b else None, held[2:], ids, first + c) for c in range(count)]
        out_ref[pl.ds(b * size, size), :] = jnp.concatenate(line, axis=1).astype(bf16)


def assemble_prolong(level_idx, cols, blocks, out_ref):
    count, slots, size = blocks.shape[2], blocks.shape[3], blocks.shape[4]
    for b in range(count):
        held = [blocks[0, 0, b, s].astype(f32) for s in range(slots)]
        ids = [cols[level_idx, 0, s, b] for s in range(1, slots)]
        line = [placed(held[0] if c == b else None, held[1:], ids, c) for c in range(count)]
        out_ref[pl.ds(b * size, size), :] = jnp.concatenate(line, axis=1).astype(bf16)


def start_kernel(places, rhs, blocks, *refs):
    table, held, inner_ref, *outers, rows, outer, pivots, sems = refs
    count, size = blocks.shape[2], blocks.shape[4]
    copies = []
    for slot, which in enumerate((0, count - 1)):
        source = rhs.at[0, pl.ds(which * size, size), :]
        copies.append(pltpu.make_async_copy(source, rows.at[slot], sems.at[slot]))
        source = blocks.at[0, 0, which, 0]
        copies.append(pltpu.make_async_copy(source, pivots.at[slot], sems.at[2 + slot]))
    copies.append(pltpu.make_async_copy(table, held, sems.at[4]))
    for copy in copies:
        copy.start()
    for copy in copies:
        copy.wait()
    first, last = (
        (rows[slot] * (relax_down / diagonal_of(pivots[slot].astype(f32)))).astype(bf16)
        for slot in range(2)
    )
    put_ends(first, last, inner_ref, outer)
    for ref, pair in zip(outers, places):
        width = ref.shape[1] // 2
        for slot, place in enumerate(pair):
            ref[:, slot * width : (slot + 1) * width] = outer[:, lanes_of(place, width)]


def first_local_kernel(rhs, _, cols, blocks, rest, base, local, rim, scale):
    assemble_galerkin(0, cols, blocks, local, rim, scale)
    smoothed = rhs[0] * (relax_down * scale[...])
    left = rhs[0] - matmul(local[...], smoothed.astype(bf16))
    rest[...] = left
    base[...] = smoothed + (relax_up * scale[...]) * left


def bit_of(level_idx):
    return lax.axis_index("wide") >> level_idx & 1


def lanes_of(place, width):
    start = 0
    for level_idx, flip, step in place:
        start = start + (bit_of(level_idx) ^ flip) * step
    return pl.ds(pl.multiple_of(start, width), width)


def first_residual_kernel(places, rest, rim, outer, inner, *refs):
    width = refs[0].shape[1]
    for slot, (ref, place) in enumerate(zip(refs, places)):
        lanes = lanes_of(place, width)
        columns = pl.ds(slot * width, width)
        rims = jnp.concatenate([inner[:, lanes], outer[:, columns]], axis=0)
        ref[...] = (rest[:, lanes] - matmul(rim[...], rims)).astype(bf16)


def residual_kernel(rhs, smoothed, scale, local, rim, outer, inner, _, out, base):
    rims = jnp.concatenate([inner[...], outer[...]], axis=0)
    left = rhs[...] - matmul(local[...], smoothed[...])
    out[...] = (left - matmul(rim[...], rims)).astype(bf16)
    made = rhs[...] * (relax_down * scale[...]) + (relax_up * scale[...]) * left
    base[...] = made.astype(base.dtype)


def last_residual_kernel(rhs, smoothed, scale, local, rim, outer, inner, share, out, base):
    rims = jnp.concatenate([inner[...], outer[...]], axis=0)
    left = rhs[...] - matmul(local[...], smoothed[...])
    residual = (left - matmul(rim[...], rims)).astype(bf16)
    out[...] = matmul(share[...], residual).astype(bf16)
    base[...] = rhs[...] * (relax_down * scale[...]) + (relax_up * scale[...]) * left


def operators_kernel(level_idx, _, rcols, rblocks, cols, blocks, *refs):
    if len(refs) > 4:
        last_blocks, *refs = refs
        assemble_share(level_idx + 1, rcols, last_blocks, refs.pop())
    rmat, local, rim, scale = refs
    assemble_restrict(level_idx, rcols, rblocks, rmat)
    assemble_galerkin(level_idx + 1, cols, blocks, local, rim, scale)


def raising(level_idx, pcols, blocks, local, scale, held):
    assemble_prolong(level_idx, pcols, blocks, held)
    applied = matmul(local[...], held[...])
    return (held[...].astype(f32) - (relax_up * scale[...]) * applied).astype(bf16)


def coarse_operators_kernel(first, levels, *refs):
    _, _, pcols, inverse, *refs = refs
    places = range(first, levels)
    blocks, refs = refs[: len(places)], refs[len(places) :]
    pairs, refs = refs[: 2 * len(places)], refs[2 * len(places) :]
    coarse, *up, held = refs
    for idx in places:
        slot = idx - first
        made = raising(idx, pcols, blocks[slot], pairs[2 * slot + 1], pairs[2 * slot], held)
        if idx == levels - 1:
            coarse[...] = matmul(made, inverse[...]).astype(bf16)
        else:
            up[slot][...] = made


def fine_operators_kernel(
    places, _, pcols, blocks_0, blocks_1, scale_0, local_0, scale_1, local_1,
    base, near, far, lower, upper, both, total, held,
):
    lower[...] = raising(0, pcols, blocks_0, local_0, scale_0, held)
    upper[...] = raising(1, pcols, blocks_1, local_1, scale_1, held)
    both[...] = matmul(lower[...], upper[...]).astype(bf16)
    width = near.shape[1]
    for slot, (place, source) in enumerate(zip(places, (near, far))):
        made = base[:, lanes_of(place, width)] + matmul(lower[...], source[...])
        total[:, slot * width : (slot + 1) * width] = made


def restricted(level_idx, rmat, kept, other):
    width = rmat.shape[1] // 2
    own = pl.multiple_of(bit_of(level_idx) * width, width)
    far = pl.multiple_of((1 - bit_of(level_idx)) * width, width)
    total = matmul(rmat[:, pl.ds(own, width)], kept[...])
    return total + matmul(rmat[:, pl.ds(far, width)], other[...])


def join_kernel(level_idx, rmat, kept, other, scale, rhs, smoothed, inner_ref, outer_ref):
    size = inner_ref.shape[0]
    current = restricted(level_idx, rmat, kept, other)
    rhs[...] = current
    rounded = (current * (relax_down * scale[...])).astype(bf16)
    smoothed[...] = rounded
    put_ends(rounded[:size], rounded[-size:], inner_ref, outer_ref)


def inverse_part(inverse, part, offset):
    depth = part.shape[0]
    piece = lax.axis_index("narrow") ^ offset
    return matmul(inverse[:, pl.ds(pl.multiple_of(piece * depth, depth), depth)], part[...])


def share_sum_kernel(far, own, *refs):
    refs[-1][...] = (far[...].astype(f32) + own[...].astype(f32)).astype(bf16)


def coarse_kernel(offsets, inverse, *refs):
    *parts, value, out = refs
    value = value[...]
    for part, offset in zip(parts, offsets):
        value = value + inverse_part(inverse, part, offset)
    out[...] = value


def up_kernel(offsets, inverse, *refs):
    value = refs[len(offsets)][...]
    for part, offset in zip(refs, offsets):
        value = value + inverse_part(inverse, part, offset)
    refs = refs[len(offsets) + 1 :]
    refs, (base, up, coarse, raised) = refs[:-4], refs[-4:]
    for step in range(len(refs) // 2):
        value = refs[2 * step][...] + matmul(refs[2 * step + 1][...], value.astype(bf16))
    value = value.astype(bf16)
    coarse[...] = value
    raised[...] = (base[...] + matmul(up[...], value)).astype(bf16)


def output_kernel(places, slots, *refs):
    coarse, (base, lower, total, both) = refs[: len(places)], refs[len(places) : len(places) + 4]
    out, made, sems = refs[-3:]
    copies = []
    for item, (place, value) in enumerate(zip(places, coarse)):
        width = value.shape[1]
        lanes = lanes_of(place, width)
        if slots[item] is None:
            made[item] = base[:, lanes] + matmul(lower[...], value[...])
        else:
            held = total[:, slots[item] * width : (slots[item] + 1) * width]
            made[item] = held + matmul(both[...], value[...])
        copy = pltpu.make_async_copy(made.at[item], out.at[0, :, lanes], sems.at[item])
        copy.start()
        copies.append(copy)
    for copy in copies:
        copy.wait()


def exchange(value, axis, bit):
    count = lax.axis_size(axis)
    return lax.ppermute(value, axis, [(i, i ^ bit) for i in range(count)])


def exchange_both(value, bit, offset):
    wide, narrow = lax.axis_size("wide"), lax.axis_size("narrow")
    pairs = [
        (w * narrow + j, (w ^ bit) * narrow + (j ^ offset))
        for w in range(wide) for j in range(narrow)
    ]
    return lax.ppermute(value, ("wide", "narrow"), pairs)


def swap_outer(outer):
    count = lax.axis_size("narrow")
    gaps = [(i, (i + 1 if i % 2 else i - 1) % count) for i in range(count)]
    return lax.ppermute(outer, "narrow", gaps)


def on_device(
    level_rhs,
    galerkin_cols,
    galerkin_blocks,
    restrict_cols,
    restrict_blocks,
    prolong_cols,
    prolong_blocks,
    coarse_inverse,
):
    levels = galerkin_cols.shape[0]
    count = galerkin_cols.shape[2]
    size = galerkin_blocks.shape[-1]
    rows, fields = level_rhs.shape[1:]
    half = fields // 2
    width = half // 2
    rcols = restrict_cols.transpose(0, 3, 1, 2), scalars()
    pcols = prolong_cols.transpose(0, 1, 3, 2), scalars()
    square_shape = array((rows, rows), bf16)
    operator_shapes = [square_shape, array((rows, 2 * size), bf16), array((rows, 1), f32)]
    rmat_shape = array((rows, 2 * rows), bf16)
    chunk_shape = array((rows, width), bf16)
    real_shape = array((rows, width), f32)
    held = [pltpu.VMEM((rows, rows), bf16)]

    def ends_shape(columns):
        return array((size, columns), bf16)

    def of_level(value, level_idx):
        return value, level_block(value, level_idx)

    def flops(columns, products=1):
        return 2 * products * rows * rows * columns

    def place_of(far, given):
        return (0, far, half), (1, given, width)

    pairs = [(place_of(1, given), place_of(0, given)) for given in (1, 0)]
    gcols, inner, *outers = run(
        functools.partial(start_kernel, pairs), "start",
        [array(galerkin_cols.shape, jnp.int32), ends_shape(fields)] + [ends_shape(half)] * 2,
        [in_hbm(level_rhs), in_hbm(galerkin_blocks), in_hbm(galerkin_cols)],
        scratch=[
            pltpu.VMEM((2, size, fields), f32), pltpu.VMEM((size, fields), bf16),
            pltpu.VMEM((2, size, size), bf16), pltpu.SemaphoreType.DMA((5,)),
        ],
    )
    gcols = in_vmem(gcols), scalars()
    first = outers[0]
    outers = [swap_outer(outer) for outer in outers]
    inner = exchange(inner, "narrow", 1)
    rest, base, local, rim, scale = run(
        first_local_kernel, "first_local", [array((rows, fields), f32)] * 2 + operator_shapes,
        [level_rhs, first, gcols, of_level(galerkin_blocks, 0)], flops=flops(fields),
    )
    operators = [(scale, local)]
    sent, kept = [], []
    for places, outer in zip(pairs, outers):
        far, near = run(
            functools.partial(first_residual_kernel, places), "first_residual", [chunk_shape] * 2,
            [rest, rim, outer, inner],
        )
        sent.append(far)
        kept.append(near)
    last = levels - 1
    bases = []
    anchor = sent[0]
    pieces = lax.axis_size("narrow")
    for level_idx in range(levels - 1):
        other = [exchange(value, "wide", 1 << level_idx) for value in sent]
        shapes = [rmat_shape] + operator_shapes
        operands = [anchor, rcols, of_level(restrict_blocks, level_idx),
                    gcols, of_level(galerkin_blocks, level_idx + 1)]
        if level_idx + 1 == last:
            shapes.append(square_shape)
            operands.append(of_level(restrict_blocks, last))
        rmat, local, rim, scale, *share = run(
            functools.partial(operators_kernel, level_idx), "operators", shapes, operands
        )
        operators.append((scale, local))
        joined = []
        for near, far in zip(kept, other):
            rhs, smoothed, *ends = run(
                functools.partial(join_kernel, level_idx), "join",
                [real_shape, chunk_shape] + [ends_shape(width)] * 2,
                [rmat, near, far, scale], flops=flops(width, 2),
            )
            inner, outer = exchange(ends[0], "narrow", 1), swap_outer(ends[1])
            joined.append((rhs, smoothed, scale, local, rim, outer, inner))
        made = []
        for operands in joined:
            value, made_base = run(
                last_residual_kernel if share else residual_kernel, "residual",
                [chunk_shape, real_shape if made or level_idx else chunk_shape],
                [*operands, *(share or [joined[-1][1]])],
                flops=flops(width, 2) if not made else late_cost,
            )
            made.append(value)
            bases.append(made_base)
        sent, kept = made[:1], made[-1:]
        anchor = made[0]
    (mine,) = kept
    far_parts = {o: exchange_both(mine, 1 << last, o) for o in range(0, pieces, 2)}
    far_base = exchange(bases[0], "wide", 1)
    own_parts = {o: exchange(mine, "narrow", o) if o else mine for o in range(0, pieces, 2)}
    coarse_mat, *ups = run(
        functools.partial(coarse_operators_kernel, 2, levels), "coarse_operators",
        [array((rows, pieces * rows), bf16)] + [square_shape] * (levels - 3),
        [mine, far_base, pcols, coarse_inverse]
        + [of_level(prolong_blocks, idx) for idx in range(2, levels)]
        + [value for pair in operators[2:] for value in pair],
        flops=flops(rows, 2 * (levels - 2) + pieces), scratch=held,
    )
    places = [place_of(0, 1), place_of(1, 1)]
    lower, upper, both, total = run(
        functools.partial(fine_operators_kernel, places), "fine_operators",
        [square_shape] * 3 + [array((rows, half), f32)],
        [mine, pcols, of_level(prolong_blocks, 0), of_level(prolong_blocks, 1),
         *operators[0], *operators[1], base, bases[0], far_base],
        flops=flops(rows, 4), scratch=held,
    )
    parts = {}
    for offset in reversed(range(0, pieces, 2)):
        (parts[offset],) = run(
            share_sum_kernel, "share_sum", [chunk_shape],
            [far_parts[offset], own_parts[offset], coarse_mat, upper],
        )
    offsets = tuple(parts)
    (value,) = run(
        functools.partial(coarse_kernel, offsets), "coarse", [real_shape],
        [coarse_mat] + [parts[o] for o in offsets] + [bases[-1]], flops=flops(width, len(offsets)),
    )
    parts = {o + 1: exchange(parts[o], "narrow", 1) for o in reversed(offsets)}
    offsets = tuple(parts)
    operands = [coarse_mat] + [parts[o] for o in offsets] + [value]
    for idx in reversed(range(2, last)):
        operands += [bases[idx], ups[idx - 2]]
    value, near = run(
        functools.partial(up_kernel, offsets), "up", [chunk_shape] * 2,
        operands + [bases[1], upper], flops=flops(width, len(offsets) + levels - 2),
    )
    diagonal, other = (exchange(value, "wide", bits) for bits in (3, 2))
    far = exchange(near, "wide", 1)
    result = None
    for group in (
        [(near, place_of(0, 0), None)],
        [(diagonal, place_of(1, 1), 1)],
        [(far, place_of(1, 0), None), (other, place_of(0, 1), 0)],
    ):
        values, places, slots = zip(*group)
        operands = [*values, base, lower, total, both]
        aliases = {}
        if result is not None:
            aliases[len(operands)] = 0
            operands.append(in_hbm(result))
        (result,) = run(
            functools.partial(output_kernel, places, slots),
            "output", [array((1, rows, fields), f32)], operands,
            flops=flops(width, len(group)), out_space=pltpu.HBM, aliases=aliases,
            scratch=[
                pltpu.VMEM((len(group), rows, width), f32), pltpu.SemaphoreType.DMA((len(group),))
            ],
        )
    return result


def solution(mesh):
    in_specs = (
        P("wide", "narrow", None),
        P(None, "wide", "narrow", None),
        P(None, "wide", "narrow", None, None, None),
        P(None, "wide", "narrow", None),
        P(None, "wide", "narrow", None, None, None),
        P(None, "wide", "narrow", None),
        P(None, "wide", "narrow", None, None, None),
        P("narrow", None),
    )
    out_specs = P("wide", "narrow", None)
    return jax.shard_map(
        on_device, mesh=mesh, in_specs=in_specs, out_specs=out_specs, check_vma=False
    )
```

```python
import functools

import jax
import jax.numpy as jnp
from jax import lax
from jax.experimental import pallas as pl
from jax.experimental.pallas import tpu as pltpu
from jax.sharding import PartitionSpec as P

relax_down = 0.7
relax_up = 0.5
f32 = jnp.float32
bf16 = jnp.bfloat16
grant = 12 * 1024 * 1024
late_cost = 4 * 10**9


def matmul(a, b):
    return jnp.dot(a, b, preferred_element_type=f32)


def array(shape, dtype):
    return jax.ShapeDtypeStruct(shape, dtype)


def whole():
    return pl.BlockSpec(memory_space=pltpu.VMEM)


def level_block(value, level_idx):
    shape = (1,) + value.shape[1:]
    return pl.BlockSpec(shape, lambda i: (level_idx,) + (0,) * (value.ndim - 1))


def scalars():
    return pl.BlockSpec(memory_space=pltpu.SMEM)


def in_hbm(value):
    return pltpu.with_memory_space_constraint(value, pltpu.HBM), pl.BlockSpec(memory_space=pltpu.HBM)


def in_vmem(value):
    return pltpu.with_memory_space_constraint(value, pltpu.VMEM)


def run(body, name, outs, operands, flops=0, scratch=(), out_space=pltpu.VMEM, aliases=None):
    arrays = [o[0] if isinstance(o, tuple) else in_vmem(o) for o in operands]
    specs = [o[1] if isinstance(o, tuple) else whole() for o in operands]
    windows = any(isinstance(o, tuple) and o[1].block_shape is not None for o in operands)
    moved = sum(a.size * a.dtype.itemsize for a in arrays)
    return pl.pallas_call(
        body,
        grid=(1,) if windows else (),
        out_shape=[out_space(o.shape, o.dtype) for o in outs],
        in_specs=specs,
        out_specs=[pl.BlockSpec(memory_space=out_space)] * len(outs),
        input_output_aliases=aliases or {},
        scratch_shapes=list(scratch),
        compiler_params=pltpu.CompilerParams(vmem_limit_bytes=grant),
        cost_estimate=pl.CostEstimate(flops=flops, bytes_accessed=moved, transcendentals=0),
        name=name,
    )(*arrays)


def diagonal_of(block):
    size = block.shape[0]
    rows = lax.broadcasted_iota(jnp.int32, (size, size), 0)
    lanes = lax.broadcasted_iota(jnp.int32, (size, size), 1)
    return jnp.sum(jnp.where(rows == lanes, block, 0.0), axis=1, keepdims=True)


def placed(base, others, ids, target):
    total = base
    for block, ident in zip(others, ids):
        term = block * jnp.where(ident == target, 1.0, 0.0).astype(f32)
        total = term if total is None else total + term
    return total


def parity_of():
    return lax.rem(lax.axis_index("narrow"), 2)


def put_ends(first, last, inner_ref, outer_ref):
    even = parity_of() == 0
    inner_ref[...] = jnp.where(even, last, first)
    outer_ref[...] = jnp.where(even, first, last)


def assemble_galerkin(level_idx, cols, blocks, local_ref, rim_ref, scale_ref):
    count, slots, size = blocks.shape[2], blocks.shape[3], blocks.shape[4]
    parity = parity_of()
    piece = lax.axis_index("narrow")
    last = lax.axis_size("narrow") - 1
    inside = jnp.where((piece == 0) | (piece == last), 0.0, 1.0).astype(f32)
    for b in range(count):
        held = [blocks[0, 0, b, s].astype(f32) for s in range(slots)]
        ids = [cols[level_idx, 0, b, s] for s in range(1, slots)]
        rows = pl.ds(b * size, size)
        scale_ref[rows, :] = 1.0 / diagonal_of(held[0])
        line = [placed(held[0] if c == b else None, held[1:], ids, c) for c in range(count)]
        local_ref[rows, :] = jnp.concatenate(line, axis=1).astype(bf16)
        rims = [
            placed(None, held[1:], ids, count + 1 - parity),
            placed(None, held[1:], ids, count + parity) * inside,
        ]
        rim_ref[rows, :] = jnp.concatenate(rims, axis=1).astype(bf16)


def assemble_restrict(level_idx, cols, blocks, out_ref):
    count, slots, size = blocks.shape[2], blocks.shape[3], blocks.shape[4]
    for b in range(count):
        held = [blocks[0, 0, b, s].astype(f32) for s in range(slots)]
        ids = [cols[level_idx, s, 0, b] for s in range(2, slots)]
        fixed = {b: held[0], count + b: held[1]}
        line = [placed(fixed.get(c), held[2:], ids, c) for c in range(2 * count)]
        out_ref[pl.ds(b * size, size), :] = jnp.concatenate(line, axis=1).astype(bf16)


def assemble_share(level_idx, cols, blocks, out_ref):
    count, slots, size = blocks.shape[2], blocks.shape[3], blocks.shape[4]
    bit = bit_of(level_idx)
    for b in range(count):
        held = [blocks[0, 0, b, s].astype(f32) for s in range(slots)]
        ids = [cols[level_idx, s, 0, b] for s in range(2, slots)]
        own = jnp.where(bit == 0, held[0], held[1])
        first = bit * count
        line = [placed(own if c == b else None, held[2:], ids, first + c) for c in range(count)]
        out_ref[pl.ds(b * size, size), :] = jnp.concatenate(line, axis=1).astype(bf16)


def assemble_prolong(level_idx, cols, blocks, out_ref):
    count, slots, size = blocks.shape[2], blocks.shape[3], blocks.shape[4]
    for b in range(count):
        held = [blocks[0, 0, b, s].astype(f32) for s in range(slots)]
        ids = [cols[level_idx, 0, s, b] for s in range(1, slots)]
        line = [placed(held[0] if c == b else None, held[1:], ids, c) for c in range(count)]
        out_ref[pl.ds(b * size, size), :] = jnp.concatenate(line, axis=1).astype(bf16)


def start_kernel(places, rhs, blocks, *refs):
    table, held, inner_ref, *outers, rows, outer, pivots, sems = refs
    count, size = blocks.shape[2], blocks.shape[4]
    copies = []
    for slot, which in enumerate((0, count - 1)):
        source = rhs.at[0, pl.ds(which * size, size), :]
        copies.append(pltpu.make_async_copy(source, rows.at[slot], sems.at[slot]))
        source = blocks.at[0, 0, which, 0]
        copies.append(pltpu.make_async_copy(source, pivots.at[slot], sems.at[2 + slot]))
    copies.append(pltpu.make_async_copy(table, held, sems.at[4]))
    for copy in copies:
        copy.start()
    for copy in copies:
        copy.wait()
    first, last = (
        (rows[slot] * (relax_down / diagonal_of(pivots[slot].astype(f32)))).astype(bf16)
        for slot in range(2)
    )
    put_ends(first, last, inner_ref, outer)
    for ref, pair in zip(outers, places):
        width = ref.shape[1] // 2
        for slot, place in enumerate(pair):
            ref[:, slot * width : (slot + 1) * width] = outer[:, lanes_of(place, width)]


def first_local_kernel(rhs, _, cols, blocks, rest, base, local, rim, scale):
    assemble_galerkin(0, cols, blocks, local, rim, scale)
    smoothed = rhs[0] * (relax_down * scale[...])
    left = rhs[0] - matmul(local[...], smoothed.astype(bf16))
    rest[...] = left
    base[...] = smoothed + (relax_up * scale[...]) * left


def bit_of(level_idx):
    return lax.axis_index("wide") >> level_idx & 1


def lanes_of(place, width):
    start = 0
    for level_idx, flip, step in place:
        start = start + (bit_of(level_idx) ^ flip) * step
    return pl.ds(pl.multiple_of(start, width), width)


def first_residual_kernel(places, rest, rim, outer, inner, *refs):
    width = refs[0].shape[1]
    for slot, (ref, place) in enumerate(zip(refs, places)):
        lanes = lanes_of(place, width)
        columns = pl.ds(slot * width, width)
        rims = jnp.concatenate([inner[:, lanes], outer[:, columns]], axis=0)
        ref[...] = (rest[:, lanes] - matmul(rim[...], rims)).astype(bf16)


def residual_kernel(rhs, smoothed, scale, local, rim, outer, inner, _, out, base):
    rims = jnp.concatenate([inner[...], outer[...]], axis=0)
    left = rhs[...] - matmul(local[...], smoothed[...])
    out[...] = (left - matmul(rim[...], rims)).astype(bf16)
    made = rhs[...] * (relax_down * scale[...]) + (relax_up * scale[...]) * left
    base[...] = made.astype(base.dtype)


def last_residual_kernel(rhs, smoothed, scale, local, rim, outer, inner, share, out, base):
    rims = jnp.concatenate([inner[...], outer[...]], axis=0)
    left = rhs[...] - matmul(local[...], smoothed[...])
    residual = (left - matmul(rim[...], rims)).astype(bf16)
    out[...] = matmul(share[...], residual).astype(bf16)
    base[...] = rhs[...] * (relax_down * scale[...]) + (relax_up * scale[...]) * left


def share_kernel(level_idx, _, rcols, rblocks, share):
    assemble_share(level_idx, rcols, rblocks, share)


def operators_kernel(level_idx, _, rcols, rblocks, cols, blocks, rmat, local, rim, scale):
    assemble_restrict(level_idx, rcols, rblocks, rmat)
    assemble_galerkin(level_idx + 1, cols, blocks, local, rim, scale)


def raising(level_idx, pcols, blocks, local, scale, held):
    assemble_prolong(level_idx, pcols, blocks, held)
    applied = matmul(local[...], held[...])
    return (held[...].astype(f32) - (relax_up * scale[...]) * applied).astype(bf16)


def coarse_operators_kernel(first, levels, *refs):
    _, _, pcols, inverse, *refs = refs
    places = range(first, levels)
    blocks, refs = refs[: len(places)], refs[len(places) :]
    pairs, refs = refs[: 2 * len(places)], refs[2 * len(places) :]
    coarse, *up, held = refs
    for idx in places:
        slot = idx - first
        made = raising(idx, pcols, blocks[slot], pairs[2 * slot + 1], pairs[2 * slot], held)
        if idx == levels - 1:
            coarse[...] = matmul(made, inverse[...]).astype(bf16)
        else:
            up[slot][...] = made


def fine_operators_kernel(
    places, _, pcols, blocks_0, blocks_1, scale_0, local_0, scale_1, local_1,
    base, near, far, lower, upper, both, total, held,
):
    lower[...] = raising(0, pcols, blocks_0, local_0, scale_0, held)
    upper[...] = raising(1, pcols, blocks_1, local_1, scale_1, held)
    both[...] = matmul(lower[...], upper[...]).astype(bf16)
    width = near.shape[1]
    for slot, (place, source) in enumerate(zip(places, (near, far))):
        made = base[:, lanes_of(place, width)] + matmul(lower[...], source[...])
        total[:, slot * width : (slot + 1) * width] = made


def restricted(level_idx, rmat, kept, other):
    width = rmat.shape[1] // 2
    own = pl.multiple_of(bit_of(level_idx) * width, width)
    far = pl.multiple_of((1 - bit_of(level_idx)) * width, width)
    total = matmul(rmat[:, pl.ds(own, width)], kept[...])
    return total + matmul(rmat[:, pl.ds(far, width)], other[...])


def join_kernel(level_idx, rmat, kept, other, scale, rhs, smoothed, inner_ref, outer_ref):
    size = inner_ref.shape[0]
    current = restricted(level_idx, rmat, kept, other)
    rhs[...] = current
    rounded = (current * (relax_down * scale[...])).astype(bf16)
    smoothed[...] = rounded
    put_ends(rounded[:size], rounded[-size:], inner_ref, outer_ref)


def inverse_part(inverse, part, offset):
    depth = part.shape[0]
    piece = lax.axis_index("narrow") ^ offset
    return matmul(inverse[:, pl.ds(pl.multiple_of(piece * depth, depth), depth)], part[...])


def share_sum_kernel(far, own, *refs):
    refs[-1][...] = (far[...].astype(f32) + own[...].astype(f32)).astype(bf16)


def coarse_kernel(offsets, inverse, *refs):
    *parts, value, out = refs
    value = value[...]
    for part, offset in zip(parts, offsets):
        value = value + inverse_part(inverse, part, offset)
    out[...] = value


def up_kernel(offsets, inverse, *refs):
    value = refs[len(offsets)][...]
    for part, offset in zip(refs, offsets):
        value = value + inverse_part(inverse, part, offset)
    refs = refs[len(offsets) + 1 :]
    refs, (base, up, coarse, raised) = refs[:-4], refs[-4:]
    for step in range(len(refs) // 2):
        value = refs[2 * step][...] + matmul(refs[2 * step + 1][...], value.astype(bf16))
    value = value.astype(bf16)
    coarse[...] = value
    raised[...] = (base[...] + matmul(up[...], value)).astype(bf16)


def output_kernel(places, slots, *refs):
    coarse, (base, lower, total, both) = refs[: len(places)], refs[len(places) : len(places) + 4]
    out, made, sems = refs[-3:]
    copies = []
    for item, (place, value) in enumerate(zip(places, coarse)):
        width = value.shape[1]
        lanes = lanes_of(place, width)
        if slots[item] is None:
            made[item] = base[:, lanes] + matmul(lower[...], value[...])
        else:
            held = total[:, slots[item] * width : (slots[item] + 1) * width]
            made[item] = held + matmul(both[...], value[...])
        copy = pltpu.make_async_copy(made.at[item], out.at[0, :, lanes], sems.at[item])
        copy.start()
        copies.append(copy)
    for copy in copies:
        copy.wait()


def exchange(value, axis, bit):
    count = lax.axis_size(axis)
    return lax.ppermute(value, axis, [(i, i ^ bit) for i in range(count)])


def exchange_both(value, bit, offset):
    wide, narrow = lax.axis_size("wide"), lax.axis_size("narrow")
    pairs = [
        (w * narrow + j, (w ^ bit) * narrow + (j ^ offset))
        for w in range(wide) for j in range(narrow)
    ]
    return lax.ppermute(value, ("wide", "narrow"), pairs)


def swap_outer(outer):
    count = lax.axis_size("narrow")
    gaps = [(i, (i + 1 if i % 2 else i - 1) % count) for i in range(count)]
    return lax.ppermute(outer, "narrow", gaps)


def on_device(
    level_rhs,
    galerkin_cols,
    galerkin_blocks,
    restrict_cols,
    restrict_blocks,
    prolong_cols,
    prolong_blocks,
    coarse_inverse,
):
    levels = galerkin_cols.shape[0]
    count = galerkin_cols.shape[2]
    size = galerkin_blocks.shape[-1]
    rows, fields = level_rhs.shape[1:]
    half = fields // 2
    width = half // 2
    rcols = restrict_cols.transpose(0, 3, 1, 2), scalars()
    pcols = prolong_cols.transpose(0, 1, 3, 2), scalars()
    square_shape = array((rows, rows), bf16)
    operator_shapes = [square_shape, array((rows, 2 * size), bf16), array((rows, 1), f32)]
    rmat_shape = array((rows, 2 * rows), bf16)
    chunk_shape = array((rows, width), bf16)
    real_shape = array((rows, width), f32)
    held = [pltpu.VMEM((rows, rows), bf16)]

    def ends_shape(columns):
        return array((size, columns), bf16)

    def of_level(value, level_idx):
        return value, level_block(value, level_idx)

    def flops(columns, products=1):
        return 2 * products * rows * rows * columns

    def place_of(far, given):
        return (0, far, half), (1, given, width)

    pairs = [(place_of(1, given), place_of(0, given)) for given in (1, 0)]
    gcols, inner, *outers = run(
        functools.partial(start_kernel, pairs), "start",
        [array(galerkin_cols.shape, jnp.int32), ends_shape(fields)] + [ends_shape(half)] * 2,
        [in_hbm(level_rhs), in_hbm(galerkin_blocks), in_hbm(galerkin_cols)],
        scratch=[
            pltpu.VMEM((2, size, fields), f32), pltpu.VMEM((size, fields), bf16),
            pltpu.VMEM((2, size, size), bf16), pltpu.SemaphoreType.DMA((5,)),
        ],
    )
    gcols = in_vmem(gcols), scalars()
    first = outers[0]
    outers = [swap_outer(outer) for outer in outers]
    inner = exchange(inner, "narrow", 1)
    rest, base, local, rim, scale = run(
        first_local_kernel, "first_local", [array((rows, fields), f32)] * 2 + operator_shapes,
        [level_rhs, first, gcols, of_level(galerkin_blocks, 0)], flops=flops(fields),
    )
    operators = [(scale, local)]
    sent, kept = [], []
    for places, outer in zip(pairs, outers):
        far, near = run(
            functools.partial(first_residual_kernel, places), "first_residual", [chunk_shape] * 2,
            [rest, rim, outer, inner],
        )
        sent.append(far)
        kept.append(near)
    last = levels - 1
    bases = []
    anchor = sent[0]
    pieces = lax.axis_size("narrow")
    for level_idx in range(levels - 1):
        other = [exchange(value, "wide", 1 << level_idx) for value in sent]
        rmat, local, rim, scale = run(
            functools.partial(operators_kernel, level_idx), "operators",
            [rmat_shape] + operator_shapes,
            [anchor, rcols, of_level(restrict_blocks, level_idx),
             gcols, of_level(galerkin_blocks, level_idx + 1)],
        )
        operators.append((scale, local))
        joined = []
        for near, far in zip(kept, other):
            rhs, smoothed, *ends = run(
                functools.partial(join_kernel, level_idx), "join",
                [real_shape, chunk_shape] + [ends_shape(width)] * 2,
                [rmat, near, far, scale], flops=flops(width, 2),
            )
            inner, outer = exchange(ends[0], "narrow", 1), swap_outer(ends[1])
            joined.append((rhs, smoothed, scale, local, rim, outer, inner))
        share = []
        if level_idx + 1 == last:
            share = run(
                functools.partial(share_kernel, last), "share", [square_shape],
                [joined[0][1], rcols, of_level(restrict_blocks, last)],
            )
        made = []
        for operands in joined:
            value, made_base = run(
                last_residual_kernel if share else residual_kernel, "residual",
                [chunk_shape, real_shape if made or level_idx else chunk_shape],
                [*operands, *(share or [joined[-1][1]])],
                flops=flops(width, 2) if not made else late_cost,
            )
            made.append(value)
            bases.append(made_base)
        sent, kept = made[:1], made[-1:]
        anchor = made[0]
    (mine,) = kept
    far_parts = {o: exchange_both(mine, 1 << last, o) for o in range(0, pieces, 2)}
    far_base = exchange(bases[0], "wide", 1)
    own_parts = {o: exchange(mine, "narrow", o) if o else mine for o in range(0, pieces, 2)}
    coarse_mat, *ups = run(
        functools.partial(coarse_operators_kernel, 2, levels), "coarse_operators",
        [array((rows, pieces * rows), bf16)] + [square_shape] * (levels - 3),
        [mine, far_base, pcols, coarse_inverse]
        + [of_level(prolong_blocks, idx) for idx in range(2, levels)]
        + [value for pair in operators[2:] for value in pair],
        flops=flops(rows, 2 * (levels - 2) + pieces), scratch=held,
    )
    places = [place_of(0, 1), place_of(1, 1)]
    lower, upper, both, total = run(
        functools.partial(fine_operators_kernel, places), "fine_operators",
        [square_shape] * 3 + [array((rows, half), f32)],
        [mine, pcols, of_level(prolong_blocks, 0), of_level(prolong_blocks, 1),
         *operators[0], *operators[1], base, bases[0], far_base],
        flops=flops(rows, 4), scratch=held,
    )
    parts = {}
    for offset in reversed(range(0, pieces, 2)):
        (parts[offset],) = run(
            share_sum_kernel, "share_sum", [chunk_shape],
            [far_parts[offset], own_parts[offset], coarse_mat, upper],
        )
    offsets = tuple(parts)
    (value,) = run(
        functools.partial(coarse_kernel, offsets), "coarse", [real_shape],
        [coarse_mat] + [parts[o] for o in offsets] + [bases[-1]], flops=flops(width, len(offsets)),
    )
    parts = {o + 1: exchange(parts[o], "narrow", 1) for o in reversed(offsets)}
    offsets = tuple(parts)
    operands = [coarse_mat] + [parts[o] for o in offsets] + [value]
    for idx in reversed(range(2, last)):
        operands += [bases[idx], ups[idx - 2]]
    value, near = run(
        functools.partial(up_kernel, offsets), "up", [chunk_shape] * 2,
        operands + [bases[1], upper], flops=flops(width, len(offsets) + levels - 2),
    )
    diagonal, other = (exchange(value, "wide", bits) for bits in (3, 2))
    far = exchange(near, "wide", 1)
    result = None
    for group in (
        [(near, place_of(0, 0), None)],
        [(diagonal, place_of(1, 1), 1)],
        [(far, place_of(1, 0), None), (other, place_of(0, 1), 0)],
    ):
        values, places, slots = zip(*group)
        operands = [*values, base, lower, total, both]
        aliases = {}
        if result is not None:
            aliases[len(operands)] = 0
            operands.append(in_hbm(result))
        (result,) = run(
            functools.partial(output_kernel, places, slots),
            "output", [array((1, rows, fields), f32)], operands,
            flops=flops(width, len(group)), out_space=pltpu.HBM, aliases=aliases,
            scratch=[
                pltpu.VMEM((len(group), rows, width), f32), pltpu.SemaphoreType.DMA((len(group),))
            ],
        )
    return result


def solution(mesh):
    in_specs = (
        P("wide", "narrow", None),
        P(None, "wide", "narrow", None),
        P(None, "wide", "narrow", None, None, None),
        P(None, "wide", "narrow", None),
        P(None, "wide", "narrow", None, None, None),
        P(None, "wide", "narrow", None),
        P(None, "wide", "narrow", None, None, None),
        P("narrow", None),
    )
    out_specs = P("wide", "narrow", None)
    return jax.shard_map(
        on_device, mesh=mesh, in_specs=in_specs, out_specs=out_specs, check_vma=False
    )
```

```python
import functools

import jax
import jax.numpy as jnp
from jax import lax
from jax.experimental import pallas as pl
from jax.experimental.pallas import tpu as pltpu
from jax.sharding import PartitionSpec as P

relax_down = 0.7
relax_up = 0.5
f32 = jnp.float32
bf16 = jnp.bfloat16
grant = 12 * 1024 * 1024
late_cost = 4 * 10**9


def matmul(a, b):
    return jnp.dot(a, b, preferred_element_type=f32)


def array(shape, dtype):
    return jax.ShapeDtypeStruct(shape, dtype)


def whole():
    return pl.BlockSpec(memory_space=pltpu.VMEM)


def level_block(value, level_idx):
    shape = (1,) + value.shape[1:]
    return pl.BlockSpec(shape, lambda i: (level_idx,) + (0,) * (value.ndim - 1))


def scalars():
    return pl.BlockSpec(memory_space=pltpu.SMEM)


def in_hbm(value):
    return pltpu.with_memory_space_constraint(value, pltpu.HBM), pl.BlockSpec(memory_space=pltpu.HBM)


def in_vmem(value):
    return pltpu.with_memory_space_constraint(value, pltpu.VMEM)


def run(body, name, outs, operands, flops=0, scratch=(), out_space=pltpu.VMEM, aliases=None):
    arrays = [o[0] if isinstance(o, tuple) else in_vmem(o) for o in operands]
    specs = [o[1] if isinstance(o, tuple) else whole() for o in operands]
    windows = any(isinstance(o, tuple) and o[1].block_shape is not None for o in operands)
    moved = sum(a.size * a.dtype.itemsize for a in arrays)
    return pl.pallas_call(
        body,
        grid=(1,) if windows else (),
        out_shape=[out_space(o.shape, o.dtype) for o in outs],
        in_specs=specs,
        out_specs=[pl.BlockSpec(memory_space=out_space)] * len(outs),
        input_output_aliases=aliases or {},
        scratch_shapes=list(scratch),
        compiler_params=pltpu.CompilerParams(vmem_limit_bytes=grant),
        cost_estimate=pl.CostEstimate(flops=flops, bytes_accessed=moved, transcendentals=0),
        name=name,
    )(*arrays)


def diagonal_of(block):
    size = block.shape[0]
    rows = lax.broadcasted_iota(jnp.int32, (size, size), 0)
    lanes = lax.broadcasted_iota(jnp.int32, (size, size), 1)
    return jnp.sum(jnp.where(rows == lanes, block, 0.0), axis=1, keepdims=True)


def placed(base, others, ids, target):
    total = base
    for block, ident in zip(others, ids):
        term = block * jnp.where(ident == target, 1.0, 0.0).astype(f32)
        total = term if total is None else total + term
    return total


def parity_of():
    return lax.rem(lax.axis_index("narrow"), 2)


def put_ends(first, last, inner_ref, outer_ref):
    even = parity_of() == 0
    inner_ref[...] = jnp.where(even, last, first)
    outer_ref[...] = jnp.where(even, first, last)


def assemble_galerkin(level_idx, cols, blocks, local_ref, rim_ref, scale_ref):
    count, slots, size = blocks.shape[2], blocks.shape[3], blocks.shape[4]
    parity = parity_of()
    piece = lax.axis_index("narrow")
    last = lax.axis_size("narrow") - 1
    inside = jnp.where((piece == 0) | (piece == last), 0.0, 1.0).astype(f32)
    for b in range(count):
        held = [blocks[0, 0, b, s].astype(f32) for s in range(slots)]
        ids = [cols[level_idx, 0, b, s] for s in range(1, slots)]
        rows = pl.ds(b * size, size)
        scale_ref[rows, :] = 1.0 / diagonal_of(held[0])
        line = [placed(held[0] if c == b else None, held[1:], ids, c) for c in range(count)]
        local_ref[rows, :] = jnp.concatenate(line, axis=1).astype(bf16)
        rims = [
            placed(None, held[1:], ids, count + 1 - parity),
            placed(None, held[1:], ids, count + parity) * inside,
        ]
        rim_ref[rows, :] = jnp.concatenate(rims, axis=1).astype(bf16)


def assemble_restrict(level_idx, cols, blocks, out_ref):
    count, slots, size = blocks.shape[2], blocks.shape[3], blocks.shape[4]
    for b in range(count):
        held = [blocks[0, 0, b, s].astype(f32) for s in range(slots)]
        ids = [cols[level_idx, s, 0, b] for s in range(2, slots)]
        fixed = {b: held[0], count + b: held[1]}
        line = [placed(fixed.get(c), held[2:], ids, c) for c in range(2 * count)]
        out_ref[pl.ds(b * size, size), :] = jnp.concatenate(line, axis=1).astype(bf16)


def assemble_share(level_idx, cols, blocks, out_ref):
    count, slots, size = blocks.shape[2], blocks.shape[3], blocks.shape[4]
    bit = bit_of(level_idx)
    for b in range(count):
        held = [blocks[0, 0, b, s].astype(f32) for s in range(slots)]
        ids = [cols[level_idx, s, 0, b] for s in range(2, slots)]
        own = jnp.where(bit == 0, held[0], held[1])
        first = bit * count
        line = [placed(own if c == b else None, held[2:], ids, first + c) for c in range(count)]
        out_ref[pl.ds(b * size, size), :] = jnp.concatenate(line, axis=1).astype(bf16)


def assemble_prolong(level_idx, cols, blocks, out_ref):
    count, slots, size = blocks.shape[2], blocks.shape[3], blocks.shape[4]
    for b in range(count):
        held = [blocks[0, 0, b, s].astype(f32) for s in range(slots)]
        ids = [cols[level_idx, 0, s, b] for s in range(1, slots)]
        line = [placed(held[0] if c == b else None, held[1:], ids, c) for c in range(count)]
        out_ref[pl.ds(b * size, size), :] = jnp.concatenate(line, axis=1).astype(bf16)


def start_kernel(places, rhs, blocks, *refs):
    table, held, inner_ref, *outers, rows, outer, pivots, sems = refs
    count, size = blocks.shape[2], blocks.shape[4]
    copies = []
    for slot, which in enumerate((0, count - 1)):
        source = rhs.at[0, pl.ds(which * size, size), :]
        copies.append(pltpu.make_async_copy(source, rows.at[slot], sems.at[slot]))
        source = blocks.at[0, 0, which, 0]
        copies.append(pltpu.make_async_copy(source, pivots.at[slot], sems.at[2 + slot]))
    copies.append(pltpu.make_async_copy(table, held, sems.at[4]))
    for copy in copies:
        copy.start()
    for copy in copies:
        copy.wait()
    first, last = (
        (rows[slot] * (relax_down / diagonal_of(pivots[slot].astype(f32)))).astype(bf16)
        for slot in range(2)
    )
    put_ends(first, last, inner_ref, outer)
    for ref, pair in zip(outers, places):
        width = ref.shape[1] // 2
        for slot, place in enumerate(pair):
            ref[:, slot * width : (slot + 1) * width] = outer[:, lanes_of(place, width)]


def first_local_kernel(rhs, _, cols, blocks, rest, base, local, rim, scale):
    assemble_galerkin(0, cols, blocks, local, rim, scale)
    smoothed = rhs[0] * (relax_down * scale[...])
    left = rhs[0] - matmul(local[...], smoothed.astype(bf16))
    rest[...] = left
    base[...] = smoothed + (relax_up * scale[...]) * left


def bit_of(level_idx):
    return lax.axis_index("wide") >> level_idx & 1


def lanes_of(place, width):
    start = 0
    for level_idx, flip, step in place:
        start = start + (bit_of(level_idx) ^ flip) * step
    return pl.ds(pl.multiple_of(start, width), width)


def first_residual_kernel(places, rest, rim, outer, inner, *refs):
    width = refs[0].shape[1]
    for slot, (ref, place) in enumerate(zip(refs, places)):
        lanes = lanes_of(place, width)
        columns = pl.ds(slot * width, width)
        rims = jnp.concatenate([inner[:, lanes], outer[:, columns]], axis=0)
        ref[...] = (rest[:, lanes] - matmul(rim[...], rims)).astype(bf16)


def residual_kernel(rhs, smoothed, scale, local, rim, outer, inner, _, out, base):
    rims = jnp.concatenate([inner[...], outer[...]], axis=0)
    left = rhs[...] - matmul(local[...], smoothed[...])
    out[...] = (left - matmul(rim[...], rims)).astype(bf16)
    made = rhs[...] * (relax_down * scale[...]) + (relax_up * scale[...]) * left
    base[...] = made.astype(base.dtype)


def last_residual_kernel(rhs, smoothed, scale, local, rim, outer, inner, share, out, base):
    rims = jnp.concatenate([inner[...], outer[...]], axis=0)
    left = rhs[...] - matmul(local[...], smoothed[...])
    residual = (left - matmul(rim[...], rims)).astype(bf16)
    out[...] = matmul(share[...], residual).astype(bf16)
    base[...] = rhs[...] * (relax_down * scale[...]) + (relax_up * scale[...]) * left


def share_kernel(level_idx, _, rcols, rblocks, share):
    assemble_share(level_idx, rcols, rblocks, share)


def operators_kernel(level_idx, _, rcols, rblocks, cols, blocks, rmat, local, rim, scale):
    assemble_restrict(level_idx, rcols, rblocks, rmat)
    assemble_galerkin(level_idx + 1, cols, blocks, local, rim, scale)


def raising(level_idx, pcols, blocks, local, scale, held):
    assemble_prolong(level_idx, pcols, blocks, held)
    applied = matmul(local[...], held[...])
    return (held[...].astype(f32) - (relax_up * scale[...]) * applied).astype(bf16)


def coarse_operators_kernel(first, levels, *refs):
    _, _, pcols, inverse, *refs = refs
    places = range(first, levels)
    blocks, refs = refs[: len(places)], refs[len(places) :]
    pairs, refs = refs[: 2 * len(places)], refs[2 * len(places) :]
    coarse, *up, held = refs
    for idx in places:
        slot = idx - first
        made = raising(idx, pcols, blocks[slot], pairs[2 * slot + 1], pairs[2 * slot], held)
        if idx == levels - 1:
            coarse[...] = matmul(made, inverse[...]).astype(bf16)
        else:
            up[slot][...] = made


def fine_operators_kernel(
    places, _, pcols, blocks_0, blocks_1, scale_0, local_0, scale_1, local_1,
    base, near, far, lower, upper, both, total, held,
):
    lower[...] = raising(0, pcols, blocks_0, local_0, scale_0, held)
    upper[...] = raising(1, pcols, blocks_1, local_1, scale_1, held)
    both[...] = matmul(lower[...], upper[...]).astype(bf16)
    width = near.shape[1]
    for slot, (place, source) in enumerate(zip(places, (near, far))):
        made = base[:, lanes_of(place, width)] + matmul(lower[...], source[...])
        total[:, slot * width : (slot + 1) * width] = made


def restricted(level_idx, rmat, kept, other):
    width = rmat.shape[1] // 2
    own = pl.multiple_of(bit_of(level_idx) * width, width)
    far = pl.multiple_of((1 - bit_of(level_idx)) * width, width)
    total = matmul(rmat[:, pl.ds(own, width)], kept[...])
    return total + matmul(rmat[:, pl.ds(far, width)], other[...])


def join_kernel(level_idx, rmat, kept, other, scale, rhs, smoothed, inner_ref, outer_ref):
    size = inner_ref.shape[0]
    current = restricted(level_idx, rmat, kept, other)
    rhs[...] = current
    rounded = (current * (relax_down * scale[...])).astype(bf16)
    smoothed[...] = rounded
    put_ends(rounded[:size], rounded[-size:], inner_ref, outer_ref)


def inverse_part(inverse, part, offset):
    depth = part.shape[0]
    piece = lax.axis_index("narrow") ^ offset
    return matmul(inverse[:, pl.ds(pl.multiple_of(piece * depth, depth), depth)], part[...])


def share_sum_kernel(far, own, *refs):
    refs[-1][...] = (far[...].astype(f32) + own[...].astype(f32)).astype(bf16)


def coarse_kernel(offsets, inverse, *refs):
    *parts, value, out = refs
    value = value[...]
    for part, offset in zip(parts, offsets):
        value = value + inverse_part(inverse, part, offset)
    out[...] = value


def up_kernel(offsets, inverse, *refs):
    value = refs[len(offsets)][...]
    for part, offset in zip(refs, offsets):
        value = value + inverse_part(inverse, part, offset)
    refs = refs[len(offsets) + 1 :]
    refs, (base, up, coarse, raised) = refs[:-4], refs[-4:]
    for step in range(len(refs) // 2):
        value = refs[2 * step][...] + matmul(refs[2 * step + 1][...], value.astype(bf16))
    value = value.astype(bf16)
    coarse[...] = value
    raised[...] = (base[...] + matmul(up[...], value)).astype(bf16)


def output_kernel(places, slots, *refs):
    coarse, (base, lower, total, both) = refs[: len(places)], refs[len(places) : len(places) + 4]
    out, made, sems = refs[-3:]
    copies = []
    for item, (place, value) in enumerate(zip(places, coarse)):
        width = value.shape[1]
        lanes = lanes_of(place, width)
        if slots[item] is None:
            made[item] = base[:, lanes] + matmul(lower[...], value[...])
        else:
            held = total[:, slots[item] * width : (slots[item] + 1) * width]
            made[item] = held + matmul(both[...], value[...])
        copy = pltpu.make_async_copy(made.at[item], out.at[0, :, lanes], sems.at[item])
        copy.start()
        copies.append(copy)
    for copy in copies:
        copy.wait()


def exchange(value, axis, bit):
    count = lax.axis_size(axis)
    return lax.ppermute(value, axis, [(i, i ^ bit) for i in range(count)])


def exchange_both(value, bit, offset):
    wide, narrow = lax.axis_size("wide"), lax.axis_size("narrow")
    pairs = [
        (w * narrow + j, (w ^ bit) * narrow + (j ^ offset))
        for w in range(wide) for j in range(narrow)
    ]
    return lax.ppermute(value, ("wide", "narrow"), pairs)


def swap_outer(outer):
    count = lax.axis_size("narrow")
    gaps = [(i, (i + 1 if i % 2 else i - 1) % count) for i in range(count)]
    return lax.ppermute(outer, "narrow", gaps)


def on_device(
    level_rhs,
    galerkin_cols,
    galerkin_blocks,
    restrict_cols,
    restrict_blocks,
    prolong_cols,
    prolong_blocks,
    coarse_inverse,
):
    levels = galerkin_cols.shape[0]
    count = galerkin_cols.shape[2]
    size = galerkin_blocks.shape[-1]
    rows, fields = level_rhs.shape[1:]
    half = fields // 2
    width = half // 2
    rcols = restrict_cols.transpose(0, 3, 1, 2), scalars()
    pcols = prolong_cols.transpose(0, 1, 3, 2), scalars()
    square_shape = array((rows, rows), bf16)
    operator_shapes = [square_shape, array((rows, 2 * size), bf16), array((rows, 1), f32)]
    rmat_shape = array((rows, 2 * rows), bf16)
    chunk_shape = array((rows, width), bf16)
    real_shape = array((rows, width), f32)
    held = [pltpu.VMEM((rows, rows), bf16)]

    def ends_shape(columns):
        return array((size, columns), bf16)

    def of_level(value, level_idx):
        return value, level_block(value, level_idx)

    def flops(columns, products=1):
        return 2 * products * rows * rows * columns

    def place_of(far, given):
        return (0, far, half), (1, given, width)

    pairs = [(place_of(1, given), place_of(0, given)) for given in (1, 0)]
    gcols, inner, *outers = run(
        functools.partial(start_kernel, pairs), "start",
        [array(galerkin_cols.shape, jnp.int32), ends_shape(fields)] + [ends_shape(half)] * 2,
        [in_hbm(level_rhs), in_hbm(galerkin_blocks), in_hbm(galerkin_cols)],
        scratch=[
            pltpu.VMEM((2, size, fields), f32), pltpu.VMEM((size, fields), bf16),
            pltpu.VMEM((2, size, size), bf16), pltpu.SemaphoreType.DMA((5,)),
        ],
    )
    gcols = in_vmem(gcols), scalars()
    first = outers[0]
    outers = [swap_outer(outer) for outer in outers]
    inner = exchange(inner, "narrow", 1)
    rest, base, local, rim, scale = run(
        first_local_kernel, "first_local", [array((rows, fields), f32)] * 2 + operator_shapes,
        [level_rhs, first, gcols, of_level(galerkin_blocks, 0)], flops=flops(fields),
    )
    operators = [(scale, local)]
    sent, kept = [], []
    for places, outer in zip(pairs, outers):
        far, near = run(
            functools.partial(first_residual_kernel, places), "first_residual", [chunk_shape] * 2,
            [rest, rim, outer, inner],
        )
        sent.append(far)
        kept.append(near)
    last = levels - 1
    bases = []
    anchor = sent[0]
    pieces = lax.axis_size("narrow")
    for level_idx in range(levels - 1):
        other = [exchange(value, "wide", 1 << level_idx) for value in sent]
        rmat, local, rim, scale = run(
            functools.partial(operators_kernel, level_idx), "operators",
            [rmat_shape] + operator_shapes,
            [anchor, rcols, of_level(restrict_blocks, level_idx),
             gcols, of_level(galerkin_blocks, level_idx + 1)],
        )
        operators.append((scale, local))
        joined = []
        for near, far in zip(kept, other):
            rhs, smoothed, *ends = run(
                functools.partial(join_kernel, level_idx), "join",
                [real_shape, chunk_shape] + [ends_shape(width)] * 2,
                [rmat, near, far, scale], flops=flops(width, 2),
            )
            inner, outer = exchange(ends[0], "narrow", 1), swap_outer(ends[1])
            joined.append((rhs, smoothed, scale, local, rim, outer, inner))
        share = []
        if level_idx + 1 == last:
            share = run(
                functools.partial(share_kernel, last), "share", [square_shape],
                [joined[0][1], rcols, of_level(restrict_blocks, last)],
            )
        made = []
        for operands in joined:
            value, made_base = run(
                last_residual_kernel if share else residual_kernel, "residual",
                [chunk_shape, real_shape if made or level_idx else chunk_shape],
                [*operands, *(share or [joined[-1][1]])],
                flops=flops(width, 2) if not made else late_cost,
            )
            made.append(value)
            bases.append(made_base)
        sent, kept = made[:1], made[-1:]
        anchor = made[0]
    (mine,) = kept
    far_parts = {o: exchange_both(mine, 1 << last, o) for o in range(0, pieces, 2)}
    far_base = exchange(bases[0], "wide", 1)
    own_parts = {o: exchange(mine, "narrow", o) if o else mine for o in range(0, pieces, 2)}
    coarse_mat, *ups = run(
        functools.partial(coarse_operators_kernel, 2, levels), "coarse_operators",
        [array((rows, pieces * rows), bf16)] + [square_shape] * (levels - 3),
        [mine, far_base, pcols, coarse_inverse]
        + [of_level(prolong_blocks, idx) for idx in range(2, levels)]
        + [value for pair in operators[2:] for value in pair],
        flops=flops(rows, 2 * (levels - 2) + pieces), scratch=held,
    )
    places = [place_of(0, 1), place_of(1, 1)]
    lower, upper, both, total = run(
        functools.partial(fine_operators_kernel, places), "fine_operators",
        [square_shape] * 3 + [array((rows, half), f32)],
        [mine, pcols, of_level(prolong_blocks, 0), of_level(prolong_blocks, 1),
         *operators[0], *operators[1], base, bases[0], far_base],
        flops=flops(rows, 4), scratch=held,
    )
    parts = {}
    for offset in reversed(range(0, pieces, 2)):
        (parts[offset],) = run(
            share_sum_kernel, "share_sum", [chunk_shape],
            [far_parts[offset], own_parts[offset], coarse_mat, upper],
        )
    offsets = tuple(parts)
    (value,) = run(
        functools.partial(coarse_kernel, offsets), "coarse", [real_shape],
        [coarse_mat] + [parts[o] for o in offsets] + [bases[-1]], flops=flops(width, len(offsets)),
    )
    parts = {o + 1: exchange(parts[o], "narrow", 1) for o in reversed(offsets)}
    offsets = tuple(parts)
    operands = [coarse_mat] + [parts[o] for o in offsets] + [value]
    for idx in reversed(range(2, last)):
        operands += [bases[idx], ups[idx - 2]]
    value, near = run(
        functools.partial(up_kernel, offsets), "up", [chunk_shape] * 2,
        operands + [bases[1], upper], flops=flops(width, len(offsets) + levels - 2),
    )
    diagonal, other = (exchange(value, "wide", bits) for bits in (3, 2))
    far = exchange(near, "wide", 1)
    result = None
    for group in (
        [(near, place_of(0, 0), None)],
        [(diagonal, place_of(1, 1), 1)],
        [(other, place_of(0, 1), 0), (far, place_of(1, 0), None)],
    ):
        values, places, slots = zip(*group)
        operands = [*values, base, lower, total, both]
        aliases = {}
        if result is not None:
            aliases[len(operands)] = 0
            operands.append(in_hbm(result))
        (result,) = run(
            functools.partial(output_kernel, places, slots),
            "output", [array((1, rows, fields), f32)], operands,
            flops=flops(width, len(group)), out_space=pltpu.HBM, aliases=aliases,
            scratch=[
                pltpu.VMEM((len(group), rows, width), f32), pltpu.SemaphoreType.DMA((len(group),))
            ],
        )
    return result


def solution(mesh):
    in_specs = (
        P("wide", "narrow", None),
        P(None, "wide", "narrow", None),
        P(None, "wide", "narrow", None, None, None),
        P(None, "wide", "narrow", None),
        P(None, "wide", "narrow", None, None, None),
        P(None, "wide", "narrow", None),
        P(None, "wide", "narrow", None, None, None),
        P("narrow", None),
    )
    out_specs = P("wide", "narrow", None)
    return jax.shard_map(
        on_device, mesh=mesh, in_specs=in_specs, out_specs=out_specs, check_vma=False
    )
```

```python
import functools

import jax
import jax.numpy as jnp
from jax import lax
from jax.experimental import pallas as pl
from jax.experimental.pallas import tpu as pltpu
from jax.sharding import PartitionSpec as P

relax_down = 0.7
relax_up = 0.5
f32 = jnp.float32
bf16 = jnp.bfloat16
grant = 12 * 1024 * 1024
late_cost = 4 * 10**9


def matmul(a, b):
    return jnp.dot(a, b, preferred_element_type=f32)


def array(shape, dtype):
    return jax.ShapeDtypeStruct(shape, dtype)


def whole():
    return pl.BlockSpec(memory_space=pltpu.VMEM)


def level_block(value, level_idx):
    shape = (1,) + value.shape[1:]
    return pl.BlockSpec(shape, lambda i: (level_idx,) + (0,) * (value.ndim - 1))


def scalars():
    return pl.BlockSpec(memory_space=pltpu.SMEM)


def in_hbm(value):
    return pltpu.with_memory_space_constraint(value, pltpu.HBM), pl.BlockSpec(memory_space=pltpu.HBM)


def in_vmem(value):
    return pltpu.with_memory_space_constraint(value, pltpu.VMEM)


def run(body, name, outs, operands, flops=0, scratch=(), out_space=pltpu.VMEM, aliases=None):
    arrays = [o[0] if isinstance(o, tuple) else in_vmem(o) for o in operands]
    specs = [o[1] if isinstance(o, tuple) else whole() for o in operands]
    windows = any(isinstance(o, tuple) and o[1].block_shape is not None for o in operands)
    moved = sum(a.size * a.dtype.itemsize for a in arrays)
    return pl.pallas_call(
        body,
        grid=(1,) if windows else (),
        out_shape=[out_space(o.shape, o.dtype) for o in outs],
        in_specs=specs,
        out_specs=[pl.BlockSpec(memory_space=out_space)] * len(outs),
        input_output_aliases=aliases or {},
        scratch_shapes=list(scratch),
        compiler_params=pltpu.CompilerParams(vmem_limit_bytes=grant),
        cost_estimate=pl.CostEstimate(flops=flops, bytes_accessed=moved, transcendentals=0),
        name=name,
    )(*arrays)


def diagonal_of(block):
    size = block.shape[0]
    rows = lax.broadcasted_iota(jnp.int32, (size, size), 0)
    lanes = lax.broadcasted_iota(jnp.int32, (size, size), 1)
    return jnp.sum(jnp.where(rows == lanes, block, 0.0), axis=1, keepdims=True)


def placed(base, others, ids, target):
    total = base
    for block, ident in zip(others, ids):
        term = block * jnp.where(ident == target, 1.0, 0.0).astype(f32)
        total = term if total is None else total + term
    return total


def parity_of():
    return lax.rem(lax.axis_index("narrow"), 2)


def put_ends(first, last, inner_ref, outer_ref):
    even = parity_of() == 0
    inner_ref[...] = jnp.where(even, last, first)
    outer_ref[...] = jnp.where(even, first, last)


def assemble_galerkin(level_idx, cols, blocks, local_ref, rim_ref, scale_ref):
    count, slots, size = blocks.shape[2], blocks.shape[3], blocks.shape[4]
    parity = parity_of()
    piece = lax.axis_index("narrow")
    last = lax.axis_size("narrow") - 1
    inside = jnp.where((piece == 0) | (piece == last), 0.0, 1.0).astype(f32)
    for b in range(count):
        held = [blocks[0, 0, b, s].astype(f32) for s in range(slots)]
        ids = [cols[level_idx, 0, b, s] for s in range(1, slots)]
        rows = pl.ds(b * size, size)
        scale_ref[rows, :] = 1.0 / diagonal_of(held[0])
        line = [placed(held[0] if c == b else None, held[1:], ids, c) for c in range(count)]
        local_ref[rows, :] = jnp.concatenate(line, axis=1).astype(bf16)
        rims = [
            placed(None, held[1:], ids, count + 1 - parity),
            placed(None, held[1:], ids, count + parity) * inside,
        ]
        rim_ref[rows, :] = jnp.concatenate(rims, axis=1).astype(bf16)


def assemble_restrict(level_idx, cols, blocks, out_ref):
    count, slots, size = blocks.shape[2], blocks.shape[3], blocks.shape[4]
    for b in range(count):
        held = [blocks[0, 0, b, s].astype(f32) for s in range(slots)]
        ids = [cols[level_idx, s, 0, b] for s in range(2, slots)]
        fixed = {b: held[0], count + b: held[1]}
        line = [placed(fixed.get(c), held[2:], ids, c) for c in range(2 * count)]
        out_ref[pl.ds(b * size, size), :] = jnp.concatenate(line, axis=1).astype(bf16)


def assemble_share(level_idx, cols, blocks, out_ref):
    count, slots, size = blocks.shape[2], blocks.shape[3], blocks.shape[4]
    bit = bit_of(level_idx)
    for b in range(count):
        held = [blocks[0, 0, b, s].astype(f32) for s in range(slots)]
        ids = [cols[level_idx, s, 0, b] for s in range(2, slots)]
        own = jnp.where(bit == 0, held[0], held[1])
        first = bit * count
        line = [placed(own if c == b else None, held[2:], ids, first + c) for c in range(count)]
        out_ref[pl.ds(b * size, size), :] = jnp.concatenate(line, axis=1).astype(bf16)


def assemble_prolong(level_idx, cols, blocks, out_ref):
    count, slots, size = blocks.shape[2], blocks.shape[3], blocks.shape[4]
    for b in range(count):
        held = [blocks[0, 0, b, s].astype(f32) for s in range(slots)]
        ids = [cols[level_idx, 0, s, b] for s in range(1, slots)]
        line = [placed(held[0] if c == b else None, held[1:], ids, c) for c in range(count)]
        out_ref[pl.ds(b * size, size), :] = jnp.concatenate(line, axis=1).astype(bf16)


def start_kernel(places, rhs, blocks, *refs):
    table, held, inner_ref, *outers, rows, outer, pivots, sems = refs
    count, size = blocks.shape[2], blocks.shape[4]
    copies = []
    for slot, which in enumerate((0, count - 1)):
        source = rhs.at[0, pl.ds(which * size, size), :]
        copies.append(pltpu.make_async_copy(source, rows.at[slot], sems.at[slot]))
        source = blocks.at[0, 0, which, 0]
        copies.append(pltpu.make_async_copy(source, pivots.at[slot], sems.at[2 + slot]))
    copies.append(pltpu.make_async_copy(table, held, sems.at[4]))
    for copy in copies:
        copy.start()
    for copy in copies:
        copy.wait()
    first, last = (
        (rows[slot] * (relax_down / diagonal_of(pivots[slot].astype(f32)))).astype(bf16)
        for slot in range(2)
    )
    put_ends(first, last, inner_ref, outer)
    for ref, pair in zip(outers, places):
        width = ref.shape[1] // 2
        for slot, place in enumerate(pair):
            ref[:, slot * width : (slot + 1) * width] = outer[:, lanes_of(place, width)]


def first_local_kernel(rhs, _, cols, blocks, rest, base, local, rim, scale):
    assemble_galerkin(0, cols, blocks, local, rim, scale)
    smoothed = rhs[0] * (relax_down * scale[...])
    left = rhs[0] - matmul(local[...], smoothed.astype(bf16))
    rest[...] = left
    base[...] = smoothed + (relax_up * scale[...]) * left


def bit_of(level_idx):
    return lax.axis_index("wide") >> level_idx & 1


def lanes_of(place, width):
    start = 0
    for level_idx, flip, step in place:
        start = start + (bit_of(level_idx) ^ flip) * step
    return pl.ds(pl.multiple_of(start, width), width)


def first_residual_kernel(places, rest, rim, outer, inner, *refs):
    width = refs[0].shape[1]
    for slot, (ref, place) in enumerate(zip(refs, places)):
        lanes = lanes_of(place, width)
        columns = pl.ds(slot * width, width)
        rims = jnp.concatenate([inner[:, lanes], outer[:, columns]], axis=0)
        ref[...] = (rest[:, lanes] - matmul(rim[...], rims)).astype(bf16)


def residual_kernel(rhs, smoothed, scale, local, rim, outer, inner, _, out, base):
    rims = jnp.concatenate([inner[...], outer[...]], axis=0)
    left = rhs[...] - matmul(local[...], smoothed[...])
    out[...] = (left - matmul(rim[...], rims)).astype(bf16)
    made = rhs[...] * (relax_down * scale[...]) + (relax_up * scale[...]) * left
    base[...] = made.astype(base.dtype)


def last_residual_kernel(
    rhs, smoothed, scale, local, rim, outer, inner, share, out, base, lower_rows
):
    rims = jnp.concatenate([inner[...], outer[...]], axis=0)
    left = rhs[...] - matmul(local[...], smoothed[...])
    residual = (left - matmul(rim[...], rims)).astype(bf16)
    made = matmul(share[...], residual).astype(bf16)
    out[...] = made
    lower_rows[...] = made[lower_rows.shape[0] :]
    base[...] = rhs[...] * (relax_down * scale[...]) + (relax_up * scale[...]) * left


def share_kernel(level_idx, _, rcols, rblocks, share):
    assemble_share(level_idx, rcols, rblocks, share)


def operators_kernel(level_idx, _, rcols, rblocks, cols, blocks, rmat, local, rim, scale):
    assemble_restrict(level_idx, rcols, rblocks, rmat)
    assemble_galerkin(level_idx + 1, cols, blocks, local, rim, scale)


def raising(level_idx, pcols, blocks, local, scale, held):
    assemble_prolong(level_idx, pcols, blocks, held)
    applied = matmul(local[...], held[...])
    return (held[...].astype(f32) - (relax_up * scale[...]) * applied).astype(bf16)


def coarse_operators_kernel(first, levels, *refs):
    _, _, pcols, inverse, *refs = refs
    places = range(first, levels)
    blocks, refs = refs[: len(places)], refs[len(places) :]
    pairs, refs = refs[: 2 * len(places)], refs[2 * len(places) :]
    coarse, *up, held = refs
    for idx in places:
        slot = idx - first
        made = raising(idx, pcols, blocks[slot], pairs[2 * slot + 1], pairs[2 * slot], held)
        if idx == levels - 1:
            coarse[...] = matmul(made, inverse[...]).astype(bf16)
        else:
            up[slot][...] = made


def fine_operators_kernel(
    places, _, pcols, blocks_0, blocks_1, scale_0, local_0, scale_1, local_1,
    base, near, far, lower, upper, both, total, held,
):
    lower[...] = raising(0, pcols, blocks_0, local_0, scale_0, held)
    upper[...] = raising(1, pcols, blocks_1, local_1, scale_1, held)
    both[...] = matmul(lower[...], upper[...]).astype(bf16)
    width = near.shape[1]
    for slot, (place, source) in enumerate(zip(places, (near, far))):
        made = base[:, lanes_of(place, width)] + matmul(lower[...], source[...])
        total[:, slot * width : (slot + 1) * width] = made


def restricted(level_idx, rmat, kept, other):
    width = rmat.shape[1] // 2
    own = pl.multiple_of(bit_of(level_idx) * width, width)
    far = pl.multiple_of((1 - bit_of(level_idx)) * width, width)
    total = matmul(rmat[:, pl.ds(own, width)], kept[...])
    return total + matmul(rmat[:, pl.ds(far, width)], other[...])


def join_kernel(level_idx, rmat, kept, other, scale, rhs, smoothed, inner_ref, outer_ref):
    size = inner_ref.shape[0]
    current = restricted(level_idx, rmat, kept, other)
    rhs[...] = current
    rounded = (current * (relax_down * scale[...])).astype(bf16)
    smoothed[...] = rounded
    put_ends(rounded[:size], rounded[-size:], inner_ref, outer_ref)


def inverse_part(inverse, part, offset):
    depth = part.shape[0]
    piece = lax.axis_index("narrow") ^ offset
    return matmul(inverse[:, pl.ds(pl.multiple_of(piece * depth, depth), depth)], part[...])


def share_sum_kernel(far, own, _, out, upper_rows):
    made = (far[...].astype(f32) + own[...].astype(f32)).astype(bf16)
    out[...] = made
    upper_rows[...] = made[: upper_rows.shape[0]]


def share_join_kernel(upper_rows, far, own, _, out):
    rows = upper_rows.shape[0]
    out[:rows, :] = upper_rows[...]
    out[rows:, :] = (far[...].astype(f32) + own[...].astype(f32)).astype(bf16)


def coarse_kernel(offsets, inverse, *refs):
    *parts, value, out = refs
    value = value[...]
    for part, offset in zip(parts, offsets):
        value = value + inverse_part(inverse, part, offset)
    out[...] = value


def up_kernel(offsets, inverse, *refs):
    value = refs[len(offsets)][...]
    for part, offset in zip(refs, offsets):
        value = value + inverse_part(inverse, part, offset)
    refs = refs[len(offsets) + 1 :]
    refs, (base, up, coarse, raised) = refs[:-4], refs[-4:]
    for step in range(len(refs) // 2):
        value = refs[2 * step][...] + matmul(refs[2 * step + 1][...], value.astype(bf16))
    value = value.astype(bf16)
    coarse[...] = value
    raised[...] = (base[...] + matmul(up[...], value)).astype(bf16)


def output_kernel(places, slots, *refs):
    coarse, (base, lower, total, both) = refs[: len(places)], refs[len(places) : len(places) + 4]
    out, made, sems = refs[-3:]
    copies = []
    for item, (place, value) in enumerate(zip(places, coarse)):
        width = value.shape[1]
        lanes = lanes_of(place, width)
        if slots[item] is None:
            made[item] = base[:, lanes] + matmul(lower[...], value[...])
        else:
            held = total[:, slots[item] * width : (slots[item] + 1) * width]
            made[item] = held + matmul(both[...], value[...])
        copy = pltpu.make_async_copy(made.at[item], out.at[0, :, lanes], sems.at[item])
        copy.start()
        copies.append(copy)
    for copy in copies:
        copy.wait()


def exchange(value, axis, bit):
    count = lax.axis_size(axis)
    return lax.ppermute(value, axis, [(i, i ^ bit) for i in range(count)])


def exchange_both(value, bit, offset):
    wide, narrow = lax.axis_size("wide"), lax.axis_size("narrow")
    pairs = [
        (w * narrow + j, (w ^ bit) * narrow + (j ^ offset))
        for w in range(wide) for j in range(narrow)
    ]
    return lax.ppermute(value, ("wide", "narrow"), pairs)


def swap_outer(outer):
    count = lax.axis_size("narrow")
    gaps = [(i, (i + 1 if i % 2 else i - 1) % count) for i in range(count)]
    return lax.ppermute(outer, "narrow", gaps)


def on_device(
    level_rhs,
    galerkin_cols,
    galerkin_blocks,
    restrict_cols,
    restrict_blocks,
    prolong_cols,
    prolong_blocks,
    coarse_inverse,
):
    levels = galerkin_cols.shape[0]
    count = galerkin_cols.shape[2]
    size = galerkin_blocks.shape[-1]
    rows, fields = level_rhs.shape[1:]
    half = fields // 2
    width = half // 2
    rcols = restrict_cols.transpose(0, 3, 1, 2), scalars()
    pcols = prolong_cols.transpose(0, 1, 3, 2), scalars()
    square_shape = array((rows, rows), bf16)
    operator_shapes = [square_shape, array((rows, 2 * size), bf16), array((rows, 1), f32)]
    rmat_shape = array((rows, 2 * rows), bf16)
    chunk_shape = array((rows, width), bf16)
    real_shape = array((rows, width), f32)
    held = [pltpu.VMEM((rows, rows), bf16)]

    def ends_shape(columns):
        return array((size, columns), bf16)

    def of_level(value, level_idx):
        return value, level_block(value, level_idx)

    def flops(columns, products=1):
        return 2 * products * rows * rows * columns

    def place_of(far, given):
        return (0, far, half), (1, given, width)

    pairs = [(place_of(1, given), place_of(0, given)) for given in (1, 0)]
    gcols, inner, *outers = run(
        functools.partial(start_kernel, pairs), "start",
        [array(galerkin_cols.shape, jnp.int32), ends_shape(fields)] + [ends_shape(half)] * 2,
        [in_hbm(level_rhs), in_hbm(galerkin_blocks), in_hbm(galerkin_cols)],
        scratch=[
            pltpu.VMEM((2, size, fields), f32), pltpu.VMEM((size, fields), bf16),
            pltpu.VMEM((2, size, size), bf16), pltpu.SemaphoreType.DMA((5,)),
        ],
    )
    gcols = in_vmem(gcols), scalars()
    first = outers[0]
    outers = [swap_outer(outer) for outer in outers]
    inner = exchange(inner, "narrow", 1)
    rest, base, local, rim, scale = run(
        first_local_kernel, "first_local", [array((rows, fields), f32)] * 2 + operator_shapes,
        [level_rhs, first, gcols, of_level(galerkin_blocks, 0)], flops=flops(fields),
    )
    operators = [(scale, local)]
    sent, kept = [], []
    for places, outer in zip(pairs, outers):
        far, near = run(
            functools.partial(first_residual_kernel, places), "first_residual", [chunk_shape] * 2,
            [rest, rim, outer, inner],
        )
        sent.append(far)
        kept.append(near)
    last = levels - 1
    bases = []
    anchor = sent[0]
    pieces = lax.axis_size("narrow")
    for level_idx in range(levels - 1):
        other = [exchange(value, "wide", 1 << level_idx) for value in sent]
        rmat, local, rim, scale = run(
            functools.partial(operators_kernel, level_idx), "operators",
            [rmat_shape] + operator_shapes,
            [anchor, rcols, of_level(restrict_blocks, level_idx),
             gcols, of_level(galerkin_blocks, level_idx + 1)],
        )
        operators.append((scale, local))
        joined = []
        for near, far in zip(kept, other):
            rhs, smoothed, *ends = run(
                functools.partial(join_kernel, level_idx), "join",
                [real_shape, chunk_shape] + [ends_shape(width)] * 2,
                [rmat, near, far, scale], flops=flops(width, 2),
            )
            inner, outer = exchange(ends[0], "narrow", 1), swap_outer(ends[1])
            joined.append((rhs, smoothed, scale, local, rim, outer, inner))
        share = []
        if level_idx + 1 == last:
            share = run(
                functools.partial(share_kernel, last), "share", [square_shape],
                [joined[0][1], rcols, of_level(restrict_blocks, last)],
            )
        made = []
        for operands in joined:
            value, made_base, *lower_rows = run(
                last_residual_kernel if share else residual_kernel, "residual",
                [chunk_shape, real_shape if made or level_idx else chunk_shape]
                + [array((rows // 2, width), bf16)] * len(share),
                [*operands, *(share or [joined[-1][1]])],
                flops=flops(width, 2) if not made else late_cost,
            )
            made.append(value)
            bases.append(made_base)
        sent, kept = made[:1], made[-1:]
        anchor = made[0]
    (mine,) = kept
    (lower_rows,) = lower_rows
    far_part = exchange_both(mine, 1 << last, 0)
    across = {
        o: (exchange_both(lower_rows, 1 << last, o), exchange(lower_rows, "narrow", o))
        for o in range(2, pieces, 2)
    }
    far_base = exchange(bases[0], "wide", 1)
    coarse_mat, *ups = run(
        functools.partial(coarse_operators_kernel, 2, levels), "coarse_operators",
        [array((rows, pieces * rows), bf16)] + [square_shape] * (levels - 3),
        [mine, far_base, pcols, coarse_inverse]
        + [of_level(prolong_blocks, idx) for idx in range(2, levels)]
        + [value for pair in operators[2:] for value in pair],
        flops=flops(rows, 2 * (levels - 2) + pieces), scratch=held,
    )
    places = [place_of(0, 1), place_of(1, 1)]
    lower, upper, both, total = run(
        functools.partial(fine_operators_kernel, places), "fine_operators",
        [square_shape] * 3 + [array((rows, half), f32)],
        [mine, pcols, of_level(prolong_blocks, 0), of_level(prolong_blocks, 1),
         *operators[0], *operators[1], base, bases[0], far_base],
        flops=flops(rows, 4), scratch=held,
    )
    total_share, upper_rows = run(
        share_sum_kernel, "share_sum", [chunk_shape, array((rows // 2, width), bf16)],
        [far_part, mine, coarse_mat],
    )
    parts = {0: total_share}
    for offset, (far_rows, own_rows) in across.items():
        (parts[offset],) = run(
            share_join_kernel, "share_join", [chunk_shape],
            [exchange(upper_rows, "narrow", offset), far_rows, own_rows, upper],
        )
    offsets = tuple(parts)
    (value,) = run(
        functools.partial(coarse_kernel, offsets), "coarse", [real_shape],
        [coarse_mat] + [parts[o] for o in offsets] + [bases[-1]], flops=flops(width, len(offsets)),
    )
    parts = {o + 1: exchange(parts[o], "narrow", 1) for o in reversed(offsets)}
    offsets = tuple(parts)
    operands = [coarse_mat] + [parts[o] for o in offsets] + [value]
    for idx in reversed(range(2, last)):
        operands += [bases[idx], ups[idx - 2]]
    value, near = run(
        functools.partial(up_kernel, offsets), "up", [chunk_shape] * 2,
        operands + [bases[1], upper], flops=flops(width, len(offsets) + levels - 2),
    )
    diagonal, other = (exchange(value, "wide", bits) for bits in (3, 2))
    far = exchange(near, "wide", 1)
    result = None
    for group in (
        [(near, place_of(0, 0), None)],
        [(diagonal, place_of(1, 1), 1)],
        [(other, place_of(0, 1), 0), (far, place_of(1, 0), None)],
    ):
        values, places, slots = zip(*group)
        operands = [*values, base, lower, total, both]
        aliases = {}
        if result is not None:
            aliases[len(operands)] = 0
            operands.append(in_hbm(result))
        (result,) = run(
            functools.partial(output_kernel, places, slots),
            "output", [array((1, rows, fields), f32)], operands,
            flops=flops(width, len(group)), out_space=pltpu.HBM, aliases=aliases,
            scratch=[
                pltpu.VMEM((len(group), rows, width), f32), pltpu.SemaphoreType.DMA((len(group),))
            ],
        )
    return result


def solution(mesh):
    in_specs = (
        P("wide", "narrow", None),
        P(None, "wide", "narrow", None),
        P(None, "wide", "narrow", None, None, None),
        P(None, "wide", "narrow", None),
        P(None, "wide", "narrow", None, None, None),
        P(None, "wide", "narrow", None),
        P(None, "wide", "narrow", None, None, None),
        P("narrow", None),
    )
    out_specs = P("wide", "narrow", None)
    return jax.shard_map(
        on_device, mesh=mesh, in_specs=in_specs, out_specs=out_specs, check_vma=False
    )
```

```python
import functools

import jax
import jax.numpy as jnp
from jax import lax
from jax.experimental import pallas as pl
from jax.experimental.pallas import tpu as pltpu
from jax.sharding import PartitionSpec as P

relax_down = 0.7
relax_up = 0.5
f32 = jnp.float32
bf16 = jnp.bfloat16
grant = 12 * 1024 * 1024
late_cost = 4 * 10**9


def matmul(a, b):
    return jnp.dot(a, b, preferred_element_type=f32)


def array(shape, dtype):
    return jax.ShapeDtypeStruct(shape, dtype)


def whole():
    return pl.BlockSpec(memory_space=pltpu.VMEM)


def level_block(value, level_idx):
    shape = (1,) + value.shape[1:]
    return pl.BlockSpec(shape, lambda i: (level_idx,) + (0,) * (value.ndim - 1))


def scalars():
    return pl.BlockSpec(memory_space=pltpu.SMEM)


def in_hbm(value):
    return pltpu.with_memory_space_constraint(value, pltpu.HBM), pl.BlockSpec(memory_space=pltpu.HBM)


def in_vmem(value):
    return pltpu.with_memory_space_constraint(value, pltpu.VMEM)


def run(body, name, outs, operands, flops=0, scratch=(), out_space=pltpu.VMEM, aliases=None):
    arrays = [o[0] if isinstance(o, tuple) else in_vmem(o) for o in operands]
    specs = [o[1] if isinstance(o, tuple) else whole() for o in operands]
    windows = any(isinstance(o, tuple) and o[1].block_shape is not None for o in operands)
    moved = sum(a.size * a.dtype.itemsize for a in arrays)
    return pl.pallas_call(
        body,
        grid=(1,) if windows else (),
        out_shape=[out_space(o.shape, o.dtype) for o in outs],
        in_specs=specs,
        out_specs=[pl.BlockSpec(memory_space=out_space)] * len(outs),
        input_output_aliases=aliases or {},
        scratch_shapes=list(scratch),
        compiler_params=pltpu.CompilerParams(vmem_limit_bytes=grant),
        cost_estimate=pl.CostEstimate(flops=flops, bytes_accessed=moved, transcendentals=0),
        name=name,
    )(*arrays)


def diagonal_of(block):
    size = block.shape[0]
    rows = lax.broadcasted_iota(jnp.int32, (size, size), 0)
    lanes = lax.broadcasted_iota(jnp.int32, (size, size), 1)
    return jnp.sum(jnp.where(rows == lanes, block, 0.0), axis=1, keepdims=True)


def placed(base, others, ids, target):
    total = base
    for block, ident in zip(others, ids):
        term = block * jnp.where(ident == target, 1.0, 0.0).astype(f32)
        total = term if total is None else total + term
    return total


def parity_of():
    return lax.rem(lax.axis_index("narrow"), 2)


def put_ends(first, last, inner_ref, outer_ref):
    even = parity_of() == 0
    inner_ref[...] = jnp.where(even, last, first)
    outer_ref[...] = jnp.where(even, first, last)


def assemble_galerkin(level_idx, cols, blocks, local_ref, rim_ref, scale_ref):
    count, slots, size = blocks.shape[2], blocks.shape[3], blocks.shape[4]
    parity = parity_of()
    piece = lax.axis_index("narrow")
    last = lax.axis_size("narrow") - 1
    inside = jnp.where((piece == 0) | (piece == last), 0.0, 1.0).astype(f32)
    for b in range(count):
        held = [blocks[0, 0, b, s].astype(f32) for s in range(slots)]
        ids = [cols[level_idx, 0, b, s] for s in range(1, slots)]
        rows = pl.ds(b * size, size)
        scale_ref[rows, :] = 1.0 / diagonal_of(held[0])
        line = [placed(held[0] if c == b else None, held[1:], ids, c) for c in range(count)]
        local_ref[rows, :] = jnp.concatenate(line, axis=1).astype(bf16)
        rims = [
            placed(None, held[1:], ids, count + 1 - parity),
            placed(None, held[1:], ids, count + parity) * inside,
        ]
        rim_ref[rows, :] = jnp.concatenate(rims, axis=1).astype(bf16)


def assemble_restrict(level_idx, cols, blocks, out_ref):
    count, slots, size = blocks.shape[2], blocks.shape[3], blocks.shape[4]
    for b in range(count):
        held = [blocks[0, 0, b, s].astype(f32) for s in range(slots)]
        ids = [cols[level_idx, s, 0, b] for s in range(2, slots)]
        fixed = {b: held[0], count + b: held[1]}
        line = [placed(fixed.get(c), held[2:], ids, c) for c in range(2 * count)]
        out_ref[pl.ds(b * size, size), :] = jnp.concatenate(line, axis=1).astype(bf16)


def assemble_share(level_idx, cols, blocks, out_ref):
    count, slots, size = blocks.shape[2], blocks.shape[3], blocks.shape[4]
    bit = bit_of(level_idx)
    for b in range(count):
        held = [blocks[0, 0, b, s].astype(f32) for s in range(slots)]
        ids = [cols[level_idx, s, 0, b] for s in range(2, slots)]
        own = jnp.where(bit == 0, held[0], held[1])
        first = bit * count
        line = [placed(own if c == b else None, held[2:], ids, first + c) for c in range(count)]
        out_ref[pl.ds(b * size, size), :] = jnp.concatenate(line, axis=1).astype(bf16)


def assemble_prolong(level_idx, cols, blocks, out_ref):
    count, slots, size = blocks.shape[2], blocks.shape[3], blocks.shape[4]
    for b in range(count):
        held = [blocks[0, 0, b, s].astype(f32) for s in range(slots)]
        ids = [cols[level_idx, 0, s, b] for s in range(1, slots)]
        line = [placed(held[0] if c == b else None, held[1:], ids, c) for c in range(count)]
        out_ref[pl.ds(b * size, size), :] = jnp.concatenate(line, axis=1).astype(bf16)


def start_kernel(places, rhs, blocks, *refs):
    table, held, inner_ref, *outers, rows, outer, pivots, sems = refs
    count, size = blocks.shape[2], blocks.shape[4]
    copies = []
    for slot, which in enumerate((0, count - 1)):
        source = rhs.at[0, pl.ds(which * size, size), :]
        copies.append(pltpu.make_async_copy(source, rows.at[slot], sems.at[slot]))
        source = blocks.at[0, 0, which, 0]
        copies.append(pltpu.make_async_copy(source, pivots.at[slot], sems.at[2 + slot]))
    copies.append(pltpu.make_async_copy(table, held, sems.at[4]))
    for copy in copies:
        copy.start()
    for copy in copies:
        copy.wait()
    first, last = (
        (rows[slot] * (relax_down / diagonal_of(pivots[slot].astype(f32)))).astype(bf16)
        for slot in range(2)
    )
    put_ends(first, last, inner_ref, outer)
    for ref, pair in zip(outers, places):
        width = ref.shape[1] // 2
        for slot, place in enumerate(pair):
            ref[:, slot * width : (slot + 1) * width] = outer[:, lanes_of(place, width)]


def first_local_kernel(rhs, _, cols, blocks, rest, base, local, rim, scale):
    assemble_galerkin(0, cols, blocks, local, rim, scale)
    smoothed = rhs[0] * (relax_down * scale[...])
    left = rhs[0] - matmul(local[...], smoothed.astype(bf16))
    rest[...] = left
    base[...] = smoothed + (relax_up * scale[...]) * left


def bit_of(level_idx):
    return lax.axis_index("wide") >> level_idx & 1


def lanes_of(place, width):
    start = 0
    for level_idx, flip, step in place:
        start = start + (bit_of(level_idx) ^ flip) * step
    return pl.ds(pl.multiple_of(start, width), width)


def first_residual_kernel(places, rest, rim, outer, inner, *refs):
    width = refs[0].shape[1]
    for slot, (ref, place) in enumerate(zip(refs, places)):
        lanes = lanes_of(place, width)
        columns = pl.ds(slot * width, width)
        rims = jnp.concatenate([inner[:, lanes], outer[:, columns]], axis=0)
        ref[...] = (rest[:, lanes] - matmul(rim[...], rims)).astype(bf16)


def local_kernel(rhs, smoothed, local, *refs):
    refs[-1][...] = rhs[...] - matmul(local[...], smoothed[...])


def residual_kernel(rhs, left, scale, rim, outer, inner, _, out, base):
    rims = jnp.concatenate([inner[...], outer[...]], axis=0)
    out[...] = (left[...] - matmul(rim[...], rims)).astype(bf16)
    made = rhs[...] * (relax_down * scale[...]) + (relax_up * scale[...]) * left[...]
    base[...] = made.astype(base.dtype)


def last_residual_kernel(rhs, left, scale, rim, outer, inner, share, out, base):
    rims = jnp.concatenate([inner[...], outer[...]], axis=0)
    residual = (left[...] - matmul(rim[...], rims)).astype(bf16)
    out[...] = matmul(share[...], residual).astype(bf16)
    base[...] = rhs[...] * (relax_down * scale[...]) + (relax_up * scale[...]) * left[...]


def share_kernel(level_idx, _, rcols, rblocks, share):
    assemble_share(level_idx, rcols, rblocks, share)


def operators_kernel(level_idx, _, rcols, rblocks, cols, blocks, rmat, local, rim, scale):
    assemble_restrict(level_idx, rcols, rblocks, rmat)
    assemble_galerkin(level_idx + 1, cols, blocks, local, rim, scale)


def raising(level_idx, pcols, blocks, local, scale, held):
    assemble_prolong(level_idx, pcols, blocks, held)
    applied = matmul(local[...], held[...])
    return (held[...].astype(f32) - (relax_up * scale[...]) * applied).astype(bf16)


def coarse_operators_kernel(first, levels, *refs):
    _, _, pcols, inverse, *refs = refs
    places = range(first, levels)
    blocks, refs = refs[: len(places)], refs[len(places) :]
    pairs, refs = refs[: 2 * len(places)], refs[2 * len(places) :]
    coarse, *up, held = refs
    for idx in places:
        slot = idx - first
        made = raising(idx, pcols, blocks[slot], pairs[2 * slot + 1], pairs[2 * slot], held)
        if idx == levels - 1:
            coarse[...] = matmul(made, inverse[...]).astype(bf16)
        else:
            up[slot][...] = made


def fine_operators_kernel(
    places, _, pcols, blocks_0, blocks_1, scale_0, local_0, scale_1, local_1,
    base, near, far, lower, upper, both, total, held,
):
    lower[...] = raising(0, pcols, blocks_0, local_0, scale_0, held)
    upper[...] = raising(1, pcols, blocks_1, local_1, scale_1, held)
    both[...] = matmul(lower[...], upper[...]).astype(bf16)
    width = near.shape[1]
    for slot, (place, source) in enumerate(zip(places, (near, far))):
        made = base[:, lanes_of(place, width)] + matmul(lower[...], source[...])
        total[:, slot * width : (slot + 1) * width] = made


def restricted(level_idx, rmat, kept, other):
    width = rmat.shape[1] // 2
    own = pl.multiple_of(bit_of(level_idx) * width, width)
    far = pl.multiple_of((1 - bit_of(level_idx)) * width, width)
    total = matmul(rmat[:, pl.ds(own, width)], kept[...])
    return total + matmul(rmat[:, pl.ds(far, width)], other[...])


def join_kernel(level_idx, rmat, kept, other, scale, rhs, smoothed, inner_ref, outer_ref):
    size = inner_ref.shape[0]
    current = restricted(level_idx, rmat, kept, other)
    rhs[...] = current
    rounded = (current * (relax_down * scale[...])).astype(bf16)
    smoothed[...] = rounded
    put_ends(rounded[:size], rounded[-size:], inner_ref, outer_ref)


def inverse_part(inverse, part, offset):
    depth = part.shape[0]
    piece = lax.axis_index("narrow") ^ offset
    return matmul(inverse[:, pl.ds(pl.multiple_of(piece * depth, depth), depth)], part[...])


def share_sum_kernel(far, own, *refs):
    refs[-1][...] = (far[...].astype(f32) + own[...].astype(f32)).astype(bf16)


def coarse_kernel(offsets, inverse, *refs):
    *parts, value, out = refs
    value = value[...]
    for part, offset in zip(parts, offsets):
        value = value + inverse_part(inverse, part, offset)
    out[...] = value


def up_kernel(offsets, inverse, *refs):
    value = refs[len(offsets)][...]
    for part, offset in zip(refs, offsets):
        value = value + inverse_part(inverse, part, offset)
    refs = refs[len(offsets) + 1 :]
    refs, (base, up, coarse, raised) = refs[:-4], refs[-4:]
    for step in range(len(refs) // 2):
        value = refs[2 * step][...] + matmul(refs[2 * step + 1][...], value.astype(bf16))
    value = value.astype(bf16)
    coarse[...] = value
    raised[...] = (base[...] + matmul(up[...], value)).astype(bf16)


def output_kernel(places, slots, *refs):
    coarse, (base, lower, total, both) = refs[: len(places)], refs[len(places) : len(places) + 4]
    out, made, sems = refs[-3:]
    copies = []
    for item, (place, value) in enumerate(zip(places, coarse)):
        width = value.shape[1]
        lanes = lanes_of(place, width)
        if slots[item] is None:
            made[item] = base[:, lanes] + matmul(lower[...], value[...])
        else:
            held = total[:, slots[item] * width : (slots[item] + 1) * width]
            made[item] = held + matmul(both[...], value[...])
        copy = pltpu.make_async_copy(made.at[item], out.at[0, :, lanes], sems.at[item])
        copy.start()
        copies.append(copy)
    for copy in copies:
        copy.wait()


def exchange(value, axis, bit):
    count = lax.axis_size(axis)
    return lax.ppermute(value, axis, [(i, i ^ bit) for i in range(count)])


def exchange_both(value, bit, offset):
    wide, narrow = lax.axis_size("wide"), lax.axis_size("narrow")
    pairs = [
        (w * narrow + j, (w ^ bit) * narrow + (j ^ offset))
        for w in range(wide) for j in range(narrow)
    ]
    return lax.ppermute(value, ("wide", "narrow"), pairs)


def swap_outer(outer):
    count = lax.axis_size("narrow")
    gaps = [(i, (i + 1 if i % 2 else i - 1) % count) for i in range(count)]
    return lax.ppermute(outer, "narrow", gaps)


def on_device(
    level_rhs,
    galerkin_cols,
    galerkin_blocks,
    restrict_cols,
    restrict_blocks,
    prolong_cols,
    prolong_blocks,
    coarse_inverse,
):
    levels = galerkin_cols.shape[0]
    count = galerkin_cols.shape[2]
    size = galerkin_blocks.shape[-1]
    rows, fields = level_rhs.shape[1:]
    half = fields // 2
    width = half // 2
    rcols = restrict_cols.transpose(0, 3, 1, 2), scalars()
    pcols = prolong_cols.transpose(0, 1, 3, 2), scalars()
    square_shape = array((rows, rows), bf16)
    operator_shapes = [square_shape, array((rows, 2 * size), bf16), array((rows, 1), f32)]
    rmat_shape = array((rows, 2 * rows), bf16)
    chunk_shape = array((rows, width), bf16)
    real_shape = array((rows, width), f32)
    held = [pltpu.VMEM((rows, rows), bf16)]

    def ends_shape(columns):
        return array((size, columns), bf16)

    def of_level(value, level_idx):
        return value, level_block(value, level_idx)

    def flops(columns, products=1):
        return 2 * products * rows * rows * columns

    def place_of(far, given):
        return (0, far, half), (1, given, width)

    pairs = [(place_of(1, given), place_of(0, given)) for given in (1, 0)]
    gcols, inner, *outers = run(
        functools.partial(start_kernel, pairs), "start",
        [array(galerkin_cols.shape, jnp.int32), ends_shape(fields)] + [ends_shape(half)] * 2,
        [in_hbm(level_rhs), in_hbm(galerkin_blocks), in_hbm(galerkin_cols)],
        scratch=[
            pltpu.VMEM((2, size, fields), f32), pltpu.VMEM((size, fields), bf16),
            pltpu.VMEM((2, size, size), bf16), pltpu.SemaphoreType.DMA((5,)),
        ],
    )
    gcols = in_vmem(gcols), scalars()
    first = outers[0]
    outers = [swap_outer(outer) for outer in outers]
    inner = exchange(inner, "narrow", 1)
    rest, base, local, rim, scale = run(
        first_local_kernel, "first_local", [array((rows, fields), f32)] * 2 + operator_shapes,
        [level_rhs, first, gcols, of_level(galerkin_blocks, 0)], flops=flops(fields),
    )
    operators = [(scale, local)]
    sent, kept = [], []
    for places, outer in zip(pairs, outers):
        far, near = run(
            functools.partial(first_residual_kernel, places), "first_residual", [chunk_shape] * 2,
            [rest, rim, outer, inner],
        )
        sent.append(far)
        kept.append(near)
    last = levels - 1
    bases = []
    anchor = sent[0]
    pieces = lax.axis_size("narrow")
    for level_idx in range(levels - 1):
        other = [exchange(value, "wide", 1 << level_idx) for value in sent]
        rmat, local, rim, scale = run(
            functools.partial(operators_kernel, level_idx), "operators",
            [rmat_shape] + operator_shapes,
            [anchor, rcols, of_level(restrict_blocks, level_idx),
             gcols, of_level(galerkin_blocks, level_idx + 1)],
        )
        operators.append((scale, local))
        joined = []
        for near, far in zip(kept, other):
            rhs, smoothed, *ends = run(
                functools.partial(join_kernel, level_idx), "join",
                [real_shape, chunk_shape] + [ends_shape(width)] * 2,
                [rmat, near, far, scale], flops=flops(width, 2),
            )
            inner, outer = exchange(ends[0], "narrow", 1), swap_outer(ends[1])
            joined.append((smoothed, rhs, scale, rim, outer, inner))
            anchor = smoothed
        share = []
        if level_idx + 1 == last:
            share = run(
                functools.partial(share_kernel, last), "share", [square_shape],
                [anchor, rcols, of_level(restrict_blocks, last)],
            )
        made = []
        for smoothed, rhs, *operands in joined:
            (left,) = run(
                local_kernel, "local", [real_shape], [rhs, smoothed, local, *made], flops=flops(width)
            )
            value, made_base = run(
                last_residual_kernel if share else residual_kernel, "residual",
                [chunk_shape, real_shape if made or level_idx else chunk_shape],
                [rhs, left, *operands, *(share or [anchor])],
                flops=flops(width, 2) if not made else late_cost,
            )
            made.append(value)
            bases.append(made_base)
        sent, kept = made[:1], made[-1:]
        anchor = made[0]
    (mine,) = kept
    far_parts = {o: exchange_both(mine, 1 << last, o) for o in range(0, pieces, 2)}
    far_base = exchange(bases[0], "wide", 1)
    own_parts = {o: exchange(mine, "narrow", o) if o else mine for o in range(0, pieces, 2)}
    coarse_mat, *ups = run(
        functools.partial(coarse_operators_kernel, 2, levels), "coarse_operators",
        [array((rows, pieces * rows), bf16)] + [square_shape] * (levels - 3),
        [mine, far_base, pcols, coarse_inverse]
        + [of_level(prolong_blocks, idx) for idx in range(2, levels)]
        + [value for pair in operators[2:] for value in pair],
        flops=flops(rows, 2 * (levels - 2) + pieces), scratch=held,
    )
    places = [place_of(0, 1), place_of(1, 1)]
    lower, upper, both, total = run(
        functools.partial(fine_operators_kernel, places), "fine_operators",
        [square_shape] * 3 + [array((rows, half), f32)],
        [mine, pcols, of_level(prolong_blocks, 0), of_level(prolong_blocks, 1),
         *operators[0], *operators[1], base, bases[0], far_base],
        flops=flops(rows, 4), scratch=held,
    )
    parts = {}
    for offset in reversed(range(0, pieces, 2)):
        (parts[offset],) = run(
            share_sum_kernel, "share_sum", [chunk_shape],
            [far_parts[offset], own_parts[offset], coarse_mat, upper],
        )
    offsets = tuple(parts)
    (value,) = run(
        functools.partial(coarse_kernel, offsets), "coarse", [real_shape],
        [coarse_mat] + [parts[o] for o in offsets] + [bases[-1]], flops=flops(width, len(offsets)),
    )
    parts = {o + 1: exchange(parts[o], "narrow", 1) for o in reversed(offsets)}
    offsets = tuple(parts)
    operands = [coarse_mat] + [parts[o] for o in offsets] + [value]
    for idx in reversed(range(2, last)):
        operands += [bases[idx], ups[idx - 2]]
    value, near = run(
        functools.partial(up_kernel, offsets), "up", [chunk_shape] * 2,
        operands + [bases[1], upper], flops=flops(width, len(offsets) + levels - 2),
    )
    diagonal, other = (exchange(value, "wide", bits) for bits in (3, 2))
    far = exchange(near, "wide", 1)
    result = None
    for group in (
        [(near, place_of(0, 0), None)],
        [(diagonal, place_of(1, 1), 1)],
        [(other, place_of(0, 1), 0), (far, place_of(1, 0), None)],
    ):
        values, places, slots = zip(*group)
        operands = [*values, base, lower, total, both]
        aliases = {}
        if result is not None:
            aliases[len(operands)] = 0
            operands.append(in_hbm(result))
        (result,) = run(
            functools.partial(output_kernel, places, slots),
            "output", [array((1, rows, fields), f32)], operands,
            flops=flops(width, len(group)), out_space=pltpu.HBM, aliases=aliases,
            scratch=[
                pltpu.VMEM((len(group), rows, width), f32), pltpu.SemaphoreType.DMA((len(group),))
            ],
        )
    return result


def solution(mesh):
    in_specs = (
        P("wide", "narrow", None),
        P(None, "wide", "narrow", None),
        P(None, "wide", "narrow", None, None, None),
        P(None, "wide", "narrow", None),
        P(None, "wide", "narrow", None, None, None),
        P(None, "wide", "narrow", None),
        P(None, "wide", "narrow", None, None, None),
        P("narrow", None),
    )
    out_specs = P("wide", "narrow", None)
    return jax.shard_map(
        on_device, mesh=mesh, in_specs=in_specs, out_specs=out_specs, check_vma=False
    )
```

```python
import functools

import jax
import jax.numpy as jnp
from jax import lax
from jax.experimental import pallas as pl
from jax.experimental.pallas import tpu as pltpu
from jax.sharding import PartitionSpec as P

relax_down = 0.7
relax_up = 0.5
f32 = jnp.float32
bf16 = jnp.bfloat16
grant = 12 * 1024 * 1024
late_cost = 4 * 10**9


def matmul(a, b):
    return jnp.dot(a, b, preferred_element_type=f32)


def array(shape, dtype):
    return jax.ShapeDtypeStruct(shape, dtype)


def whole():
    return pl.BlockSpec(memory_space=pltpu.VMEM)


def level_block(value, level_idx):
    shape = (1,) + value.shape[1:]
    return pl.BlockSpec(shape, lambda i: (level_idx,) + (0,) * (value.ndim - 1))


def scalars():
    return pl.BlockSpec(memory_space=pltpu.SMEM)


def in_hbm(value):
    return pltpu.with_memory_space_constraint(value, pltpu.HBM), pl.BlockSpec(memory_space=pltpu.HBM)


def in_vmem(value):
    return pltpu.with_memory_space_constraint(value, pltpu.VMEM)


def run(body, name, outs, operands, flops=0, scratch=(), out_space=pltpu.VMEM, aliases=None):
    arrays = [o[0] if isinstance(o, tuple) else in_vmem(o) for o in operands]
    specs = [o[1] if isinstance(o, tuple) else whole() for o in operands]
    windows = any(isinstance(o, tuple) and o[1].block_shape is not None for o in operands)
    moved = sum(a.size * a.dtype.itemsize for a in arrays)
    return pl.pallas_call(
        body,
        grid=(1,) if windows else (),
        out_shape=[out_space(o.shape, o.dtype) for o in outs],
        in_specs=specs,
        out_specs=[pl.BlockSpec(memory_space=out_space)] * len(outs),
        input_output_aliases=aliases or {},
        scratch_shapes=list(scratch),
        compiler_params=pltpu.CompilerParams(vmem_limit_bytes=grant),
        cost_estimate=pl.CostEstimate(flops=flops, bytes_accessed=moved, transcendentals=0),
        name=name,
    )(*arrays)


def diagonal_of(block):
    size = block.shape[0]
    rows = lax.broadcasted_iota(jnp.int32, (size, size), 0)
    lanes = lax.broadcasted_iota(jnp.int32, (size, size), 1)
    return jnp.sum(jnp.where(rows == lanes, block, 0.0), axis=1, keepdims=True)


def placed(base, others, ids, target):
    total = base
    for block, ident in zip(others, ids):
        term = block * jnp.where(ident == target, 1.0, 0.0).astype(f32)
        total = term if total is None else total + term
    return total


def parity_of():
    return lax.rem(lax.axis_index("narrow"), 2)


def put_ends(first, last, inner_ref, outer_ref):
    even = parity_of() == 0
    inner_ref[...] = jnp.where(even, last, first)
    outer_ref[...] = jnp.where(even, first, last)


def assemble_galerkin(level_idx, cols, blocks, local_ref, rim_ref, scale_ref):
    count, slots, size = blocks.shape[2], blocks.shape[3], blocks.shape[4]
    parity = parity_of()
    piece = lax.axis_index("narrow")
    last = lax.axis_size("narrow") - 1
    inside = jnp.where((piece == 0) | (piece == last), 0.0, 1.0).astype(f32)
    for b in range(count):
        held = [blocks[0, 0, b, s].astype(f32) for s in range(slots)]
        ids = [cols[level_idx, 0, b, s] for s in range(1, slots)]
        rows = pl.ds(b * size, size)
        scale_ref[rows, :] = 1.0 / diagonal_of(held[0])
        line = [placed(held[0] if c == b else None, held[1:], ids, c) for c in range(count)]
        local_ref[rows, :] = jnp.concatenate(line, axis=1).astype(bf16)
        rims = [
            placed(None, held[1:], ids, count + 1 - parity),
            placed(None, held[1:], ids, count + parity) * inside,
        ]
        rim_ref[rows, :] = jnp.concatenate(rims, axis=1).astype(bf16)


def assemble_restrict(level_idx, cols, blocks, out_ref):
    count, slots, size = blocks.shape[2], blocks.shape[3], blocks.shape[4]
    for b in range(count):
        held = [blocks[0, 0, b, s].astype(f32) for s in range(slots)]
        ids = [cols[level_idx, s, 0, b] for s in range(2, slots)]
        fixed = {b: held[0], count + b: held[1]}
        line = [placed(fixed.get(c), held[2:], ids, c) for c in range(2 * count)]
        out_ref[pl.ds(b * size, size), :] = jnp.concatenate(line, axis=1).astype(bf16)


def assemble_share(level_idx, cols, blocks, out_ref):
    count, slots, size = blocks.shape[2], blocks.shape[3], blocks.shape[4]
    bit = bit_of(level_idx)
    for b in range(count):
        held = [blocks[0, 0, b, s].astype(f32) for s in range(slots)]
        ids = [cols[level_idx, s, 0, b] for s in range(2, slots)]
        own = jnp.where(bit == 0, held[0], held[1])
        first = bit * count
        line = [placed(own if c == b else None, held[2:], ids, first + c) for c in range(count)]
        out_ref[pl.ds(b * size, size), :] = jnp.concatenate(line, axis=1).astype(bf16)


def assemble_prolong(level_idx, cols, blocks, out_ref):
    count, slots, size = blocks.shape[2], blocks.shape[3], blocks.shape[4]
    for b in range(count):
        held = [blocks[0, 0, b, s].astype(f32) for s in range(slots)]
        ids = [cols[level_idx, 0, s, b] for s in range(1, slots)]
        line = [placed(held[0] if c == b else None, held[1:], ids, c) for c in range(count)]
        out_ref[pl.ds(b * size, size), :] = jnp.concatenate(line, axis=1).astype(bf16)


def start_kernel(places, rhs, blocks, *refs):
    table, held, inner_ref, *outers, rows, outer, pivots, sems = refs
    count, size = blocks.shape[2], blocks.shape[4]
    copies = []
    for slot, which in enumerate((0, count - 1)):
        source = rhs.at[0, pl.ds(which * size, size), :]
        copies.append(pltpu.make_async_copy(source, rows.at[slot], sems.at[slot]))
        source = blocks.at[0, 0, which, 0]
        copies.append(pltpu.make_async_copy(source, pivots.at[slot], sems.at[2 + slot]))
    copies.append(pltpu.make_async_copy(table, held, sems.at[4]))
    for copy in copies:
        copy.start()
    for copy in copies:
        copy.wait()
    first, last = (
        (rows[slot] * (relax_down / diagonal_of(pivots[slot].astype(f32)))).astype(bf16)
        for slot in range(2)
    )
    put_ends(first, last, inner_ref, outer)
    for ref, pair in zip(outers, places):
        width = ref.shape[1] // 2
        for slot, place in enumerate(pair):
            ref[:, slot * width : (slot + 1) * width] = outer[:, lanes_of(place, width)]


def first_local_kernel(rhs, _, cols, blocks, rest, base, local, rim, scale):
    assemble_galerkin(0, cols, blocks, local, rim, scale)
    smoothed = rhs[0] * (relax_down * scale[...])
    left = rhs[0] - matmul(local[...], smoothed.astype(bf16))
    rest[...] = left
    base[...] = smoothed + (relax_up * scale[...]) * left


def bit_of(level_idx):
    return lax.axis_index("wide") >> level_idx & 1


def lanes_of(place, width):
    start = 0
    for level_idx, flip, step in place:
        start = start + (bit_of(level_idx) ^ flip) * step
    return pl.ds(pl.multiple_of(start, width), width)


def first_residual_kernel(places, rest, rim, outer, inner, *refs):
    width = refs[-1].shape[1]
    for slot, (ref, place) in enumerate(zip(refs[-2:], places)):
        lanes = lanes_of(place, width)
        columns = pl.ds(slot * width, width)
        rims = jnp.concatenate([inner[:, lanes], outer[:, columns]], axis=0)
        ref[...] = (rest[:, lanes] - matmul(rim[...], rims)).astype(bf16)


def residual_kernel(rhs, smoothed, scale, local, rim, outer, inner, _, out, base):
    rims = jnp.concatenate([inner[...], outer[...]], axis=0)
    left = rhs[...] - matmul(local[...], smoothed[...])
    out[...] = (left - matmul(rim[...], rims)).astype(bf16)
    made = rhs[...] * (relax_down * scale[...]) + (relax_up * scale[...]) * left
    base[...] = made.astype(base.dtype)


def last_residual_kernel(rhs, smoothed, scale, local, rim, outer, inner, share, out, base):
    rims = jnp.concatenate([inner[...], outer[...]], axis=0)
    left = rhs[...] - matmul(local[...], smoothed[...])
    residual = (left - matmul(rim[...], rims)).astype(bf16)
    out[...] = matmul(share[...], residual).astype(bf16)
    base[...] = rhs[...] * (relax_down * scale[...]) + (relax_up * scale[...]) * left


def share_kernel(level_idx, _, rcols, rblocks, share):
    assemble_share(level_idx, rcols, rblocks, share)


def operators_kernel(level_idx, _, rcols, rblocks, cols, blocks, rmat, local, rim, scale):
    assemble_restrict(level_idx, rcols, rblocks, rmat)
    assemble_galerkin(level_idx + 1, cols, blocks, local, rim, scale)


def raising(level_idx, pcols, blocks, local, scale, held):
    assemble_prolong(level_idx, pcols, blocks, held)
    applied = matmul(local[...], held[...])
    return (held[...].astype(f32) - (relax_up * scale[...]) * applied).astype(bf16)


def coarse_operators_kernel(first, levels, *refs):
    _, _, pcols, inverse, *refs = refs
    places = range(first, levels)
    blocks, refs = refs[: len(places)], refs[len(places) :]
    pairs, refs = refs[: 2 * len(places)], refs[2 * len(places) :]
    coarse, *up, held = refs
    for idx in places:
        slot = idx - first
        made = raising(idx, pcols, blocks[slot], pairs[2 * slot + 1], pairs[2 * slot], held)
        if idx == levels - 1:
            coarse[...] = matmul(made, inverse[...]).astype(bf16)
        else:
            up[slot][...] = made


def fine_operators_kernel(
    places, _, pcols, blocks_0, blocks_1, scale_0, local_0, scale_1, local_1,
    base, near, far, lower, upper, both, total, held,
):
    lower[...] = raising(0, pcols, blocks_0, local_0, scale_0, held)
    upper[...] = raising(1, pcols, blocks_1, local_1, scale_1, held)
    both[...] = matmul(lower[...], upper[...]).astype(bf16)
    width = near.shape[1]
    for slot, (place, source) in enumerate(zip(places, (near, far))):
        made = base[:, lanes_of(place, width)] + matmul(lower[...], source[...])
        total[:, slot * width : (slot + 1) * width] = made


def restricted(level_idx, rmat, kept, other):
    width = rmat.shape[1] // 2
    own = pl.multiple_of(bit_of(level_idx) * width, width)
    far = pl.multiple_of((1 - bit_of(level_idx)) * width, width)
    total = matmul(rmat[:, pl.ds(own, width)], kept[...])
    return total + matmul(rmat[:, pl.ds(far, width)], other[...])


def join_kernel(level_idx, rmat, kept, other, scale, rhs, smoothed, inner_ref, outer_ref):
    size = inner_ref.shape[0]
    current = restricted(level_idx, rmat, kept, other)
    rhs[...] = current
    rounded = (current * (relax_down * scale[...])).astype(bf16)
    smoothed[...] = rounded
    put_ends(rounded[:size], rounded[-size:], inner_ref, outer_ref)


def inverse_part(inverse, part, offset):
    depth = part.shape[0]
    piece = lax.axis_index("narrow") ^ offset
    return matmul(inverse[:, pl.ds(pl.multiple_of(piece * depth, depth), depth)], part[...])


def share_sum_kernel(far, own, *refs):
    refs[-1][...] = (far[...].astype(f32) + own[...].astype(f32)).astype(bf16)


def coarse_kernel(offsets, inverse, *refs):
    *parts, value, out = refs
    value = value[...]
    for part, offset in zip(parts, offsets):
        value = value + inverse_part(inverse, part, offset)
    out[...] = value


def up_kernel(offsets, inverse, *refs):
    value = refs[len(offsets)][...]
    for part, offset in zip(refs, offsets):
        value = value + inverse_part(inverse, part, offset)
    refs = refs[len(offsets) + 1 :]
    refs, (base, up, coarse, raised) = refs[:-4], refs[-4:]
    for step in range(len(refs) // 2):
        value = refs[2 * step][...] + matmul(refs[2 * step + 1][...], value.astype(bf16))
    value = value.astype(bf16)
    coarse[...] = value
    raised[...] = (base[...] + matmul(up[...], value)).astype(bf16)


def output_kernel(places, slots, *refs):
    coarse, (base, lower, total, both) = refs[: len(places)], refs[len(places) : len(places) + 4]
    out, made, sems = refs[-3:]
    copies = []
    for item, (place, value) in enumerate(zip(places, coarse)):
        width = value.shape[1]
        lanes = lanes_of(place, width)
        if slots[item] is None:
            made[item] = base[:, lanes] + matmul(lower[...], value[...])
        else:
            held = total[:, slots[item] * width : (slots[item] + 1) * width]
            made[item] = held + matmul(both[...], value[...])
        copy = pltpu.make_async_copy(made.at[item], out.at[0, :, lanes], sems.at[item])
        copy.start()
        copies.append(copy)
    for copy in copies:
        copy.wait()


def exchange(value, axis, bit):
    count = lax.axis_size(axis)
    return lax.ppermute(value, axis, [(i, i ^ bit) for i in range(count)])


def exchange_both(value, bit, offset):
    wide, narrow = lax.axis_size("wide"), lax.axis_size("narrow")
    pairs = [
        (w * narrow + j, (w ^ bit) * narrow + (j ^ offset))
        for w in range(wide) for j in range(narrow)
    ]
    return lax.ppermute(value, ("wide", "narrow"), pairs)


def swap_outer(outer):
    count = lax.axis_size("narrow")
    gaps = [(i, (i + 1 if i % 2 else i - 1) % count) for i in range(count)]
    return lax.ppermute(outer, "narrow", gaps)


def on_device(
    level_rhs,
    galerkin_cols,
    galerkin_blocks,
    restrict_cols,
    restrict_blocks,
    prolong_cols,
    prolong_blocks,
    coarse_inverse,
):
    levels = galerkin_cols.shape[0]
    count = galerkin_cols.shape[2]
    size = galerkin_blocks.shape[-1]
    rows, fields = level_rhs.shape[1:]
    half = fields // 2
    width = half // 2
    rcols = restrict_cols.transpose(0, 3, 1, 2), scalars()
    pcols = prolong_cols.transpose(0, 1, 3, 2), scalars()
    square_shape = array((rows, rows), bf16)
    operator_shapes = [square_shape, array((rows, 2 * size), bf16), array((rows, 1), f32)]
    rmat_shape = array((rows, 2 * rows), bf16)
    chunk_shape = array((rows, width), bf16)
    real_shape = array((rows, width), f32)
    held = [pltpu.VMEM((rows, rows), bf16)]

    def ends_shape(columns):
        return array((size, columns), bf16)

    def of_level(value, level_idx):
        return value, level_block(value, level_idx)

    def flops(columns, products=1):
        return 2 * products * rows * rows * columns

    def place_of(far, given):
        return (0, far, half), (1, given, width)

    pairs = [(place_of(1, given), place_of(0, given)) for given in (1, 0)]
    gcols, inner, *outers = run(
        functools.partial(start_kernel, pairs), "start",
        [array(galerkin_cols.shape, jnp.int32), ends_shape(fields)] + [ends_shape(half)] * 2,
        [in_hbm(level_rhs), in_hbm(galerkin_blocks), in_hbm(galerkin_cols)],
        scratch=[
            pltpu.VMEM((2, size, fields), f32), pltpu.VMEM((size, fields), bf16),
            pltpu.VMEM((2, size, size), bf16), pltpu.SemaphoreType.DMA((5,)),
        ],
    )
    gcols = in_vmem(gcols), scalars()
    first = outers[0]
    outers = [swap_outer(outer) for outer in outers]
    inner = exchange(inner, "narrow", 1)
    rest, base, local, rim, scale = run(
        first_local_kernel, "first_local", [array((rows, fields), f32)] * 2 + operator_shapes,
        [level_rhs, first, gcols, of_level(galerkin_blocks, 0)], flops=flops(fields),
    )
    operators = [(scale, local)]
    first_operands = [rest, rim, inner]

    def first_chunk(slot, after):
        rest, rim, inner = first_operands
        return run(
            functools.partial(first_residual_kernel, pairs[slot]), "first_residual",
            [chunk_shape] * 2, [rest, rim, outers[slot], inner, *after],
        )

    sent, kept = zip(first_chunk(0, ()))
    last = levels - 1
    bases = []
    anchor = sent[0]
    pieces = lax.axis_size("narrow")
    for level_idx in range(levels - 1):
        other = [exchange(value, "wide", 1 << level_idx) for value in sent]
        rmat, local, rim, scale = run(
            functools.partial(operators_kernel, level_idx), "operators",
            [rmat_shape] + operator_shapes,
            [anchor, rcols, of_level(restrict_blocks, level_idx),
             gcols, of_level(galerkin_blocks, level_idx + 1)],
        )
        operators.append((scale, local))
        if level_idx == 0:
            far, near = first_chunk(1, [scale])
            other.append(exchange(far, "wide", 1))
            kept = [kept[0], near]
        joined = []
        for near, far in zip(kept, other):
            rhs, smoothed, *ends = run(
                functools.partial(join_kernel, level_idx), "join",
                [real_shape, chunk_shape] + [ends_shape(width)] * 2,
                [rmat, near, far, scale], flops=flops(width, 2),
            )
            inner, outer = exchange(ends[0], "narrow", 1), swap_outer(ends[1])
            joined.append((rhs, smoothed, scale, local, rim, outer, inner))
        share = []
        if level_idx + 1 == last:
            share = run(
                functools.partial(share_kernel, last), "share", [square_shape],
                [joined[0][1], rcols, of_level(restrict_blocks, last)],
            )
        made = []
        for operands in joined:
            value, made_base = run(
                last_residual_kernel if share else residual_kernel, "residual",
                [chunk_shape, real_shape if made or level_idx else chunk_shape],
                [*operands, *(share or [joined[-1][1]])],
                flops=flops(width, 2) if not made else late_cost,
            )
            made.append(value)
            bases.append(made_base)
        sent, kept = made[:1], made[-1:]
        anchor = made[0]
    (mine,) = kept
    far_parts = {o: exchange_both(mine, 1 << last, o) for o in range(0, pieces, 2)}
    far_base = exchange(bases[0], "wide", 1)
    own_parts = {o: exchange(mine, "narrow", o) if o else mine for o in range(0, pieces, 2)}
    coarse_mat, *ups = run(
        functools.partial(coarse_operators_kernel, 2, levels), "coarse_operators",
        [array((rows, pieces * rows), bf16)] + [square_shape] * (levels - 3),
        [mine, far_base, pcols, coarse_inverse]
        + [of_level(prolong_blocks, idx) for idx in range(2, levels)]
        + [value for pair in operators[2:] for value in pair],
        flops=flops(rows, 2 * (levels - 2) + pieces), scratch=held,
    )
    places = [place_of(0, 1), place_of(1, 1)]
    lower, upper, both, total = run(
        functools.partial(fine_operators_kernel, places), "fine_operators",
        [square_shape] * 3 + [array((rows, half), f32)],
        [mine, pcols, of_level(prolong_blocks, 0), of_level(prolong_blocks, 1),
         *operators[0], *operators[1], base, bases[0], far_base],
        flops=flops(rows, 4), scratch=held,
    )
    parts = {}
    for offset in reversed(range(0, pieces, 2)):
        (parts[offset],) = run(
            share_sum_kernel, "share_sum", [chunk_shape],
            [far_parts[offset], own_parts[offset], coarse_mat, upper],
        )
    offsets = tuple(parts)
    (value,) = run(
        functools.partial(coarse_kernel, offsets), "coarse", [real_shape],
        [coarse_mat] + [parts[o] for o in offsets] + [bases[-1]], flops=flops(width, len(offsets)),
    )
    parts = {o + 1: exchange(parts[o], "narrow", 1) for o in reversed(offsets)}
    offsets = tuple(parts)
    operands = [coarse_mat] + [parts[o] for o in offsets] + [value]
    for idx in reversed(range(2, last)):
        operands += [bases[idx], ups[idx - 2]]
    value, near = run(
        functools.partial(up_kernel, offsets), "up", [chunk_shape] * 2,
        operands + [bases[1], upper], flops=flops(width, len(offsets) + levels - 2),
    )
    diagonal, other = (exchange(value, "wide", bits) for bits in (3, 2))
    far = exchange(near, "wide", 1)
    result = None
    for group in (
        [(near, place_of(0, 0), None)],
        [(diagonal, place_of(1, 1), 1)],
        [(other, place_of(0, 1), 0), (far, place_of(1, 0), None)],
    ):
        values, places, slots = zip(*group)
        operands = [*values, base, lower, total, both]
        aliases = {}
        if result is not None:
            aliases[len(operands)] = 0
            operands.append(in_hbm(result))
        (result,) = run(
            functools.partial(output_kernel, places, slots),
            "output", [array((1, rows, fields), f32)], operands,
            flops=flops(width, len(group)), out_space=pltpu.HBM, aliases=aliases,
            scratch=[
                pltpu.VMEM((len(group), rows, width), f32), pltpu.SemaphoreType.DMA((len(group),))
            ],
        )
    return result


def solution(mesh):
    in_specs = (
        P("wide", "narrow", None),
        P(None, "wide", "narrow", None),
        P(None, "wide", "narrow", None, None, None),
        P(None, "wide", "narrow", None),
        P(None, "wide", "narrow", None, None, None),
        P(None, "wide", "narrow", None),
        P(None, "wide", "narrow", None, None, None),
        P("narrow", None),
    )
    out_specs = P("wide", "narrow", None)
    return jax.shard_map(
        on_device, mesh=mesh, in_specs=in_specs, out_specs=out_specs, check_vma=False
    )
```

```python
import functools

import jax
import jax.numpy as jnp
from jax import lax
from jax.experimental import pallas as pl
from jax.experimental.pallas import tpu as pltpu
from jax.sharding import PartitionSpec as P

relax_down = 0.7
relax_up = 0.5
f32 = jnp.float32
bf16 = jnp.bfloat16
grant = 12 * 1024 * 1024
late_cost = 4 * 10**9


def matmul(a, b):
    return jnp.dot(a, b, preferred_element_type=f32)


def array(shape, dtype):
    return jax.ShapeDtypeStruct(shape, dtype)


def whole():
    return pl.BlockSpec(memory_space=pltpu.VMEM)


def level_block(value, level_idx):
    shape = (1,) + value.shape[1:]
    return pl.BlockSpec(shape, lambda i: (level_idx,) + (0,) * (value.ndim - 1))


def scalars():
    return pl.BlockSpec(memory_space=pltpu.SMEM)


def in_hbm(value):
    return pltpu.with_memory_space_constraint(value, pltpu.HBM), pl.BlockSpec(memory_space=pltpu.HBM)


def in_vmem(value):
    return pltpu.with_memory_space_constraint(value, pltpu.VMEM)


def run(body, name, outs, operands, flops=0, scratch=(), out_space=pltpu.VMEM, aliases=None):
    arrays = [o[0] if isinstance(o, tuple) else in_vmem(o) for o in operands]
    specs = [o[1] if isinstance(o, tuple) else whole() for o in operands]
    windows = any(isinstance(o, tuple) and o[1].block_shape is not None for o in operands)
    moved = sum(a.size * a.dtype.itemsize for a in arrays)
    return pl.pallas_call(
        body,
        grid=(1,) if windows else (),
        out_shape=[out_space(o.shape, o.dtype) for o in outs],
        in_specs=specs,
        out_specs=[pl.BlockSpec(memory_space=out_space)] * len(outs),
        input_output_aliases=aliases or {},
        scratch_shapes=list(scratch),
        compiler_params=pltpu.CompilerParams(vmem_limit_bytes=grant),
        cost_estimate=pl.CostEstimate(flops=flops, bytes_accessed=moved, transcendentals=0),
        name=name,
    )(*arrays)


def diagonal_of(block):
    size = block.shape[0]
    rows = lax.broadcasted_iota(jnp.int32, (size, size), 0)
    lanes = lax.broadcasted_iota(jnp.int32, (size, size), 1)
    return jnp.sum(jnp.where(rows == lanes, block, 0.0), axis=1, keepdims=True)


def placed(base, others, ids, target):
    total = base
    for block, ident in zip(others, ids):
        term = block * jnp.where(ident == target, 1.0, 0.0).astype(f32)
        total = term if total is None else total + term
    return total


def parity_of():
    return lax.rem(lax.axis_index("narrow"), 2)


def put_ends(first, last, inner_ref, outer_ref):
    even = parity_of() == 0
    inner_ref[...] = jnp.where(even, last, first)
    outer_ref[...] = jnp.where(even, first, last)


def assemble_galerkin(level_idx, cols, blocks, local_ref, rim_ref, scale_ref):
    count, slots, size = blocks.shape[2], blocks.shape[3], blocks.shape[4]
    parity = parity_of()
    piece = lax.axis_index("narrow")
    last = lax.axis_size("narrow") - 1
    inside = jnp.where((piece == 0) | (piece == last), 0.0, 1.0).astype(f32)
    for b in range(count):
        held = [blocks[0, 0, b, s].astype(f32) for s in range(slots)]
        ids = [cols[level_idx, 0, b, s] for s in range(1, slots)]
        rows = pl.ds(b * size, size)
        scale_ref[rows, :] = 1.0 / diagonal_of(held[0])
        line = [placed(held[0] if c == b else None, held[1:], ids, c) for c in range(count)]
        local_ref[rows, :] = jnp.concatenate(line, axis=1).astype(bf16)
        rims = [
            placed(None, held[1:], ids, count + 1 - parity),
            placed(None, held[1:], ids, count + parity) * inside,
        ]
        rim_ref[rows, :] = jnp.concatenate(rims, axis=1).astype(bf16)


def assemble_restrict(level_idx, cols, blocks, out_ref):
    count, slots, size = blocks.shape[2], blocks.shape[3], blocks.shape[4]
    for b in range(count):
        held = [blocks[0, 0, b, s].astype(f32) for s in range(slots)]
        ids = [cols[level_idx, s, 0, b] for s in range(2, slots)]
        fixed = {b: held[0], count + b: held[1]}
        line = [placed(fixed.get(c), held[2:], ids, c) for c in range(2 * count)]
        out_ref[pl.ds(b * size, size), :] = jnp.concatenate(line, axis=1).astype(bf16)


def assemble_share(level_idx, cols, blocks, out_ref):
    count, slots, size = blocks.shape[2], blocks.shape[3], blocks.shape[4]
    bit = bit_of(level_idx)
    for b in range(count):
        held = [blocks[0, 0, b, s].astype(f32) for s in range(slots)]
        ids = [cols[level_idx, s, 0, b] for s in range(2, slots)]
        own = jnp.where(bit == 0, held[0], held[1])
        first = bit * count
        line = [placed(own if c == b else None, held[2:], ids, first + c) for c in range(count)]
        out_ref[pl.ds(b * size, size), :] = jnp.concatenate(line, axis=1).astype(bf16)


def assemble_prolong(level_idx, cols, blocks, out_ref):
    count, slots, size = blocks.shape[2], blocks.shape[3], blocks.shape[4]
    for b in range(count):
        held = [blocks[0, 0, b, s].astype(f32) for s in range(slots)]
        ids = [cols[level_idx, 0, s, b] for s in range(1, slots)]
        line = [placed(held[0] if c == b else None, held[1:], ids, c) for c in range(count)]
        out_ref[pl.ds(b * size, size), :] = jnp.concatenate(line, axis=1).astype(bf16)


def start_kernel(places, rhs, blocks, *refs):
    table, held, inner_ref, *outers, rows, outer, pivots, sems = refs
    count, size = blocks.shape[2], blocks.shape[4]
    copies = []
    for slot, which in enumerate((0, count - 1)):
        source = rhs.at[0, pl.ds(which * size, size), :]
        copies.append(pltpu.make_async_copy(source, rows.at[slot], sems.at[slot]))
        source = blocks.at[0, 0, which, 0]
        copies.append(pltpu.make_async_copy(source, pivots.at[slot], sems.at[2 + slot]))
    copies.append(pltpu.make_async_copy(table, held, sems.at[4]))
    for copy in copies:
        copy.start()
    for copy in copies:
        copy.wait()
    first, last = (
        (rows[slot] * (relax_down / diagonal_of(pivots[slot].astype(f32)))).astype(bf16)
        for slot in range(2)
    )
    put_ends(first, last, inner_ref, outer)
    for ref, pair in zip(outers, places):
        width = ref.shape[1] // 2
        for slot, place in enumerate(pair):
            ref[:, slot * width : (slot + 1) * width] = outer[:, lanes_of(place, width)]


def first_local_kernel(rhs, _, cols, blocks, rest, base, local, rim, scale):
    assemble_galerkin(0, cols, blocks, local, rim, scale)
    smoothed = rhs[0] * (relax_down * scale[...])
    left = rhs[0] - matmul(local[...], smoothed.astype(bf16))
    rest[...] = left
    base[...] = smoothed + (relax_up * scale[...]) * left


def bit_of(level_idx):
    return lax.axis_index("wide") >> level_idx & 1


def lanes_of(place, width):
    start = 0
    for level_idx, flip, step in place:
        start = start + (bit_of(level_idx) ^ flip) * step
    return pl.ds(pl.multiple_of(start, width), width)


def first_residual_kernel(places, rest, rim, outer, inner, *refs):
    width = refs[0].shape[1]
    for slot, (ref, place) in enumerate(zip(refs, places)):
        lanes = lanes_of(place, width)
        columns = pl.ds(slot * width, width)
        rims = jnp.concatenate([inner[:, lanes], outer[:, columns]], axis=0)
        ref[...] = (rest[:, lanes] - matmul(rim[...], rims)).astype(bf16)


def residual_kernel(rhs, smoothed, scale, local, rim, outer, inner, _, out, base):
    rims = jnp.concatenate([inner[...], outer[...]], axis=0)
    left = rhs[...] - matmul(local[...], smoothed[...])
    out[...] = (left - matmul(rim[...], rims)).astype(bf16)
    made = rhs[...] * (relax_down * scale[...]) + (relax_up * scale[...]) * left
    base[...] = made.astype(base.dtype)


def last_residual_kernel(rhs, smoothed, scale, local, rim, outer, inner, share, out, base):
    rims = jnp.concatenate([inner[...], outer[...]], axis=0)
    left = rhs[...] - matmul(local[...], smoothed[...])
    residual = (left - matmul(rim[...], rims)).astype(bf16)
    out[...] = matmul(share[...], residual).astype(bf16)
    base[...] = rhs[...] * (relax_down * scale[...]) + (relax_up * scale[...]) * left


def share_kernel(level_idx, _, rcols, rblocks, share):
    assemble_share(level_idx, rcols, rblocks, share)


def operators_kernel(level_idx, _, rcols, rblocks, cols, blocks, rmat, local, rim, scale):
    assemble_restrict(level_idx, rcols, rblocks, rmat)
    assemble_galerkin(level_idx + 1, cols, blocks, local, rim, scale)


def raising(level_idx, pcols, blocks, local, scale, held):
    assemble_prolong(level_idx, pcols, blocks, held)
    applied = matmul(local[...], held[...])
    return (held[...].astype(f32) - (relax_up * scale[...]) * applied).astype(bf16)


def coarse_operators_kernel(first, levels, *refs):
    _, _, pcols, inverse, *refs = refs
    places = range(first, levels)
    blocks, refs = refs[: len(places)], refs[len(places) :]
    pairs, refs = refs[: 2 * len(places)], refs[2 * len(places) :]
    coarse, *up, held = refs
    for idx in places:
        slot = idx - first
        made = raising(idx, pcols, blocks[slot], pairs[2 * slot + 1], pairs[2 * slot], held)
        if idx == levels - 1:
            coarse[...] = matmul(made, inverse[...]).astype(bf16)
        else:
            up[slot][...] = made


def fine_operators_kernel(
    places, _, pcols, blocks_0, blocks_1, scale_0, local_0, scale_1, local_1,
    base, near, far, lower, upper, both, total, held,
):
    lower[...] = raising(0, pcols, blocks_0, local_0, scale_0, held)
    upper[...] = raising(1, pcols, blocks_1, local_1, scale_1, held)
    both[...] = matmul(lower[...], upper[...]).astype(bf16)
    width = near.shape[1]
    for slot, (place, source) in enumerate(zip(places, (near, far))):
        made = base[:, lanes_of(place, width)] + matmul(lower[...], source[...])
        total[:, slot * width : (slot + 1) * width] = made


def restricted(level_idx, rmat, kept, other):
    width = rmat.shape[1] // 2
    own = pl.multiple_of(bit_of(level_idx) * width, width)
    far = pl.multiple_of((1 - bit_of(level_idx)) * width, width)
    total = matmul(rmat[:, pl.ds(own, width)], kept[...])
    return total + matmul(rmat[:, pl.ds(far, width)], other[...])


def join_kernel(level_idx, rmat, kept, other, scale, rhs, smoothed, inner_ref, outer_ref):
    size = inner_ref.shape[0]
    current = restricted(level_idx, rmat, kept, other)
    rhs[...] = current
    rounded = (current * (relax_down * scale[...])).astype(bf16)
    smoothed[...] = rounded
    put_ends(rounded[:size], rounded[-size:], inner_ref, outer_ref)


def inverse_part(inverse, part, offset):
    depth = part.shape[0]
    piece = lax.axis_index("narrow") ^ offset
    return matmul(inverse[:, pl.ds(pl.multiple_of(piece * depth, depth), depth)], part[...])


def share_sum_kernel(far, own, *refs):
    refs[-1][...] = (far[...].astype(f32) + own[...].astype(f32)).astype(bf16)


def coarse_kernel(offsets, inverse, *refs):
    *parts, value, out = refs
    value = value[...]
    for part, offset in zip(parts, offsets):
        value = value + inverse_part(inverse, part, offset)
    out[...] = value


def up_kernel(offsets, inverse, *refs):
    value = refs[len(offsets)][...]
    for part, offset in zip(refs, offsets):
        value = value + inverse_part(inverse, part, offset)
    refs = refs[len(offsets) + 1 :]
    refs, (base, up, coarse, raised) = refs[:-4], refs[-4:]
    for step in range(len(refs) // 2):
        value = refs[2 * step][...] + matmul(refs[2 * step + 1][...], value.astype(bf16))
    value = value.astype(bf16)
    coarse[...] = value
    raised[...] = (base[...] + matmul(up[...], value)).astype(bf16)


def output_kernel(places, slots, *refs):
    coarse, (base, lower, total, both) = refs[: len(places)], refs[len(places) : len(places) + 4]
    out, made, sems = refs[-3:]
    copies = []
    for item, (place, value) in enumerate(zip(places, coarse)):
        width = value.shape[1]
        lanes = lanes_of(place, width)
        if slots[item] is None:
            made[item] = base[:, lanes] + matmul(lower[...], value[...])
        else:
            held = total[:, slots[item] * width : (slots[item] + 1) * width]
            made[item] = held + matmul(both[...], value[...])
        copy = pltpu.make_async_copy(made.at[item], out.at[0, :, lanes], sems.at[item])
        copy.start()
        copies.append(copy)
    for copy in copies:
        copy.wait()


def exchange(value, axis, bit):
    count = lax.axis_size(axis)
    return lax.ppermute(value, axis, [(i, i ^ bit) for i in range(count)])


def exchange_both(value, bit, offset):
    wide, narrow = lax.axis_size("wide"), lax.axis_size("narrow")
    pairs = [
        (w * narrow + j, (w ^ bit) * narrow + (j ^ offset))
        for w in range(wide) for j in range(narrow)
    ]
    return lax.ppermute(value, ("wide", "narrow"), pairs)


def swap_outer(outer):
    count = lax.axis_size("narrow")
    gaps = [(i, (i + 1 if i % 2 else i - 1) % count) for i in range(count)]
    return lax.ppermute(outer, "narrow", gaps)


def on_device(
    level_rhs,
    galerkin_cols,
    galerkin_blocks,
    restrict_cols,
    restrict_blocks,
    prolong_cols,
    prolong_blocks,
    coarse_inverse,
):
    levels = galerkin_cols.shape[0]
    count = galerkin_cols.shape[2]
    size = galerkin_blocks.shape[-1]
    rows, fields = level_rhs.shape[1:]
    half = fields // 2
    width = half // 2
    rcols = restrict_cols.transpose(0, 3, 1, 2), scalars()
    pcols = prolong_cols.transpose(0, 1, 3, 2), scalars()
    square_shape = array((rows, rows), bf16)
    operator_shapes = [square_shape, array((rows, 2 * size), bf16), array((rows, 1), f32)]
    rmat_shape = array((rows, 2 * rows), bf16)
    chunk_shape = array((rows, width), bf16)
    real_shape = array((rows, width), f32)
    held = [pltpu.VMEM((rows, rows), bf16)]

    def ends_shape(columns):
        return array((size, columns), bf16)

    def of_level(value, level_idx):
        return value, level_block(value, level_idx)

    def flops(columns, products=1):
        return 2 * products * rows * rows * columns

    def place_of(far, given):
        return (0, far, half), (1, given, width)

    pairs = [(place_of(1, given), place_of(0, given)) for given in (1, 0)]
    gcols, inner, *outers = run(
        functools.partial(start_kernel, pairs), "start",
        [array(galerkin_cols.shape, jnp.int32), ends_shape(fields)] + [ends_shape(half)] * 2,
        [in_hbm(level_rhs), in_hbm(galerkin_blocks), in_hbm(galerkin_cols)],
        scratch=[
            pltpu.VMEM((2, size, fields), f32), pltpu.VMEM((size, fields), bf16),
            pltpu.VMEM((2, size, size), bf16), pltpu.SemaphoreType.DMA((5,)),
        ],
    )
    gcols = in_vmem(gcols), scalars()
    first = outers[0]
    outers = [swap_outer(outer) for outer in outers]
    inner = exchange(inner, "narrow", 1)
    rest, base, local, rim, scale = run(
        first_local_kernel, "first_local", [array((rows, fields), f32)] * 2 + operator_shapes,
        [level_rhs, first, gcols, of_level(galerkin_blocks, 0)], flops=flops(fields),
    )
    operators = [(scale, local)]
    sent, kept = [], []
    for places, outer in zip(pairs, outers):
        far, near = run(
            functools.partial(first_residual_kernel, places), "first_residual", [chunk_shape] * 2,
            [rest, rim, outer, inner],
        )
        sent.append(far)
        kept.append(near)
    last = levels - 1
    bases = []
    anchor = sent[0]
    pieces = lax.axis_size("narrow")
    for level_idx in range(levels - 1):
        other = [exchange(value, "wide", 1 << level_idx) for value in sent]
        rmat, local, rim, scale = run(
            functools.partial(operators_kernel, level_idx), "operators",
            [rmat_shape] + operator_shapes,
            [anchor, rcols, of_level(restrict_blocks, level_idx),
             gcols, of_level(galerkin_blocks, level_idx + 1)],
        )
        operators.append((scale, local))
        joined = []
        for near, far in zip(kept, other):
            rhs, smoothed, *ends = run(
                functools.partial(join_kernel, level_idx), "join",
                [real_shape, chunk_shape] + [ends_shape(width)] * 2,
                [rmat, near, far, scale], flops=flops(width, 2),
            )
            inner, outer = exchange(ends[0], "narrow", 1), swap_outer(ends[1])
            joined.append((rhs, smoothed, scale, local, rim, outer, inner))
        share = []
        if level_idx + 1 == last:
            share = run(
                functools.partial(share_kernel, last), "share", [square_shape],
                [joined[0][1], rcols, of_level(restrict_blocks, last)],
            )
        made = []
        for operands in joined:
            value, made_base = run(
                last_residual_kernel if share else residual_kernel, "residual",
                [chunk_shape, real_shape if made or level_idx else chunk_shape],
                [*operands, *(share or [joined[-1][1]])],
                flops=flops(width, 2) if not made else late_cost,
            )
            made.append(value)
            bases.append(made_base)
        sent, kept = made[:1], made[-1:]
        anchor = made[0]
    (mine,) = kept
    far_parts = {o: exchange_both(mine, 1 << last, o) for o in range(0, pieces, 2)}
    far_base = exchange(bases[0], "wide", 1)
    own_parts = {o: exchange(mine, "narrow", o) if o else mine for o in range(0, pieces, 2)}
    coarse_mat, *ups = run(
        functools.partial(coarse_operators_kernel, 2, levels), "coarse_operators",
        [array((rows, pieces * rows), bf16)] + [square_shape] * (levels - 3),
        [mine, far_base, pcols, coarse_inverse]
        + [of_level(prolong_blocks, idx) for idx in range(2, levels)]
        + [value for pair in operators[2:] for value in pair],
        flops=flops(rows, 2 * (levels - 2) + pieces), scratch=held,
    )
    places = [place_of(0, 1), place_of(1, 1)]
    lower, upper, both, total = run(
        functools.partial(fine_operators_kernel, places), "fine_operators",
        [square_shape] * 3 + [array((rows, half), f32)],
        [mine, pcols, of_level(prolong_blocks, 0), of_level(prolong_blocks, 1),
         *operators[0], *operators[1], base, bases[0], far_base],
        flops=flops(rows, 4), scratch=held,
    )
    parts = {}
    for offset in reversed(range(0, pieces, 2)):
        (parts[offset],) = run(
            share_sum_kernel, "share_sum", [chunk_shape],
            [far_parts[offset], own_parts[offset], coarse_mat, upper],
        )
    offsets = tuple(parts)
    (value,) = run(
        functools.partial(coarse_kernel, offsets), "coarse", [real_shape],
        [coarse_mat] + [parts[o] for o in offsets] + [bases[-1]], flops=flops(width, len(offsets)),
    )
    parts = {o + 1: exchange(parts[o], "narrow", 1) for o in offsets}
    offsets = tuple(parts)
    operands = [coarse_mat] + [parts[o] for o in offsets] + [value]
    for idx in reversed(range(2, last)):
        operands += [bases[idx], ups[idx - 2]]
    value, near = run(
        functools.partial(up_kernel, offsets), "up", [chunk_shape] * 2,
        operands + [bases[1], upper], flops=flops(width, len(offsets) + levels - 2),
    )
    diagonal, other = (exchange(value, "wide", bits) for bits in (3, 2))
    far = exchange(near, "wide", 1)
    result = None
    for group in (
        [(near, place_of(0, 0), None)],
        [(diagonal, place_of(1, 1), 1)],
        [(other, place_of(0, 1), 0), (far, place_of(1, 0), None)],
    ):
        values, places, slots = zip(*group)
        operands = [*values, base, lower, total, both]
        aliases = {}
        if result is not None:
            aliases[len(operands)] = 0
            operands.append(in_hbm(result))
        (result,) = run(
            functools.partial(output_kernel, places, slots),
            "output", [array((1, rows, fields), f32)], operands,
            flops=flops(width, len(group)), out_space=pltpu.HBM, aliases=aliases,
            scratch=[
                pltpu.VMEM((len(group), rows, width), f32), pltpu.SemaphoreType.DMA((len(group),))
            ],
        )
    return result


def solution(mesh):
    in_specs = (
        P("wide", "narrow", None),
        P(None, "wide", "narrow", None),
        P(None, "wide", "narrow", None, None, None),
        P(None, "wide", "narrow", None),
        P(None, "wide", "narrow", None, None, None),
        P(None, "wide", "narrow", None),
        P(None, "wide", "narrow", None, None, None),
        P("narrow", None),
    )
    out_specs = P("wide", "narrow", None)
    return jax.shard_map(
        on_device, mesh=mesh, in_specs=in_specs, out_specs=out_specs, check_vma=False
    )
```

```python
import functools

import jax
import jax.numpy as jnp
from jax import lax
from jax.experimental import pallas as pl
from jax.experimental.pallas import tpu as pltpu
from jax.sharding import PartitionSpec as P

relax_down = 0.7
relax_up = 0.5
f32 = jnp.float32
bf16 = jnp.bfloat16
grant = 12 * 1024 * 1024
late_cost = 4 * 10**9


def matmul(a, b):
    return jnp.dot(a, b, preferred_element_type=f32)


def array(shape, dtype):
    return jax.ShapeDtypeStruct(shape, dtype)


def whole():
    return pl.BlockSpec(memory_space=pltpu.VMEM)


def level_block(value, level_idx):
    shape = (1,) + value.shape[1:]
    return pl.BlockSpec(shape, lambda i: (level_idx,) + (0,) * (value.ndim - 1))


def scalars():
    return pl.BlockSpec(memory_space=pltpu.SMEM)


def in_hbm(value):
    return pltpu.with_memory_space_constraint(value, pltpu.HBM), pl.BlockSpec(memory_space=pltpu.HBM)


def in_vmem(value):
    return pltpu.with_memory_space_constraint(value, pltpu.VMEM)


def run(body, name, outs, operands, flops=0, scratch=(), out_space=pltpu.VMEM, aliases=None):
    arrays = [o[0] if isinstance(o, tuple) else in_vmem(o) for o in operands]
    specs = [o[1] if isinstance(o, tuple) else whole() for o in operands]
    windows = any(isinstance(o, tuple) and o[1].block_shape is not None for o in operands)
    moved = sum(a.size * a.dtype.itemsize for a in arrays)
    return pl.pallas_call(
        body,
        grid=(1,) if windows else (),
        out_shape=[out_space(o.shape, o.dtype) for o in outs],
        in_specs=specs,
        out_specs=[pl.BlockSpec(memory_space=out_space)] * len(outs),
        input_output_aliases=aliases or {},
        scratch_shapes=list(scratch),
        compiler_params=pltpu.CompilerParams(vmem_limit_bytes=grant),
        cost_estimate=pl.CostEstimate(flops=flops, bytes_accessed=moved, transcendentals=0),
        name=name,
    )(*arrays)


def diagonal_of(block):
    size = block.shape[0]
    rows = lax.broadcasted_iota(jnp.int32, (size, size), 0)
    lanes = lax.broadcasted_iota(jnp.int32, (size, size), 1)
    return jnp.sum(jnp.where(rows == lanes, block, 0.0), axis=1, keepdims=True)


def placed(base, others, ids, target):
    total = base
    for block, ident in zip(others, ids):
        term = block * jnp.where(ident == target, 1.0, 0.0).astype(f32)
        total = term if total is None else total + term
    return total


def parity_of():
    return lax.rem(lax.axis_index("narrow"), 2)


def put_ends(first, last, inner_ref, outer_ref):
    even = parity_of() == 0
    inner_ref[...] = jnp.where(even, last, first)
    outer_ref[...] = jnp.where(even, first, last)


def assemble_galerkin(level_idx, cols, blocks, local_ref, rim_ref, scale_ref):
    count, slots, size = blocks.shape[2], blocks.shape[3], blocks.shape[4]
    parity = parity_of()
    piece = lax.axis_index("narrow")
    last = lax.axis_size("narrow") - 1
    inside = jnp.where((piece == 0) | (piece == last), 0.0, 1.0).astype(f32)
    for b in range(count):
        held = [blocks[0, 0, b, s].astype(f32) for s in range(slots)]
        ids = [cols[level_idx, 0, b, s] for s in range(1, slots)]
        rows = pl.ds(b * size, size)
        scale_ref[rows, :] = 1.0 / diagonal_of(held[0])
        line = [placed(held[0] if c == b else None, held[1:], ids, c) for c in range(count)]
        local_ref[rows, :] = jnp.concatenate(line, axis=1).astype(bf16)
        rims = [
            placed(None, held[1:], ids, count + 1 - parity),
            placed(None, held[1:], ids, count + parity) * inside,
        ]
        rim_ref[rows, :] = jnp.concatenate(rims, axis=1).astype(bf16)


def assemble_restrict(level_idx, cols, blocks, out_ref):
    count, slots, size = blocks.shape[2], blocks.shape[3], blocks.shape[4]
    for b in range(count):
        held = [blocks[0, 0, b, s].astype(f32) for s in range(slots)]
        ids = [cols[level_idx, s, 0, b] for s in range(2, slots)]
        fixed = {b: held[0], count + b: held[1]}
        line = [placed(fixed.get(c), held[2:], ids, c) for c in range(2 * count)]
        out_ref[pl.ds(b * size, size), :] = jnp.concatenate(line, axis=1).astype(bf16)


def assemble_share(level_idx, cols, blocks, out_ref):
    count, slots, size = blocks.shape[2], blocks.shape[3], blocks.shape[4]
    bit = bit_of(level_idx)
    for b in range(count):
        held = [blocks[0, 0, b, s].astype(f32) for s in range(slots)]
        ids = [cols[level_idx, s, 0, b] for s in range(2, slots)]
        own = jnp.where(bit == 0, held[0], held[1])
        first = bit * count
        line = [placed(own if c == b else None, held[2:], ids, first + c) for c in range(count)]
        out_ref[pl.ds(b * size, size), :] = jnp.concatenate(line, axis=1).astype(bf16)


def assemble_prolong(level_idx, cols, blocks, out_ref):
    count, slots, size = blocks.shape[2], blocks.shape[3], blocks.shape[4]
    for b in range(count):
        held = [blocks[0, 0, b, s].astype(f32) for s in range(slots)]
        ids = [cols[level_idx, 0, s, b] for s in range(1, slots)]
        line = [placed(held[0] if c == b else None, held[1:], ids, c) for c in range(count)]
        out_ref[pl.ds(b * size, size), :] = jnp.concatenate(line, axis=1).astype(bf16)


def start_kernel(places, rhs, blocks, *refs):
    table, held, *ends, rows, inner, outer, pivots, sems = refs
    count, size = blocks.shape[2], blocks.shape[4]
    copies = []
    for slot, which in enumerate((0, count - 1)):
        source = rhs.at[0, pl.ds(which * size, size), :]
        copies.append(pltpu.make_async_copy(source, rows.at[slot], sems.at[slot]))
        source = blocks.at[0, 0, which, 0]
        copies.append(pltpu.make_async_copy(source, pivots.at[slot], sems.at[2 + slot]))
    copies.append(pltpu.make_async_copy(table, held, sems.at[4]))
    for copy in copies:
        copy.start()
    for copy in copies:
        copy.wait()
    first, last = (
        (rows[slot] * (relax_down / diagonal_of(pivots[slot].astype(f32)))).astype(bf16)
        for slot in range(2)
    )
    put_ends(first, last, inner, outer)
    for source, made in ((inner, ends[: len(places)]), (outer, ends[len(places) :])):
        for ref, pair in zip(made, places):
            width = ref.shape[1] // 2
            for slot, place in enumerate(pair):
                ref[:, slot * width : (slot + 1) * width] = source[:, lanes_of(place, width)]


def first_local_kernel(rhs, _, cols, blocks, rest, base, local, rim, scale):
    assemble_galerkin(0, cols, blocks, local, rim, scale)
    smoothed = rhs[0] * (relax_down * scale[...])
    left = rhs[0] - matmul(local[...], smoothed.astype(bf16))
    rest[...] = left
    base[...] = smoothed + (relax_up * scale[...]) * left


def bit_of(level_idx):
    return lax.axis_index("wide") >> level_idx & 1


def lanes_of(place, width):
    start = 0
    for level_idx, flip, step in place:
        start = start + (bit_of(level_idx) ^ flip) * step
    return pl.ds(pl.multiple_of(start, width), width)


def first_residual_kernel(places, rest, rim, outer, inner, *refs):
    width = refs[0].shape[1]
    for slot, (ref, place) in enumerate(zip(refs, places)):
        lanes = lanes_of(place, width)
        columns = pl.ds(slot * width, width)
        rims = jnp.concatenate([inner[:, columns], outer[:, columns]], axis=0)
        ref[...] = (rest[:, lanes] - matmul(rim[...], rims)).astype(bf16)


def residual_kernel(rhs, smoothed, scale, local, rim, outer, inner, _, out, base):
    rims = jnp.concatenate([inner[...], outer[...]], axis=0)
    left = rhs[...] - matmul(local[...], smoothed[...])
    out[...] = (left - matmul(rim[...], rims)).astype(bf16)
    made = rhs[...] * (relax_down * scale[...]) + (relax_up * scale[...]) * left
    base[...] = made.astype(base.dtype)


def last_residual_kernel(rhs, smoothed, scale, local, rim, outer, inner, share, out, base):
    rims = jnp.concatenate([inner[...], outer[...]], axis=0)
    left = rhs[...] - matmul(local[...], smoothed[...])
    residual = (left - matmul(rim[...], rims)).astype(bf16)
    out[...] = matmul(share[...], residual).astype(bf16)
    base[...] = rhs[...] * (relax_down * scale[...]) + (relax_up * scale[...]) * left


def share_kernel(level_idx, _, rcols, rblocks, share):
    assemble_share(level_idx, rcols, rblocks, share)


def operators_kernel(level_idx, _, rcols, rblocks, cols, blocks, rmat, local, rim, scale):
    assemble_restrict(level_idx, rcols, rblocks, rmat)
    assemble_galerkin(level_idx + 1, cols, blocks, local, rim, scale)


def raising(level_idx, pcols, blocks, local, scale, held):
    assemble_prolong(level_idx, pcols, blocks, held)
    applied = matmul(local[...], held[...])
    return (held[...].astype(f32) - (relax_up * scale[...]) * applied).astype(bf16)


def coarse_operators_kernel(first, levels, *refs):
    _, _, pcols, inverse, *refs = refs
    places = range(first, levels)
    blocks, refs = refs[: len(places)], refs[len(places) :]
    pairs, refs = refs[: 2 * len(places)], refs[2 * len(places) :]
    coarse, *up, held = refs
    for idx in places:
        slot = idx - first
        made = raising(idx, pcols, blocks[slot], pairs[2 * slot + 1], pairs[2 * slot], held)
        if idx == levels - 1:
            coarse[...] = matmul(made, inverse[...]).astype(bf16)
        else:
            up[slot][...] = made


def fine_operators_kernel(
    places, _, pcols, blocks_0, blocks_1, scale_0, local_0, scale_1, local_1,
    base, near, far, lower, upper, both, total, held,
):
    lower[...] = raising(0, pcols, blocks_0, local_0, scale_0, held)
    upper[...] = raising(1, pcols, blocks_1, local_1, scale_1, held)
    both[...] = matmul(lower[...], upper[...]).astype(bf16)
    width = near.shape[1]
    for slot, (place, source) in enumerate(zip(places, (near, far))):
        made = base[:, lanes_of(place, width)] + matmul(lower[...], source[...])
        total[:, slot * width : (slot + 1) * width] = made


def restricted(level_idx, rmat, kept, other):
    width = rmat.shape[1] // 2
    own = pl.multiple_of(bit_of(level_idx) * width, width)
    far = pl.multiple_of((1 - bit_of(level_idx)) * width, width)
    total = matmul(rmat[:, pl.ds(own, width)], kept[...])
    return total + matmul(rmat[:, pl.ds(far, width)], other[...])


def join_kernel(level_idx, rmat, kept, other, scale, rhs, smoothed, inner_ref, outer_ref):
    size = inner_ref.shape[0]
    current = restricted(level_idx, rmat, kept, other)
    rhs[...] = current
    rounded = (current * (relax_down * scale[...])).astype(bf16)
    smoothed[...] = rounded
    put_ends(rounded[:size], rounded[-size:], inner_ref, outer_ref)


def inverse_part(inverse, part, offset):
    depth = part.shape[0]
    piece = lax.axis_index("narrow") ^ offset
    return matmul(inverse[:, pl.ds(pl.multiple_of(piece * depth, depth), depth)], part[...])


def share_sum_kernel(far, own, *refs):
    refs[-1][...] = (far[...].astype(f32) + own[...].astype(f32)).astype(bf16)


def coarse_kernel(offsets, inverse, *refs):
    *parts, value, out = refs
    value = value[...]
    for part, offset in zip(parts, offsets):
        value = value + inverse_part(inverse, part, offset)
    out[...] = value


def up_kernel(offsets, inverse, *refs):
    value = refs[len(offsets)][...]
    for part, offset in zip(refs, offsets):
        value = value + inverse_part(inverse, part, offset)
    refs = refs[len(offsets) + 1 :]
    refs, (base, up, coarse, raised) = refs[:-4], refs[-4:]
    for step in range(len(refs) // 2):
        value = refs[2 * step][...] + matmul(refs[2 * step + 1][...], value.astype(bf16))
    value = value.astype(bf16)
    coarse[...] = value
    raised[...] = (base[...] + matmul(up[...], value)).astype(bf16)


def output_kernel(places, slots, *refs):
    coarse, (base, lower, total, both) = refs[: len(places)], refs[len(places) : len(places) + 4]
    out, made, sems = refs[-3:]
    copies = []
    for item, (place, value) in enumerate(zip(places, coarse)):
        width = value.shape[1]
        lanes = lanes_of(place, width)
        if slots[item] is None:
            made[item] = base[:, lanes] + matmul(lower[...], value[...])
        else:
            held = total[:, slots[item] * width : (slots[item] + 1) * width]
            made[item] = held + matmul(both[...], value[...])
        copy = pltpu.make_async_copy(made.at[item], out.at[0, :, lanes], sems.at[item])
        copy.start()
        copies.append(copy)
    for copy in copies:
        copy.wait()


def exchange(value, axis, bit):
    count = lax.axis_size(axis)
    return lax.ppermute(value, axis, [(i, i ^ bit) for i in range(count)])


def exchange_both(value, bit, offset):
    wide, narrow = lax.axis_size("wide"), lax.axis_size("narrow")
    pairs = [
        (w * narrow + j, (w ^ bit) * narrow + (j ^ offset))
        for w in range(wide) for j in range(narrow)
    ]
    return lax.ppermute(value, ("wide", "narrow"), pairs)


def swap_outer(outer):
    count = lax.axis_size("narrow")
    gaps = [(i, (i + 1 if i % 2 else i - 1) % count) for i in range(count)]
    return lax.ppermute(outer, "narrow", gaps)


def on_device(
    level_rhs,
    galerkin_cols,
    galerkin_blocks,
    restrict_cols,
    restrict_blocks,
    prolong_cols,
    prolong_blocks,
    coarse_inverse,
):
    levels = galerkin_cols.shape[0]
    count = galerkin_cols.shape[2]
    size = galerkin_blocks.shape[-1]
    rows, fields = level_rhs.shape[1:]
    half = fields // 2
    width = half // 2
    rcols = restrict_cols.transpose(0, 3, 1, 2), scalars()
    pcols = prolong_cols.transpose(0, 1, 3, 2), scalars()
    square_shape = array((rows, rows), bf16)
    operator_shapes = [square_shape, array((rows, 2 * size), bf16), array((rows, 1), f32)]
    rmat_shape = array((rows, 2 * rows), bf16)
    chunk_shape = array((rows, width), bf16)
    real_shape = array((rows, width), f32)
    held = [pltpu.VMEM((rows, rows), bf16)]

    def ends_shape(columns):
        return array((size, columns), bf16)

    def of_level(value, level_idx):
        return value, level_block(value, level_idx)

    def flops(columns, products=1):
        return 2 * products * rows * rows * columns

    def place_of(far, given):
        return (0, far, half), (1, given, width)

    pairs = [(place_of(1, given), place_of(0, given)) for given in (1, 0)]
    gcols, *ends = run(
        functools.partial(start_kernel, pairs), "start",
        [array(galerkin_cols.shape, jnp.int32)] + [ends_shape(half)] * 4,
        [in_hbm(level_rhs), in_hbm(galerkin_blocks), in_hbm(galerkin_cols)],
        scratch=[
            pltpu.VMEM((2, size, fields), f32),
            pltpu.VMEM((size, fields), bf16), pltpu.VMEM((size, fields), bf16),
            pltpu.VMEM((2, size, size), bf16), pltpu.SemaphoreType.DMA((5,)),
        ],
    )
    gcols = in_vmem(gcols), scalars()
    first = ends[0]
    outers = [swap_outer(outer) for outer in ends[2:]]
    inners = [exchange(inner, "narrow", 1) for inner in ends[:2]]
    rest, base, local, rim, scale = run(
        first_local_kernel, "first_local", [array((rows, fields), f32)] * 2 + operator_shapes,
        [level_rhs, first, gcols, of_level(galerkin_blocks, 0)], flops=flops(fields),
    )
    operators = [(scale, local)]
    sent, kept = [], []
    for places, inner, outer in zip(pairs, inners, outers):
        far, near = run(
            functools.partial(first_residual_kernel, places), "first_residual", [chunk_shape] * 2,
            [rest, rim, outer, inner],
        )
        sent.append(far)
        kept.append(near)
    last = levels - 1
    bases = []
    anchor = sent[0]
    pieces = lax.axis_size("narrow")
    for level_idx in range(levels - 1):
        other = [exchange(value, "wide", 1 << level_idx) for value in sent]
        rmat, local, rim, scale = run(
            functools.partial(operators_kernel, level_idx), "operators",
            [rmat_shape] + operator_shapes,
            [anchor, rcols, of_level(restrict_blocks, level_idx),
             gcols, of_level(galerkin_blocks, level_idx + 1)],
        )
        operators.append((scale, local))
        joined = []
        for near, far in zip(kept, other):
            rhs, smoothed, *ends = run(
                functools.partial(join_kernel, level_idx), "join",
                [real_shape, chunk_shape] + [ends_shape(width)] * 2,
                [rmat, near, far, scale], flops=flops(width, 2),
            )
            inner, outer = exchange(ends[0], "narrow", 1), swap_outer(ends[1])
            joined.append((rhs, smoothed, scale, local, rim, outer, inner))
        share = []
        if level_idx + 1 == last:
            share = run(
                functools.partial(share_kernel, last), "share", [square_shape],
                [joined[0][1], rcols, of_level(restrict_blocks, last)],
            )
        made = []
        for operands in joined:
            value, made_base = run(
                last_residual_kernel if share else residual_kernel, "residual",
                [chunk_shape, real_shape if made or level_idx else chunk_shape],
                [*operands, *(share or [joined[-1][1]])],
                flops=flops(width, 2) if not made else late_cost,
            )
            made.append(value)
            bases.append(made_base)
        sent, kept = made[:1], made[-1:]
        anchor = made[0]
    (mine,) = kept
    far_parts = {o: exchange_both(mine, 1 << last, o) for o in range(0, pieces, 2)}
    far_base = exchange(bases[0], "wide", 1)
    own_parts = {o: exchange(mine, "narrow", o) if o else mine for o in range(0, pieces, 2)}
    coarse_mat, *ups = run(
        functools.partial(coarse_operators_kernel, 2, levels), "coarse_operators",
        [array((rows, pieces * rows), bf16)] + [square_shape] * (levels - 3),
        [mine, far_base, pcols, coarse_inverse]
        + [of_level(prolong_blocks, idx) for idx in range(2, levels)]
        + [value for pair in operators[2:] for value in pair],
        flops=flops(rows, 2 * (levels - 2) + pieces), scratch=held,
    )
    places = [place_of(0, 1), place_of(1, 1)]
    lower, upper, both, total = run(
        functools.partial(fine_operators_kernel, places), "fine_operators",
        [square_shape] * 3 + [array((rows, half), f32)],
        [mine, pcols, of_level(prolong_blocks, 0), of_level(prolong_blocks, 1),
         *operators[0], *operators[1], base, bases[0], far_base],
        flops=flops(rows, 4), scratch=held,
    )
    parts = {}
    for offset in reversed(range(0, pieces, 2)):
        (parts[offset],) = run(
            share_sum_kernel, "share_sum", [chunk_shape],
            [far_parts[offset], own_parts[offset], coarse_mat, upper],
        )
    offsets = tuple(parts)
    (value,) = run(
        functools.partial(coarse_kernel, offsets), "coarse", [real_shape],
        [coarse_mat] + [parts[o] for o in offsets] + [bases[-1]], flops=flops(width, len(offsets)),
    )
    parts = {o + 1: exchange(parts[o], "narrow", 1) for o in reversed(offsets)}
    offsets = tuple(parts)
    operands = [coarse_mat] + [parts[o] for o in offsets] + [value]
    for idx in reversed(range(2, last)):
        operands += [bases[idx], ups[idx - 2]]
    value, near = run(
        functools.partial(up_kernel, offsets), "up", [chunk_shape] * 2,
        operands + [bases[1], upper], flops=flops(width, len(offsets) + levels - 2),
    )
    diagonal, other = (exchange(value, "wide", bits) for bits in (3, 2))
    far = exchange(near, "wide", 1)
    result = None
    for group in (
        [(near, place_of(0, 0), None)],
        [(diagonal, place_of(1, 1), 1)],
        [(other, place_of(0, 1), 0), (far, place_of(1, 0), None)],
    ):
        values, places, slots = zip(*group)
        operands = [*values, base, lower, total, both]
        aliases = {}
        if result is not None:
            aliases[len(operands)] = 0
            operands.append(in_hbm(result))
        (result,) = run(
            functools.partial(output_kernel, places, slots),
            "output", [array((1, rows, fields), f32)], operands,
            flops=flops(width, len(group)), out_space=pltpu.HBM, aliases=aliases,
            scratch=[
                pltpu.VMEM((len(group), rows, width), f32), pltpu.SemaphoreType.DMA((len(group),))
            ],
        )
    return result


def solution(mesh):
    in_specs = (
        P("wide", "narrow", None),
        P(None, "wide", "narrow", None),
        P(None, "wide", "narrow", None, None, None),
        P(None, "wide", "narrow", None),
        P(None, "wide", "narrow", None, None, None),
        P(None, "wide", "narrow", None),
        P(None, "wide", "narrow", None, None, None),
        P("narrow", None),
    )
    out_specs = P("wide", "narrow", None)
    return jax.shard_map(
        on_device, mesh=mesh, in_specs=in_specs, out_specs=out_specs, check_vma=False
    )
```
